512 devices in a mesh: solve: 64 (over x, z, core), cross: 8 (over y).
Axes of the slice: x: 4, y: 8, z: 8, core: 2. Of those that a mesh axis runs over, the one named last changes fastest.
Arguments:
- thermal_state_pair: float32 [2, 1024, 8192], P(None, 'solve', 'cross'), may hold values from -4 to 6
- longitudinal_interface_transfer: float32 [2, 1024, 8192], P(None, 'solve', 'cross'), may hold values from 524 to 7489
- transverse_diffusivity_cells: float32 [2, 1024, 8192], P(None, 'solve', 'cross'), may hold values from 0.02 to 0.24
- sheet_exchange_coefficient: float32 [1024, 8192], P('solve', 'cross'), may hold values from 0.05 to 10
Outputs:
- solution: float32 [2, 1024, 8192], P(None, 'solve', 'cross')
The draws below stay inside these ranges and needn't reach their ends.
All inputs are finite; a program needn't handle non-finite values.
Results may differ from the reference program's by a relative error of at most 0.0003.
Values sent between devices are 32-bit elements; how exact they have to be, the bound alone decides.
A program may use at most 128 MiB of HBM per device.

```python
import math
import jax
import jax.numpy as jnp
from jax import lax

COLS_DEV = 1024
PLANES = 2
NL = 1024
NC = 8192
N_CROSS = 8


def draw_thermal_state_pair(key, part):
    key = jax.random.fold_in(key, 7)
    column_key = jax.random.fold_in(key, 11)
    column_part = jax.random.uniform(column_key, (PLANES, 1, NC), jnp.float32, -1.0, 1.0)
    level_part = jnp.array([3.5, -1.5], jnp.float32)[:, None, None]
    rough_part = jnp.clip(jax.random.normal(key, (PLANES, NL, NC), jnp.float32), -1.5, 1.5)
    return level_part + rough_part + column_part


def draw_sheet_exchange_coefficient(key, part):
    key = jax.random.fold_in(key, 5)
    block_span = max(NL // 12, 2)
    block_count = NL // block_span + 2
    row_offset = jax.random.randint(jax.random.fold_in(key, 1), (1, NC), 0, block_span)
    block_index = (jnp.arange(NL, dtype=jnp.int32)[:, None] + row_offset) // block_span
    block_flags = jax.random.randint(jax.random.fold_in(key, 2), (block_count, NC), 0, 2)
    block_number = jnp.arange(block_count, dtype=jnp.int32)[:, None]
    block_flags = jnp.where(block_number == 0, 0, jnp.where(block_number == 1, 1, block_flags))
    chosen_kind = jnp.take_along_axis(block_flags, block_index.astype(jnp.int32), axis=0)
    weak_values = jnp.exp(jax.random.uniform(jax.random.fold_in(key, 3), (NL, NC), jnp.float32, jnp.log(0.05), jnp.log(0.15)))
    strong_values = jnp.exp(jax.random.uniform(jax.random.fold_in(key, 4), (NL, NC), jnp.float32, jnp.log(4.0), jnp.log(10.0)))
    return jnp.where(chosen_kind == 1, strong_values, weak_values)


def levels(rng, shape, shards, least, largest):
    loudness = 1.0
    for axis_at, shards_of in shards:
        steps = jax.random.uniform(jax.random.fold_in(jax.random.fold_in(rng, 6), axis_at), (shards_of,), jnp.float32, least / len(shards), largest / len(shards))
        loudness = loudness * jnp.repeat(jnp.exp(steps), shape[axis_at] // shards_of).reshape((-1,) + (1,) * (len(shape) - 1 - axis_at))
    return loudness


def setup_inputs(seed: int = 0) -> dict:
    keys = jax.random.split(jax.random.key(seed), 5)
    return {
        "thermal_state_pair": draw_thermal_state_pair(jax.random.fold_in(keys[4], 71), 0),
        "longitudinal_interface_transfer": jnp.clip(jnp.exp(math.log(7489.0) - 2.659699 * jax.random.uniform(keys[1], (PLANES, NL, NC), jnp.float32) ** levels(keys[1], (PLANES, NL, NC), ((1, 64), (2, 8)), -0.2, 0.2)), 524.0, 7489.0),
        "transverse_diffusivity_cells": jnp.clip(0.02 + 0.22 * jax.random.uniform(keys[2], (PLANES, NL, NC), jnp.float32) ** levels(keys[2], (PLANES, NL, NC), ((1, 64), (2, 8)), -0.2, 0.2), 0.02, 0.24),
        "sheet_exchange_coefficient": draw_sheet_exchange_coefficient(jax.random.fold_in(keys[4], 71), 0),
    }


def forward_row(carry, row):
    inverse_first_first, inverse_first_second, inverse_second_second, zed_a, zed_b = carry
    diagonal_first, diagonal_second, coupling_field, face_first_plane, face_second_plane, rhs_a, rhs_b = row
    eliminated_first_first = diagonal_first - face_first_plane * face_first_plane * inverse_first_first
    eliminated_first_second = -coupling_field - face_first_plane * face_second_plane * inverse_first_second
    eliminated_second_second = diagonal_second - face_second_plane * face_second_plane * inverse_second_second
    rhs_a = rhs_a + face_first_plane * zed_a
    rhs_b = rhs_b + face_second_plane * zed_b
    block_determinant = eliminated_first_first * eliminated_second_second - eliminated_first_second * eliminated_first_second
    updated_first_first = eliminated_second_second / block_determinant
    updated_first_second = -eliminated_first_second / block_determinant
    updated_second_second = eliminated_first_first / block_determinant
    new_za = updated_first_first * rhs_a + updated_first_second * rhs_b
    new_zb = updated_first_second * rhs_a + updated_second_second * rhs_b
    result = (updated_first_first, updated_first_second, updated_second_second, new_za, new_zb)
    return result, result


def backward_row(carry, row):
    value_a, value_b = carry
    inverse_first_first, inverse_first_second, inverse_second_second, zed_a, zed_b, upper_a, upper_b = row
    push_a = upper_a * value_a
    push_b = upper_b * value_b
    new_a = zed_a + inverse_first_first * push_a + inverse_first_second * push_b
    new_b = zed_b + inverse_first_second * push_a + inverse_second_second * push_b
    return (new_a, new_b), (new_a, new_b)


def solve_block(pieces):
    diagonal, lower, upper, thermal_injection, coupling_field = pieces
    zeros = jnp.zeros_like(coupling_field[0])
    start = (zeros, zeros, zeros, zeros, zeros)
    rows = (diagonal[0], diagonal[1], coupling_field, lower[0], lower[1], thermal_injection[0], thermal_injection[1])
    unused, factors = lax.scan(forward_row, start, rows)
    rows_back = factors + (upper[0], upper[1])
    unused_back, values = lax.scan(backward_row, (zeros, zeros), rows_back, reverse=True)
    return jnp.stack([values[0], values[1]])


def reference(thermal_state_pair, longitudinal_interface_transfer, transverse_diffusivity_cells, sheet_exchange_coefficient):
    broaden_map = ((0, 0), (0, 0), (1, 1))
    warmed_patch = jnp.pad(thermal_state_pair, broaden_map)
    transfer_map = jnp.pad(transverse_diffusivity_cells, broaden_map)
    interface_toward_following = 0.5 * (transfer_map[:, :, 1:-1] + transfer_map[:, :, 2:]) * (warmed_patch[:, :, 2:] - thermal_state_pair)
    interface_toward_previous = 0.5 * (transfer_map[:, :, :-2] + transfer_map[:, :, 1:-1]) * (thermal_state_pair - warmed_patch[:, :, :-2])
    thermal_injection = thermal_state_pair + interface_toward_following - interface_toward_previous
    zero_row = jnp.zeros_like(longitudinal_interface_transfer[:, :1, :])
    lower = jnp.concatenate([zero_row, longitudinal_interface_transfer[:, :-1, :]], axis=1)
    diagonal = 1.0 + lower + longitudinal_interface_transfer + sheet_exchange_coefficient[None]

    def blocks(array):
        return array.reshape(array.shape[0], NL, N_CROSS, COLS_DEV).transpose(2, 0, 1, 3)

    coupling_blocks = sheet_exchange_coefficient.reshape(NL, N_CROSS, COLS_DEV).transpose(1, 0, 2)
    solved = lax.map(solve_block, (blocks(diagonal), blocks(lower), blocks(longitudinal_interface_transfer), blocks(thermal_injection), coupling_blocks))
    return solved.transpose(1, 2, 0, 3).reshape(2, NL, NC)
```

```python
import functools

import jax
import jax.numpy as jnp
from jax import lax
from jax.experimental import pallas as pl
from jax.experimental.pallas import tpu as pltpu
from jax.sharding import PartitionSpec as P

MESH = pl.DeviceIdType.MESH
ROWS, SUBS, LANES = 16, 8, 128
GROUP = 16
HALF = LANES // 2
FLAT = 2 * ROWS * SUBS
NFIELD = 14


def inverse(coupling, first, second):
    scale = 1.0 / (coupling * (first + second) + first * second)
    return (coupling + second) * scale, coupling * scale, (coupling + first) * scale


def merge(left, right):
    ea1, ea2, sa, n11, n12, n21, n22, ec1, ec2, sc = left
    fa1, fa2, fs, m11, m12, m21, m22, fc1, fc2, gs = right
    eb1, eb2, sb = ec1 + fa1, ec2 + fa2, sc + fs
    r1 = eb1 + ((n11 + n21) + (m11 + m12))
    r2 = eb2 + ((n12 + n22) + (m21 + m22))
    i11, i12, i22 = inverse(sb, r1, r2)
    g11, g12 = n11 * i11 + n12 * i12, n11 * i12 + n12 * i22
    g21, g22 = n21 * i11 + n22 * i12, n21 * i12 + n22 * i22
    h11, h12 = i11 * m11 + i12 * m21, i11 * m12 + i12 * m22
    h21, h22 = i12 * m11 + i22 * m21, i12 * m12 + i22 * m22
    joined = (
        ea1 + (g11 * eb1 + g12 * eb2),
        ea2 + (g21 * eb1 + g22 * eb2),
        sa + (g11 * n21 + g12 * n22),
        g11 * m11 + g12 * m21,
        g11 * m12 + g12 * m22,
        g21 * m11 + g22 * m21,
        g21 * m12 + g22 * m22,
        fc1 + (h11 * eb1 + h21 * eb2),
        fc2 + (h12 * eb1 + h22 * eb2),
        gs + (m11 * h12 + m21 * h22),
    )
    return joined, (i11, i12, i22, g11, g12, g21, g22, h11, h12, h21, h22)


def merge_leaf(sa, sb, n1, n2, m1, m2):
    r1, r2 = 1.0 + (n1 + m1), 1.0 + (n2 + m2)
    i11, i12, i22 = inverse(sb, r1, r2)
    g11, g12, g21, g22 = n1 * i11, n1 * i12, n2 * i12, n2 * i22
    h11, h12, h21, h22 = i11 * m1, i12 * m2, i12 * m1, i22 * m2
    joined = (
        1.0 + (g11 + g12),
        1.0 + (g21 + g22),
        sa + g12 * n2,
        g11 * m1,
        g12 * m2,
        g21 * m1,
        g22 * m2,
        h11 + h21,
        h12 + h22,
        m1 * h12,
    )
    return joined, (i11, i12, i22, g11, g12, g21, g22, h11, h12, h21, h22)


def merge_loads(back, left, right):
    i11, i12, i22, g11, g12, g21, g22, h11, h12, h21, h22 = back
    a1, a2, b1, b2 = left
    c1, c2, d1, d2 = right
    b1, b2 = b1 + c1, b2 + c2
    loads = (
        a1 + (g11 * b1 + g12 * b2),
        a2 + (g21 * b1 + g22 * b2),
        d1 + (h11 * b1 + h21 * b2),
        d2 + (h12 * b1 + h22 * b2),
    )
    return loads, (i11 * b1 + i12 * b2, i12 * b1 + i22 * b2)


def merge_leaf_loads(back, a, b):
    i11, i12, i22, g11, g12, g21, g22, h11, h12, h21, h22 = back
    a1, a2 = a
    b1, b2 = b
    loads = (
        a1 + (g11 * b1 + g12 * b2),
        a2 + (g21 * b1 + g22 * b2),
        h11 * b1 + h21 * b2,
        h12 * b1 + h22 * b2,
    )
    return loads, (i11 * b1 + i12 * b2, i12 * b1 + i22 * b2)


def middle(back, own, before, after):
    g11, g12, g21, g22, h11, h12, h21, h22 = back[3:]
    a1, a2 = before
    c1, c2 = after
    return (
        own[0] + ((g11 * a1 + g21 * a2) + (h11 * c1 + h12 * c2)),
        own[1] + ((g12 * a1 + g22 * a2) + (h21 * c1 + h22 * c2)),
    )


def kernel(
    groups,
    temp_hbm,
    face_hbm,
    diff_hbm,
    sheet_hbm,
    out_ref,
    temp,
    face,
    diff,
    sheet,
    source,
    edge_send,
    edge_recv,
    part_send,
    part_recv,
    line_send,
    line_recv,
    pick,
    node_send,
    node_recv,
    in_sem,
    edge_ssem,
    edge_rsem,
    part_ssem,
    part_rsem,
    line_ssem,
    line_rsem,
    node_ssem,
    node_rsem,
):
    solve = lax.axis_index("solve")
    cross = lax.axis_index("cross")
    n_cross = lax.axis_size("cross")
    place = lax.rem(solve, GROUP)
    group = lax.div(solve, GROUP)
    base = solve - place

    loads_in = [
        pltpu.make_async_copy(src, dst, in_sem.at[i])
        for i, (src, dst) in enumerate(
            ((temp_hbm, temp), (diff_hbm, diff), (face_hbm, face), (sheet_hbm, sheet))
        )
    ]
    for copy in loads_in:
        copy.start()

    order = [8, 9, 7, 10, 6, 11, 5, 12, 4, 13, 3, 14, 2, 15, 1]
    mates = [lax.rem(place + step, GROUP) for step in order]
    others = [lax.rem(group + step, groups) for step in range(1, groups)]
    right = lax.rem(cross + 1, n_cross)
    left = lax.rem(cross + n_cross - 1, n_cross)

    barrier = pltpu.get_barrier_semaphore()
    for side in (left, right):
        pl.semaphore_signal(barrier, 1, device_id={"cross": side}, device_id_type=MESH)
    for mate in mates:
        pl.semaphore_signal(barrier, 1, device_id={"solve": base + mate}, device_id_type=MESH)
    for other in others:
        pl.semaphore_signal(
            barrier, 1, device_id={"solve": other * GROUP + place}, device_id_type=MESH
        )

    lane = lax.broadcasted_iota(jnp.int32, (SUBS, LANES), 1)
    sub = lax.broadcasted_iota(jnp.int32, (SUBS, LANES), 0)
    low = lane < HALF

    def spin(value, shift):
        return pltpu.roll(value, shift % LANES, 1)

    def tile(ref, block, column):
        return ref[pl.ds((block * SUBS + column) * SUBS, SUBS), :]

    loads_in[0].wait()
    loads_in[1].wait()
    edges = []
    for column, shift in ((0, 0), (SUBS - 1, 1)):
        packed = jnp.zeros((SUBS, LANES), jnp.float32)
        for j in range(8):
            part = tile(temp if j < 4 else diff, j % 4, column)
            packed = jnp.where(lane == j, spin(part, j + shift), packed)
        edges.append(packed)
    edge_send[0] = edges[0]
    edge_send[1] = edges[1]

    pl.semaphore_wait(barrier, 2 + len(mates) + len(others))
    edge_copies = [
        pltpu.make_async_remote_copy(
            src_ref=edge_send.at[i],
            dst_ref=edge_recv.at[i],
            send_sem=edge_ssem.at[i],
            recv_sem=edge_rsem.at[i],
            device_id={"cross": side},
            device_id_type=MESH,
        )
        for i, side in enumerate((left, right))
    ]
    for copy in edge_copies:
        copy.start()

    zero = jnp.zeros((SUBS, LANES), jnp.float32)
    for block in range(4):
        heat = [tile(temp, block, t) for t in range(SUBS)]
        cond = [tile(diff, block, t) for t in range(SUBS)]
        heat_turned = [spin(v, -1) for v in heat] + [zero]
        cond_turned = [spin(v, -1) for v in cond] + [zero]
        last = lane == LANES - 1
        before = zero
        for t in range(SUBS):
            next_heat = jnp.where(last, heat_turned[t + 1], heat_turned[t])
            next_cond = jnp.where(last, cond_turned[t + 1], cond_turned[t])
            flux = 0.5 * (cond[t] + next_cond) * (next_heat - heat[t])
            if t == SUBS - 1:
                flux = jnp.where(last, 0.0, flux)
            turned = spin(flux, 1)
            previous = jnp.where(lane == 0, before, turned)
            before = turned
            source[pl.ds((block * SUBS + t) * SUBS, SUBS), :] = heat[t] + flux - previous

    def row(ref, plane, i):
        start = (plane * 2 + i // SUBS) * SUBS * SUBS + i % SUBS
        return ref[pl.ds(start, SUBS, stride=SUBS), :]

    loads_in[2].wait()
    loads_in[3].wait()
    backs = []
    level = []
    back = []
    for m in range(ROWS // 2):
        element, way = merge_leaf(
            row(sheet, 0, 2 * m),
            row(sheet, 0, 2 * m + 1),
            row(face, 0, 2 * m),
            row(face, 1, 2 * m),
            row(face, 0, 2 * m + 1),
            row(face, 1, 2 * m + 1),
        )
        level.append(element)
        back.append(way)
    backs.append(back)
    while len(level) > 1:
        pairs = [merge(level[2 * m], level[2 * m + 1]) for m in range(len(level) // 2)]
        level = [pair[0] for pair in pairs]
        backs.append([pair[1] for pair in pairs])
    element = level[0]

    for i in (0, 1):
        edge_copies[i].wait_recv()
    for column, own, got, inside in (
        (0, edges[0], edge_recv[1], cross > 0),
        (SUBS - 1, edges[1], edge_recv[0], cross < n_cross - 1),
    ):
        got = jnp.where(inside, got, 0.0)
        flux = 0.5 * spin(own + got, -4) * (got - own)
        at = 0 if column == 0 else LANES - 1
        for j in range(4):
            where = pl.ds((j * SUBS + column) * SUBS, SUBS)
            source[where, :] += jnp.where(lane == at, spin(flux, at - j), 0.0)

    owns = []
    level = []
    own = []
    for m in range(ROWS // 2):
        loads, value = merge_leaf_loads(
            backs[0][m],
            (row(source, 0, 2 * m), row(source, 1, 2 * m)),
            (row(source, 0, 2 * m + 1), row(source, 1, 2 * m + 1)),
        )
        level.append(loads)
        own.append(value)
    owns.append(own)
    for back in backs[1:]:
        pairs = [
            merge_loads(back[m], level[2 * m], level[2 * m + 1]) for m in range(len(back))
        ]
        level = [pair[0] for pair in pairs]
        owns.append([pair[1] for pair in pairs])

    fields = element + level[0]
    for j in range(NFIELD // 2):
        lo, hi = fields[j], fields[j + NFIELD // 2]
        part_send[pl.ds(j, SUBS, stride=2 * SUBS), :] = jnp.where(low, lo, spin(hi, HALF))
        part_send[pl.ds(SUBS + j, SUBS, stride=2 * SUBS), :] = jnp.where(low, spin(lo, HALF), hi)
    for half in (0, SUBS):
        part_send[pl.ds(half + SUBS - 1, SUBS, stride=2 * SUBS), :] = zero

    def slot(ref, index, rows):
        return ref.at[pl.ds(pl.multiple_of(index * rows, rows), rows)]

    part_copies = [
        pltpu.make_async_remote_copy(
            src_ref=slot(part_send, mate, SUBS),
            dst_ref=slot(part_recv, place, SUBS),
            send_sem=part_ssem,
            recv_sem=part_rsem,
            device_id={"solve": base + mate},
            device_id_type=MESH,
        )
        for mate in mates
    ]
    for copy in part_copies:
        copy.start()
    here = pl.ds(pl.multiple_of(place * SUBS, SUBS), SUBS)
    part_recv[here, :] = part_send[here, :]
    everything = part_recv.at[pl.ds(0, (GROUP - 1) * SUBS)]
    pltpu.make_async_copy(everything, everything, part_rsem).wait()

    def unpack(offset):
        rows = [
            part_recv[pl.ds(offset + j, SUBS, stride=2 * SUBS), :] for j in range(NFIELD // 2)
        ]
        return tuple(rows) + tuple(spin(value, HALF) for value in rows)

    def climb(left_fields, right_fields):
        element, way = merge(left_fields[:10], right_fields[:10])
        loads, value = merge_loads(way, left_fields[10:], right_fields[10:])
        return element + loads, way, value

    def lift(value, shift):
        return pltpu.roll(value, SUBS - shift, 0)

    def drop(value, shift):
        return pltpu.roll(value, shift, 0)

    trail = []
    fields, way, value = climb(unpack(0), unpack(SUBS))
    trail.append((way, value, 0))
    for shift in (1, 2, 4):
        fields, way, value = climb(fields, tuple(lift(v, shift) for v in fields))
        trail.append((way, value, shift))

    for j in range(NFIELD):
        line_send[pl.ds(j, 1), :] = fields[j][0:1, :]
    line_send[pl.ds(NFIELD, 2), :] = zero[0:2, :]
    line_copies = [
        pltpu.make_async_remote_copy(
            src_ref=line_send,
            dst_ref=slot(line_recv, group, 2 * SUBS),
            send_sem=line_ssem,
            recv_sem=line_rsem,
            device_id={"solve": other * GROUP + place},
            device_id_type=MESH,
        )
        for other in others
    ]
    for copy in line_copies:
        copy.start()
    line_recv[pl.ds(pl.multiple_of(group * 2 * SUBS, 2 * SUBS), 2 * SUBS), :] = line_send[...]
    everything = line_recv.at[pl.ds(0, (groups - 1) * 2 * SUBS)]
    pltpu.make_async_copy(everything, everything, line_rsem).wait()

    chain = []
    for g in range(groups):
        chain.append(
            tuple(line_recv[pl.ds(g * 2 * SUBS + j, 1), :] for j in range(NFIELD))
        )
    steps = []
    while len(chain) > 1:
        joined = [climb(chain[2 * m], chain[2 * m + 1]) for m in range(len(chain) // 2)]
        steps.append([item[1:] for item in joined])
        chain = [item[0] for item in joined]
    ea1, ea2, sa, n11, n12, n21, n22, _, _, _, f1, f2, _, _ = chain[0]
    i11, i12, i22 = inverse(sa, ea1 + (n11 + n12), ea2 + (n21 + n22))
    nothing = jnp.zeros_like(f1)
    nodes = [(i11 * f1 + i12 * f2, i12 * f1 + i22 * f2), (nothing, nothing)]
    for step in reversed(steps):
        finer = []
        for m, (way, value) in enumerate(step):
            finer += [nodes[m], middle(way, value, nodes[m], nodes[m + 1])]
        nodes = finer + [nodes[-1]]
    for plane in (0, 1):
        for g in range(groups + 1):
            pick[plane, pl.ds(g, 1), :] = nodes[g][plane]
    ends = []
    for step in (0, 1):
        ends.append(
            tuple(
                jnp.broadcast_to(pick[plane, pl.ds(group + step, 1), :], (SUBS, LANES))
                for plane in (0, 1)
            )
        )
    before, after = ends

    for way, value, shift in reversed(trail):
        inner = middle(way, value, before, after)
        if shift == 0:
            break
        first = (sub & shift) == 0
        before = tuple(jnp.where(first, b, drop(v, shift)) for b, v in zip(before, inner))
        after = tuple(jnp.where(first, v, drop(a, shift)) for v, a in zip(inner, after))

    def both(pair):
        return jnp.where(low, pair[0], spin(pair[1], HALF))

    start_row, inner_row, end_row = both(before), both(inner), both(after)
    for j, value in enumerate((start_row, inner_row, inner_row, end_row)):
        node_send[pl.ds(j, SUBS, stride=4), :] = value
    node_copies = [
        pltpu.make_async_remote_copy(
            src_ref=slot(node_send, mate, 2),
            dst_ref=slot(node_recv, place, 2),
            send_sem=node_ssem,
            recv_sem=node_rsem,
            device_id={"solve": base + mate},
            device_id_type=MESH,
        )
        for mate in mates
    ]
    for copy in node_copies:
        copy.start()
    here = pl.ds(pl.multiple_of(place * 2, 2), 2)
    node_recv[here, :] = node_send[here, :]
    everything = node_recv.at[pl.ds(0, (GROUP - 1) * 2)]
    pltpu.make_async_copy(everything, everything, node_rsem).wait()

    ends = []
    for j in (0, 1):
        lower_half = node_recv[pl.ds(j, SUBS, stride=4), :]
        upper_half = node_recv[pl.ds(2 + j, SUBS, stride=4), :]
        ends.append(
            (
                jnp.where(low, lower_half, spin(upper_half, HALF)),
                jnp.where(low, spin(lower_half, HALF), upper_half),
            )
        )

    nodes = ends
    for back, own in zip(reversed(backs), reversed(owns)):
        finer = []
        for m in range(len(back)):
            finer += [nodes[m], middle(back[m], own[m], nodes[m], nodes[m + 1])]
        nodes = finer + [nodes[-1]]
    for i in range(ROWS):
        for plane in (0, 1):
            start = (plane * 2 + i // SUBS) * SUBS * SUBS + i % SUBS
            out_ref[pl.ds(start, SUBS, stride=SUBS), :] = nodes[i][plane]

    for copy in edge_copies:
        copy.wait_send()
    sent = part_send.at[pl.ds(0, (GROUP - 1) * SUBS)]
    pltpu.make_async_copy(sent, sent, part_ssem).wait()
    sent = line_recv.at[pl.ds(0, (groups - 1) * 2 * SUBS)]
    pltpu.make_async_copy(sent, sent, line_ssem).wait()
    sent = node_send.at[pl.ds(0, (GROUP - 1) * 2)]
    pltpu.make_async_copy(sent, sent, node_ssem).wait()


def tiles(array):
    array = array.reshape(-1, ROWS // SUBS, SUBS, SUBS, LANES)
    return array.transpose(0, 1, 3, 2, 4).reshape(-1, LANES)


def per_device(temperature, transfer, diffusivity, exchange):
    groups = lax.axis_size("solve") // GROUP
    vmem = lambda *shape: pltpu.VMEM(shape, jnp.float32)
    dma = pltpu.SemaphoreType.DMA
    out = pl.pallas_call(
        functools.partial(kernel, groups),
        out_shape=jax.ShapeDtypeStruct((FLAT, LANES), jnp.float32),
        in_specs=[pl.BlockSpec(memory_space=pltpu.HBM)] * 4,
        out_specs=pl.BlockSpec(memory_space=pltpu.VMEM),
        scratch_shapes=[
            vmem(FLAT, LANES),
            vmem(FLAT, LANES),
            vmem(FLAT, LANES),
            vmem(FLAT // 2, LANES),
            vmem(FLAT, LANES),
            vmem(2, SUBS, LANES),
            vmem(2, SUBS, LANES),
            vmem(GROUP * SUBS, LANES),
            vmem(GROUP * SUBS, LANES),
            vmem(2 * SUBS, LANES),
            vmem(groups * 2 * SUBS, LANES),
            vmem(2, SUBS, LANES),
            vmem(GROUP * 2, LANES),
            vmem(GROUP * 2, LANES),
            dma((4,)),
            dma((2,)),
            dma((2,)),
            dma,
            dma,
            dma,
            dma,
            dma,
            dma,
        ],
        compiler_params=pltpu.CompilerParams(
            collective_id=0, has_side_effects=True, vmem_limit_bytes=60 * 1024 * 1024
        ),
        cost_estimate=pl.CostEstimate(
            flops=4_000_000, bytes_accessed=600_000, transcendentals=0
        ),
        name="line_step",
    )(tiles(temperature), tiles(transfer), tiles(diffusivity), tiles(exchange))
    out = out.reshape(2, ROWS // SUBS, SUBS, SUBS, LANES).transpose(0, 1, 3, 2, 4)
    return out.reshape(2, ROWS, SUBS * LANES)


def solution(mesh):
    specs = (P(None, "solve", "cross"),) * 3 + (P("solve", "cross"),)
    return jax.shard_map(
        per_device,
        mesh=mesh,
        in_specs=specs,
        out_specs=P(None, "solve", "cross"),
        check_vma=False,
    )
```

```python
import functools

import jax
import jax.numpy as jnp
from jax import lax
from jax.experimental import pallas as pl
from jax.experimental.pallas import tpu as pltpu
from jax.sharding import PartitionSpec as P

MESH = pl.DeviceIdType.MESH
ROWS, SUBS, LANES = 16, 8, 128
GROUP = 16
HALF = LANES // 2
FLAT = 2 * ROWS * SUBS
NFIELD = 14


def inverse(coupling, first, second):
    scale = 1.0 / (coupling * (first + second) + first * second)
    return (coupling + second) * scale, coupling * scale, (coupling + first) * scale


def merge(left, right):
    ea1, ea2, sa, n11, n12, n21, n22, ec1, ec2, sc = left
    fa1, fa2, fs, m11, m12, m21, m22, fc1, fc2, gs = right
    eb1, eb2, sb = ec1 + fa1, ec2 + fa2, sc + fs
    r1 = eb1 + ((n11 + n21) + (m11 + m12))
    r2 = eb2 + ((n12 + n22) + (m21 + m22))
    i11, i12, i22 = inverse(sb, r1, r2)
    g11, g12 = n11 * i11 + n12 * i12, n11 * i12 + n12 * i22
    g21, g22 = n21 * i11 + n22 * i12, n21 * i12 + n22 * i22
    h11, h12 = i11 * m11 + i12 * m21, i11 * m12 + i12 * m22
    h21, h22 = i12 * m11 + i22 * m21, i12 * m12 + i22 * m22
    joined = (
        ea1 + (g11 * eb1 + g12 * eb2),
        ea2 + (g21 * eb1 + g22 * eb2),
        sa + (g11 * n21 + g12 * n22),
        g11 * m11 + g12 * m21,
        g11 * m12 + g12 * m22,
        g21 * m11 + g22 * m21,
        g21 * m12 + g22 * m22,
        fc1 + (h11 * eb1 + h21 * eb2),
        fc2 + (h12 * eb1 + h22 * eb2),
        gs + (m11 * h12 + m21 * h22),
    )
    return joined, (i11, i12, i22, g11, g12, g21, g22, h11, h12, h21, h22)


def merge_leaf(sa, sb, n1, n2, m1, m2):
    r1, r2 = 1.0 + (n1 + m1), 1.0 + (n2 + m2)
    i11, i12, i22 = inverse(sb, r1, r2)
    g11, g12, g21, g22 = n1 * i11, n1 * i12, n2 * i12, n2 * i22
    h11, h12, h21, h22 = i11 * m1, i12 * m2, i12 * m1, i22 * m2
    joined = (
        1.0 + (g11 + g12),
        1.0 + (g21 + g22),
        sa + g12 * n2,
        g11 * m1,
        g12 * m2,
        g21 * m1,
        g22 * m2,
        h11 + h21,
        h12 + h22,
        m1 * h12,
    )
    return joined, (i11, i12, i22, g11, g12, g21, g22, h11, h12, h21, h22)


def merge_loads(back, left, right):
    i11, i12, i22, g11, g12, g21, g22, h11, h12, h21, h22 = back
    a1, a2, b1, b2 = left
    c1, c2, d1, d2 = right
    b1, b2 = b1 + c1, b2 + c2
    loads = (
        a1 + (g11 * b1 + g12 * b2),
        a2 + (g21 * b1 + g22 * b2),
        d1 + (h11 * b1 + h21 * b2),
        d2 + (h12 * b1 + h22 * b2),
    )
    return loads, (i11 * b1 + i12 * b2, i12 * b1 + i22 * b2)


def merge_leaf_loads(back, a, b):
    i11, i12, i22, g11, g12, g21, g22, h11, h12, h21, h22 = back
    a1, a2 = a
    b1, b2 = b
    loads = (
        a1 + (g11 * b1 + g12 * b2),
        a2 + (g21 * b1 + g22 * b2),
        h11 * b1 + h21 * b2,
        h12 * b1 + h22 * b2,
    )
    return loads, (i11 * b1 + i12 * b2, i12 * b1 + i22 * b2)


def middle(back, own, before, after):
    g11, g12, g21, g22, h11, h12, h21, h22 = back[3:]
    a1, a2 = before
    c1, c2 = after
    return (
        own[0] + ((g11 * a1 + g21 * a2) + (h11 * c1 + h12 * c2)),
        own[1] + ((g12 * a1 + g22 * a2) + (h21 * c1 + h22 * c2)),
    )


def kernel(
    groups,
    temp_hbm,
    face_hbm,
    diff_hbm,
    sheet_hbm,
    out_ref,
    temp,
    face,
    diff,
    sheet,
    source,
    edge_send,
    edge_recv,
    part_send,
    part_recv,
    line_send,
    line_recv,
    pick,
    node_send,
    node_recv,
    in_sem,
    edge_ssem,
    edge_rsem,
    part_ssem,
    part_rsem,
    line_ssem,
    line_rsem,
    node_ssem,
    node_rsem,
):
    solve = lax.axis_index("solve")
    cross = lax.axis_index("cross")
    n_cross = lax.axis_size("cross")
    place = lax.rem(solve, GROUP)
    group = lax.div(solve, GROUP)
    base = solve - place

    loads_in = [
        pltpu.make_async_copy(src, dst, in_sem.at[i])
        for i, (src, dst) in enumerate(
            ((temp_hbm, temp), (diff_hbm, diff), (face_hbm, face), (sheet_hbm, sheet))
        )
    ]
    for copy in loads_in:
        copy.start()

    order = [8, 9, 7, 10, 6, 11, 5, 12, 4, 13, 3, 14, 2, 15, 1]
    mates = [lax.rem(place + step, GROUP) for step in order]
    others = [lax.rem(group + step, groups) for step in range(1, groups)]
    right = lax.rem(cross + 1, n_cross)
    left = lax.rem(cross + n_cross - 1, n_cross)

    barrier = pltpu.get_barrier_semaphore()
    for side in (left, right):
        pl.semaphore_signal(barrier, 1, device_id={"cross": side}, device_id_type=MESH)
    for mate in mates:
        pl.semaphore_signal(barrier, 1, device_id={"solve": base + mate}, device_id_type=MESH)
    for other in others:
        pl.semaphore_signal(
            barrier, 1, device_id={"solve": other * GROUP + place}, device_id_type=MESH
        )

    lane = lax.broadcasted_iota(jnp.int32, (SUBS, LANES), 1)
    sub = lax.broadcasted_iota(jnp.int32, (SUBS, LANES), 0)
    low = lane < HALF

    def spin(value, shift):
        return pltpu.roll(value, shift % LANES, 1)

    def tile(ref, block, column):
        return ref[pl.ds((block * SUBS + column) * SUBS, SUBS), :]

    loads_in[0].wait()
    loads_in[1].wait()
    edges = []
    for column, shift in ((0, 0), (SUBS - 1, 1)):
        packed = jnp.zeros((SUBS, LANES), jnp.float32)
        for j in range(8):
            part = tile(temp if j < 4 else diff, j % 4, column)
            packed = jnp.where(lane == j, spin(part, j + shift), packed)
        edges.append(packed)
    edge_send[0] = edges[0]
    edge_send[1] = edges[1]

    pl.semaphore_wait(barrier, 2 + len(mates) + len(others))
    edge_copies = [
        pltpu.make_async_remote_copy(
            src_ref=edge_send.at[i],
            dst_ref=edge_recv.at[i],
            send_sem=edge_ssem.at[i],
            recv_sem=edge_rsem.at[i],
            device_id={"cross": side},
            device_id_type=MESH,
        )
        for i, side in enumerate((left, right))
    ]
    for copy in edge_copies:
        copy.start()

    zero = jnp.zeros((SUBS, LANES), jnp.float32)
    for block in range(4):
        heat = [tile(temp, block, t) for t in range(SUBS)]
        cond = [tile(diff, block, t) for t in range(SUBS)]
        heat_turned = [spin(v, -1) for v in heat] + [zero]
        cond_turned = [spin(v, -1) for v in cond] + [zero]
        last = lane == LANES - 1
        before = zero
        for t in range(SUBS):
            next_heat = jnp.where(last, heat_turned[t + 1], heat_turned[t])
            next_cond = jnp.where(last, cond_turned[t + 1], cond_turned[t])
            flux = 0.5 * (cond[t] + next_cond) * (next_heat - heat[t])
            if t == SUBS - 1:
                flux = jnp.where(last, 0.0, flux)
            turned = spin(flux, 1)
            previous = jnp.where(lane == 0, before, turned)
            before = turned
            source[pl.ds((block * SUBS + t) * SUBS, SUBS), :] = heat[t] + flux - previous

    def row(ref, plane, i):
        start = (plane * 2 + i // SUBS) * SUBS * SUBS + i % SUBS
        return ref[pl.ds(start, SUBS, stride=SUBS), :]

    loads_in[2].wait()
    loads_in[3].wait()
    backs = []
    level = []
    back = []
    for m in range(ROWS // 2):
        element, way = merge_leaf(
            row(sheet, 0, 2 * m),
            row(sheet, 0, 2 * m + 1),
            row(face, 0, 2 * m),
            row(face, 1, 2 * m),
            row(face, 0, 2 * m + 1),
            row(face, 1, 2 * m + 1),
        )
        level.append(element)
        back.append(way)
    backs.append(back)
    while len(level) > 1:
        pairs = [merge(level[2 * m], level[2 * m + 1]) for m in range(len(level) // 2)]
        level = [pair[0] for pair in pairs]
        backs.append([pair[1] for pair in pairs])
    element = level[0]

    for i in (0, 1):
        edge_copies[i].wait_recv()
    for column, own, got, inside in (
        (0, edges[0], edge_recv[1], cross > 0),
        (SUBS - 1, edges[1], edge_recv[0], cross < n_cross - 1),
    ):
        got = jnp.where(inside, got, 0.0)
        flux = 0.5 * spin(own + got, -4) * (got - own)
        at = 0 if column == 0 else LANES - 1
        for j in range(4):
            where = pl.ds((j * SUBS + column) * SUBS, SUBS)
            source[where, :] += jnp.where(lane == at, spin(flux, at - j), 0.0)

    owns = []
    level = []
    own = []
    for m in range(ROWS // 2):
        loads, value = merge_leaf_loads(
            backs[0][m],
            (row(source, 0, 2 * m), row(source, 1, 2 * m)),
            (row(source, 0, 2 * m + 1), row(source, 1, 2 * m + 1)),
        )
        level.append(loads)
        own.append(value)
    owns.append(own)
    for back in backs[1:]:
        pairs = [
            merge_loads(back[m], level[2 * m], level[2 * m + 1]) for m in range(len(back))
        ]
        level = [pair[0] for pair in pairs]
        owns.append([pair[1] for pair in pairs])

    fields = element + level[0]
    for j in range(NFIELD // 2):
        lo, hi = fields[j], fields[j + NFIELD // 2]
        part_send[pl.ds(j, SUBS, stride=2 * SUBS), :] = jnp.where(low, lo, spin(hi, HALF))
        part_send[pl.ds(SUBS + j, SUBS, stride=2 * SUBS), :] = jnp.where(low, spin(lo, HALF), hi)
    for half in (0, SUBS):
        part_send[pl.ds(half + SUBS - 1, SUBS, stride=2 * SUBS), :] = zero

    def slot(ref, index, rows):
        return ref.at[pl.ds(pl.multiple_of(index * rows, rows), rows)]

    part_copies = [
        pltpu.make_async_remote_copy(
            src_ref=slot(part_send, mate, SUBS),
            dst_ref=slot(part_recv, place, SUBS),
            send_sem=part_ssem,
            recv_sem=part_rsem,
            device_id={"solve": base + mate},
            device_id_type=MESH,
        )
        for mate in mates
    ]
    for copy in part_copies:
        copy.start()
    here = pl.ds(pl.multiple_of(place * SUBS, SUBS), SUBS)
    part_recv[here, :] = part_send[here, :]
    everything = part_recv.at[pl.ds(0, (GROUP - 1) * SUBS)]
    pltpu.make_async_copy(everything, everything, part_rsem).wait()

    def unpack(offset):
        rows = [
            part_recv[pl.ds(offset + j, SUBS, stride=2 * SUBS), :] for j in range(NFIELD // 2)
        ]
        return tuple(rows) + tuple(spin(value, HALF) for value in rows)

    def climb(left_fields, right_fields):
        element, way = merge(left_fields[:10], right_fields[:10])
        loads, value = merge_loads(way, left_fields[10:], right_fields[10:])
        return element + loads, way, value

    def lift(value, shift):
        return pltpu.roll(value, SUBS - shift, 0)

    def drop(value, shift):
        return pltpu.roll(value, shift, 0)

    trail = []
    fields, way, value = climb(unpack(0), unpack(SUBS))
    trail.append((way, value, 0))
    for shift in (1, 2, 4):
        fields, way, value = climb(fields, tuple(lift(v, shift) for v in fields))
        trail.append((way, value, shift))

    for j in range(NFIELD):
        line_send[pl.ds(j, 1), :] = fields[j][0:1, :]
    line_send[pl.ds(NFIELD, 2), :] = zero[0:2, :]
    line_copies = [
        pltpu.make_async_remote_copy(
            src_ref=line_send,
            dst_ref=slot(line_recv, group, 2 * SUBS),
            send_sem=line_ssem,
            recv_sem=line_rsem,
            device_id={"solve": other * GROUP + place},
            device_id_type=MESH,
        )
        for other in others
    ]
    for copy in line_copies:
        copy.start()
    line_recv[pl.ds(pl.multiple_of(group * 2 * SUBS, 2 * SUBS), 2 * SUBS), :] = line_send[...]
    everything = line_recv.at[pl.ds(0, (groups - 1) * 2 * SUBS)]
    pltpu.make_async_copy(everything, everything, line_rsem).wait()

    chain = []
    for g in range(groups):
        chain.append(
            tuple(line_recv[pl.ds(g * 2 * SUBS + j, 1), :] for j in range(NFIELD))
        )
    steps = []
    while len(chain) > 1:
        joined = [climb(chain[2 * m], chain[2 * m + 1]) for m in range(len(chain) // 2)]
        steps.append([item[1:] for item in joined])
        chain = [item[0] for item in joined]
    ea1, ea2, sa, n11, n12, n21, n22, _, _, _, f1, f2, _, _ = chain[0]
    i11, i12, i22 = inverse(sa, ea1 + (n11 + n12), ea2 + (n21 + n22))
    nothing = jnp.zeros_like(f1)
    nodes = [(i11 * f1 + i12 * f2, i12 * f1 + i22 * f2), (nothing, nothing)]
    for step in reversed(steps):
        finer = []
        for m, (way, value) in enumerate(step):
            finer += [nodes[m], middle(way, value, nodes[m], nodes[m + 1])]
        nodes = finer + [nodes[-1]]
    for plane in (0, 1):
        for g in range(groups + 1):
            pick[plane, pl.ds(g, 1), :] = nodes[g][plane]
    ends = []
    for step in (0, 1):
        ends.append(
            tuple(
                jnp.broadcast_to(pick[plane, pl.ds(group + step, 1), :], (SUBS, LANES))
                for plane in (0, 1)
            )
        )
    before, after = ends

    for way, value, shift in reversed(trail):
        inner = middle(way, value, before, after)
        if shift == 0:
            break
        first = (sub & shift) == 0
        before = tuple(jnp.where(first, b, drop(v, shift)) for b, v in zip(before, inner))
        after = tuple(jnp.where(first, v, drop(a, shift)) for v, a in zip(inner, after))

    def both(pair):
        return jnp.where(low, pair[0], spin(pair[1], HALF))

    start_row, inner_row, end_row = both(before), both(inner), both(after)
    for j, value in enumerate((start_row, inner_row, inner_row, end_row)):
        node_send[pl.ds(j, SUBS, stride=4), :] = value
    node_copies = [
        pltpu.make_async_remote_copy(
            src_ref=slot(node_send, mate, 2),
            dst_ref=slot(node_recv, place, 2),
            send_sem=node_ssem,
            recv_sem=node_rsem,
            device_id={"solve": base + mate},
            device_id_type=MESH,
        )
        for mate in mates
    ]
    for copy in node_copies:
        copy.start()
    here = pl.ds(pl.multiple_of(place * 2, 2), 2)
    node_recv[here, :] = node_send[here, :]
    everything = node_recv.at[pl.ds(0, (GROUP - 1) * 2)]
    pltpu.make_async_copy(everything, everything, node_rsem).wait()

    ends = []
    for j in (0, 1):
        lower_half = node_recv[pl.ds(j, SUBS, stride=4), :]
        upper_half = node_recv[pl.ds(2 + j, SUBS, stride=4), :]
        ends.append(
            (
                jnp.where(low, lower_half, spin(upper_half, HALF)),
                jnp.where(low, spin(lower_half, HALF), upper_half),
            )
        )

    nodes = ends
    for back, own in zip(reversed(backs), reversed(owns)):
        finer = []
        for m in range(len(back)):
            finer += [nodes[m], middle(back[m], own[m], nodes[m], nodes[m + 1])]
        nodes = finer + [nodes[-1]]
    for i in range(ROWS):
        for plane in (0, 1):
            start = (plane * 2 + i // SUBS) * SUBS * SUBS + i % SUBS
            out_ref[pl.ds(start, SUBS, stride=SUBS), :] = nodes[i][plane]

    for copy in edge_copies:
        copy.wait_send()
    sent = part_send.at[pl.ds(0, (GROUP - 1) * SUBS)]
    pltpu.make_async_copy(sent, sent, part_ssem).wait()
    sent = line_recv.at[pl.ds(0, (groups - 1) * 2 * SUBS)]
    pltpu.make_async_copy(sent, sent, line_ssem).wait()
    sent = node_send.at[pl.ds(0, (GROUP - 1) * 2)]
    pltpu.make_async_copy(sent, sent, node_ssem).wait()


def tiles(array):
    array = array.reshape(-1, ROWS // SUBS, SUBS, SUBS, LANES)
    return array.transpose(0, 1, 3, 2, 4).reshape(-1, LANES)


def per_device(temperature, transfer, diffusivity, exchange):
    groups = lax.axis_size("solve") // GROUP
    vmem = lambda *shape: pltpu.VMEM(shape, jnp.float32)
    dma = pltpu.SemaphoreType.DMA
    out = pl.pallas_call(
        functools.partial(kernel, groups),
        out_shape=jax.ShapeDtypeStruct((FLAT, LANES), jnp.float32),
        in_specs=[pl.BlockSpec(memory_space=pltpu.HBM)] * 4,
        out_specs=pl.BlockSpec(memory_space=pltpu.VMEM),
        scratch_shapes=[
            vmem(FLAT, LANES),
            vmem(FLAT, LANES),
            vmem(FLAT, LANES),
            vmem(FLAT // 2, LANES),
            vmem(FLAT, LANES),
            vmem(2, SUBS, LANES),
            vmem(2, SUBS, LANES),
            vmem(GROUP * SUBS, LANES),
            vmem(GROUP * SUBS, LANES),
            vmem(2 * SUBS, LANES),
            vmem(groups * 2 * SUBS, LANES),
            vmem(2, SUBS, LANES),
            vmem(GROUP * 2, LANES),
            vmem(GROUP * 2, LANES),
            dma((4,)),
            dma((2,)),
            dma((2,)),
            dma,
            dma,
            dma,
            dma,
            dma,
            dma,
        ],
        compiler_params=pltpu.CompilerParams(
            collective_id=0, has_side_effects=True, vmem_limit_bytes=16 * 1024 * 1024
        ),
        cost_estimate=pl.CostEstimate(
            flops=4_000_000, bytes_accessed=600_000, transcendentals=0
        ),
        name="line_step",
    )(
        *(
            pltpu.with_memory_space_constraint(tiles(array), pltpu.HBM)
            for array in (temperature, transfer, diffusivity, exchange)
        )
    )
    out = out.reshape(2, ROWS // SUBS, SUBS, SUBS, LANES).transpose(0, 1, 3, 2, 4)
    return out.reshape(2, ROWS, SUBS * LANES)


def solution(mesh):
    specs = (P(None, "solve", "cross"),) * 3 + (P("solve", "cross"),)
    return jax.shard_map(
        per_device,
        mesh=mesh,
        in_specs=specs,
        out_specs=P(None, "solve", "cross"),
        check_vma=False,
    )
```

```python
import jax
import jax.numpy as jnp
from jax import lax
from jax.experimental import pallas as pl
from jax.experimental.pallas import tpu as pltpu
from jax.sharding import PartitionSpec as P

MESH = pl.DeviceIdType.MESH
ROWS, SUBS, LANES = 16, 8, 128
GROUP, GROUPS = 8, 8
SLOT = 16
FLAT = 2 * ROWS * SUBS
NFIELD = 14


def inverse(coupling, first, second):
    scale = 1.0 / (coupling * (first + second) + first * second)
    return (coupling + second) * scale, coupling * scale, (coupling + first) * scale


def merge(left, right):
    ea1, ea2, sa, n11, n12, n21, n22, ec1, ec2, sc = left
    fa1, fa2, fs, m11, m12, m21, m22, fc1, fc2, gs = right
    eb1, eb2, sb = ec1 + fa1, ec2 + fa2, sc + fs
    r1 = eb1 + ((n11 + n21) + (m11 + m12))
    r2 = eb2 + ((n12 + n22) + (m21 + m22))
    i11, i12, i22 = inverse(sb, r1, r2)
    g11, g12 = n11 * i11 + n12 * i12, n11 * i12 + n12 * i22
    g21, g22 = n21 * i11 + n22 * i12, n21 * i12 + n22 * i22
    h11, h12 = i11 * m11 + i12 * m21, i11 * m12 + i12 * m22
    h21, h22 = i12 * m11 + i22 * m21, i12 * m12 + i22 * m22
    joined = (
        ea1 + (g11 * eb1 + g12 * eb2),
        ea2 + (g21 * eb1 + g22 * eb2),
        sa + (g11 * n21 + g12 * n22),
        g11 * m11 + g12 * m21,
        g11 * m12 + g12 * m22,
        g21 * m11 + g22 * m21,
        g21 * m12 + g22 * m22,
        fc1 + (h11 * eb1 + h21 * eb2),
        fc2 + (h12 * eb1 + h22 * eb2),
        gs + (m11 * h12 + m21 * h22),
    )
    return joined, (i11, i12, i22, g11, g12, g21, g22, h11, h12, h21, h22)


def merge_leaf(sa, sb, n1, n2, m1, m2):
    r1, r2 = 1.0 + (n1 + m1), 1.0 + (n2 + m2)
    i11, i12, i22 = inverse(sb, r1, r2)
    g11, g12, g21, g22 = n1 * i11, n1 * i12, n2 * i12, n2 * i22
    h11, h12, h21, h22 = i11 * m1, i12 * m2, i12 * m1, i22 * m2
    joined = (
        1.0 + (g11 + g12),
        1.0 + (g21 + g22),
        sa + g12 * n2,
        g11 * m1,
        g12 * m2,
        g21 * m1,
        g22 * m2,
        h11 + h21,
        h12 + h22,
        m1 * h12,
    )
    return joined, (i11, i12, i22, g11, g12, g21, g22, h11, h12, h21, h22)


def merge_loads(back, left, right):
    i11, i12, i22, g11, g12, g21, g22, h11, h12, h21, h22 = back
    a1, a2, b1, b2 = left
    c1, c2, d1, d2 = right
    b1, b2 = b1 + c1, b2 + c2
    loads = (
        a1 + (g11 * b1 + g12 * b2),
        a2 + (g21 * b1 + g22 * b2),
        d1 + (h11 * b1 + h21 * b2),
        d2 + (h12 * b1 + h22 * b2),
    )
    return loads, (i11 * b1 + i12 * b2, i12 * b1 + i22 * b2)


def merge_leaf_loads(back, a, b):
    i11, i12, i22, g11, g12, g21, g22, h11, h12, h21, h22 = back
    a1, a2 = a
    b1, b2 = b
    loads = (
        a1 + (g11 * b1 + g12 * b2),
        a2 + (g21 * b1 + g22 * b2),
        h11 * b1 + h21 * b2,
        h12 * b1 + h22 * b2,
    )
    return loads, (i11 * b1 + i12 * b2, i12 * b1 + i22 * b2)


def middle(back, own, before, after):
    g11, g12, g21, g22, h11, h12, h21, h22 = back[3:]
    a1, a2 = before
    c1, c2 = after
    return (
        own[0] + ((g11 * a1 + g21 * a2) + (h11 * c1 + h12 * c2)),
        own[1] + ((g12 * a1 + g22 * a2) + (h21 * c1 + h22 * c2)),
    )


def kernel(
    temp_hbm,
    face_hbm,
    diff_hbm,
    sheet_hbm,
    out_ref,
    temp,
    face,
    diff,
    sheet,
    source,
    edge_send,
    edge_recv,
    part_send,
    part_recv,
    line_send,
    line_recv,
    pick,
    node_send,
    node_recv,
    in_sem,
    edge_ssem,
    edge_rsem,
    part_ssem,
    part_rsem,
    line_ssem,
    line_rsem,
    node_ssem,
    node_rsem,
):
    solve = lax.axis_index("solve")
    cross = lax.axis_index("cross")
    n_cross = lax.axis_size("cross")
    place = lax.rem(solve, GROUP)
    group = lax.div(solve, GROUP)
    base = solve - place

    loads_in = [
        pltpu.make_async_copy(src, dst, in_sem.at[i])
        for i, (src, dst) in enumerate(
            ((temp_hbm, temp), (diff_hbm, diff), (face_hbm, face), (sheet_hbm, sheet))
        )
    ]
    for copy in loads_in:
        copy.start()

    mates = [lax.rem(place + step, GROUP) for step in (4, 5, 3, 6, 2, 7, 1)]
    others = [lax.rem(group + step, GROUPS) for step in (1, 7, 3, 5, 2, 6, 4)]
    right = lax.rem(cross + 1, n_cross)
    left = lax.rem(cross + n_cross - 1, n_cross)

    barrier = pltpu.get_barrier_semaphore()
    for side in (left, right):
        pl.semaphore_signal(barrier, 1, device_id={"cross": side}, device_id_type=MESH)
    for mate in mates:
        pl.semaphore_signal(barrier, 1, device_id={"solve": base + mate}, device_id_type=MESH)
    for other in others:
        pl.semaphore_signal(
            barrier, 1, device_id={"solve": other * GROUP + place}, device_id_type=MESH
        )

    lane = lax.broadcasted_iota(jnp.int32, (SUBS, LANES), 1)
    sub = lax.broadcasted_iota(jnp.int32, (SUBS, LANES), 0)

    def spin(value, shift):
        return pltpu.roll(value, shift % LANES, 1)

    def tile(ref, block, column):
        return ref[pl.ds((block * SUBS + column) * SUBS, SUBS), :]

    loads_in[0].wait()
    loads_in[1].wait()
    edges = []
    for column, shift in ((0, 0), (SUBS - 1, 1)):
        packed = jnp.zeros((SUBS, LANES), jnp.float32)
        for j in range(8):
            part = tile(temp if j < 4 else diff, j % 4, column)
            packed = jnp.where(lane == j, spin(part, j + shift), packed)
        edges.append(packed)
    edge_send[0] = edges[0]
    edge_send[1] = edges[1]

    pl.semaphore_wait(barrier, 2 + len(mates) + len(others))
    edge_copies = [
        pltpu.make_async_remote_copy(
            src_ref=edge_send.at[i],
            dst_ref=edge_recv.at[i],
            send_sem=edge_ssem.at[i],
            recv_sem=edge_rsem.at[i],
            device_id={"cross": side},
            device_id_type=MESH,
        )
        for i, side in enumerate((left, right))
    ]
    for copy in edge_copies:
        copy.start()

    zero = jnp.zeros((SUBS, LANES), jnp.float32)
    for block in range(4):
        heat = [tile(temp, block, t) for t in range(SUBS)]
        cond = [tile(diff, block, t) for t in range(SUBS)]
        heat_turned = [spin(v, -1) for v in heat] + [zero]
        cond_turned = [spin(v, -1) for v in cond] + [zero]
        last = lane == LANES - 1
        before = zero
        for t in range(SUBS):
            next_heat = jnp.where(last, heat_turned[t + 1], heat_turned[t])
            next_cond = jnp.where(last, cond_turned[t + 1], cond_turned[t])
            flux = 0.5 * (cond[t] + next_cond) * (next_heat - heat[t])
            if t == SUBS - 1:
                flux = jnp.where(last, 0.0, flux)
            turned = spin(flux, 1)
            previous = jnp.where(lane == 0, before, turned)
            before = turned
            source[pl.ds((block * SUBS + t) * SUBS, SUBS), :] = heat[t] + flux - previous

    def row(ref, plane, i):
        start = (plane * 2 + i // SUBS) * SUBS * SUBS + i % SUBS
        return ref[pl.ds(start, SUBS, stride=SUBS), :]

    loads_in[2].wait()
    loads_in[3].wait()
    backs = []
    level = []
    back = []
    for m in range(ROWS // 2):
        element, way = merge_leaf(
            row(sheet, 0, 2 * m),
            row(sheet, 0, 2 * m + 1),
            row(face, 0, 2 * m),
            row(face, 1, 2 * m),
            row(face, 0, 2 * m + 1),
            row(face, 1, 2 * m + 1),
        )
        level.append(element)
        back.append(way)
    backs.append(back)
    while len(level) > 1:
        pairs = [merge(level[2 * m], level[2 * m + 1]) for m in range(len(level) // 2)]
        level = [pair[0] for pair in pairs]
        backs.append([pair[1] for pair in pairs])
    element = level[0]

    for i in (0, 1):
        edge_copies[i].wait_recv()
    for column, own, got, inside in (
        (0, edges[0], edge_recv[1], cross > 0),
        (SUBS - 1, edges[1], edge_recv[0], cross < n_cross - 1),
    ):
        got = jnp.where(inside, got, 0.0)
        flux = 0.5 * spin(own + got, -4) * (got - own)
        at = 0 if column == 0 else LANES - 1
        for j in range(4):
            where = pl.ds((j * SUBS + column) * SUBS, SUBS)
            source[where, :] += jnp.where(lane == at, spin(flux, at - j), 0.0)

    owns = []
    level = []
    own = []
    for m in range(ROWS // 2):
        loads, value = merge_leaf_loads(
            backs[0][m],
            (row(source, 0, 2 * m), row(source, 1, 2 * m)),
            (row(source, 0, 2 * m + 1), row(source, 1, 2 * m + 1)),
        )
        level.append(loads)
        own.append(value)
    owns.append(own)
    for back in backs[1:]:
        pairs = [
            merge_loads(back[m], level[2 * m], level[2 * m + 1]) for m in range(len(back))
        ]
        level = [pair[0] for pair in pairs]
        owns.append([pair[1] for pair in pairs])

    def slot(ref, index, rows, used):
        return ref.at[pl.ds(pl.multiple_of(index * rows, rows), used)]

    def climb(left_fields, right_fields):
        element, way = merge(left_fields[:10], right_fields[:10])
        loads, value = merge_loads(way, left_fields[10:], right_fields[10:])
        return element + loads, way, value

    def climb_all(fields):
        trail = []
        for shift in (1, 2, 4):
            raised = tuple(pltpu.roll(value, SUBS - shift, 0) for value in fields)
            fields, way, value = climb(fields, raised)
            trail.append((way, value, shift))
        return fields, trail

    def descend_all(trail, before, after):
        for way, value, shift in reversed(trail):
            inner = middle(way, value, before, after)
            first = (sub & shift) == 0
            before = tuple(
                jnp.where(first, b, pltpu.roll(v, shift, 0)) for b, v in zip(before, inner)
            )
            after = tuple(
                jnp.where(first, v, pltpu.roll(a, shift, 0)) for v, a in zip(inner, after)
            )
        return before, after

    fields = element + level[0]
    for j in range(NFIELD):
        part_send[pl.ds(j, SUBS, stride=SLOT), :] = fields[j]
    part_copies = [
        pltpu.make_async_remote_copy(
            src_ref=slot(part_send, mate, SLOT, NFIELD),
            dst_ref=slot(part_recv, place, SLOT, NFIELD),
            send_sem=part_ssem,
            recv_sem=part_rsem,
            device_id={"solve": base + mate},
            device_id_type=MESH,
        )
        for mate in mates
    ]
    for copy in part_copies:
        copy.start()
    here = pl.ds(pl.multiple_of(place * SLOT, SLOT), NFIELD)
    part_recv[here, :] = part_send[here, :]
    everything = part_recv.at[pl.ds(0, (GROUP - 1) * NFIELD)]
    pltpu.make_async_copy(everything, everything, part_rsem).wait()

    fields, trail = climb_all(
        tuple(part_recv[pl.ds(j, SUBS, stride=SLOT), :] for j in range(NFIELD))
    )

    for j in range(NFIELD):
        line_send[pl.ds(j, 1), :] = fields[j][0:1, :]
    line_copies = [
        pltpu.make_async_remote_copy(
            src_ref=line_send.at[pl.ds(0, NFIELD)],
            dst_ref=slot(line_recv, group, SLOT, NFIELD),
            send_sem=line_ssem,
            recv_sem=line_rsem,
            device_id={"solve": other * GROUP + place},
            device_id_type=MESH,
        )
        for other in others
    ]
    for copy in line_copies:
        copy.start()
    here = pl.ds(pl.multiple_of(group * SLOT, SLOT), NFIELD)
    line_recv[here, :] = line_send[pl.ds(0, NFIELD), :]
    everything = line_recv.at[pl.ds(0, (GROUPS - 1) * NFIELD)]
    pltpu.make_async_copy(everything, everything, line_rsem).wait()
    fields, line_trail = climb_all(
        tuple(line_recv[pl.ds(j, SUBS, stride=SLOT), :] for j in range(NFIELD))
    )
    ea1, ea2, sa, n11, n12, n21, n22, _, _, _, f1, f2, _, _ = fields
    i11, i12, i22 = inverse(sa, ea1 + (n11 + n12), ea2 + (n21 + n22))
    start_values = (i11 * f1 + i12 * f2, i12 * f1 + i22 * f2)
    before, after = descend_all(line_trail, start_values, (zero, zero))
    for j, value in enumerate(before + after):
        pick[j] = value
    values = [
        jnp.broadcast_to(pick[j, pl.ds(group, 1), :], (SUBS, LANES)) for j in range(4)
    ]

    before, after = descend_all(trail, tuple(values[:2]), tuple(values[2:]))
    for j, value in enumerate(before + after):
        node_send[pl.ds(j, SUBS, stride=4), :] = value
    node_copies = [
        pltpu.make_async_remote_copy(
            src_ref=slot(node_send, mate, 4, 4),
            dst_ref=slot(node_recv, place, 4, 4),
            send_sem=node_ssem,
            recv_sem=node_rsem,
            device_id={"solve": base + mate},
            device_id_type=MESH,
        )
        for mate in mates
    ]
    for copy in node_copies:
        copy.start()
    here = pl.ds(pl.multiple_of(place * 4, 4), 4)
    node_recv[here, :] = node_send[here, :]
    everything = node_recv.at[pl.ds(0, (GROUP - 1) * 4)]
    pltpu.make_async_copy(everything, everything, node_rsem).wait()
    values = [node_recv[pl.ds(j, SUBS, stride=4), :] for j in range(4)]
    ends = [tuple(values[:2]), tuple(values[2:])]

    nodes = ends
    for back, own in zip(reversed(backs), reversed(owns)):
        finer = []
        for m in range(len(back)):
            finer += [nodes[m], middle(back[m], own[m], nodes[m], nodes[m + 1])]
        nodes = finer + [nodes[-1]]
    for i in range(ROWS):
        for plane in (0, 1):
            start = (plane * 2 + i // SUBS) * SUBS * SUBS + i % SUBS
            out_ref[pl.ds(start, SUBS, stride=SUBS), :] = nodes[i][plane]

    for copy in edge_copies:
        copy.wait_send()
    for ref, sem, rows in (
        (part_send, part_ssem, (GROUP - 1) * NFIELD),
        (line_recv, line_ssem, (GROUPS - 1) * NFIELD),
        (node_send, node_ssem, (GROUP - 1) * 4),
    ):
        sent = ref.at[pl.ds(0, rows)]
        pltpu.make_async_copy(sent, sent, sem).wait()


def tiles(array):
    array = array.reshape(-1, ROWS // SUBS, SUBS, SUBS, LANES)
    return array.transpose(0, 1, 3, 2, 4).reshape(-1, LANES)


def per_device(temperature, transfer, diffusivity, exchange):
    vmem = lambda *shape: pltpu.VMEM(shape, jnp.float32)
    dma = pltpu.SemaphoreType.DMA
    out = pl.pallas_call(
        kernel,
        out_shape=jax.ShapeDtypeStruct((FLAT, LANES), jnp.float32),
        in_specs=[pl.BlockSpec(memory_space=pltpu.HBM)] * 4,
        out_specs=pl.BlockSpec(memory_space=pltpu.VMEM),
        scratch_shapes=[
            vmem(FLAT, LANES),
            vmem(FLAT, LANES),
            vmem(FLAT, LANES),
            vmem(FLAT // 2, LANES),
            vmem(FLAT, LANES),
            vmem(2, SUBS, LANES),
            vmem(2, SUBS, LANES),
            vmem(GROUP * SLOT, LANES),
            vmem(GROUP * SLOT, LANES),
            vmem(SLOT, LANES),
            vmem(GROUPS * SLOT, LANES),
            vmem(4, SUBS, LANES),
            vmem(GROUP * 4, LANES),
            vmem(GROUP * 4, LANES),
            dma((4,)),
            dma((2,)),
            dma((2,)),
            dma,
            dma,
            dma,
            dma,
            dma,
            dma,
        ],
        compiler_params=pltpu.CompilerParams(
            collective_id=0, has_side_effects=True, vmem_limit_bytes=16 * 1024 * 1024
        ),
        cost_estimate=pl.CostEstimate(
            flops=4_000_000, bytes_accessed=600_000, transcendentals=0
        ),
        name="line_step",
    )(
        *(
            pltpu.with_memory_space_constraint(tiles(array), pltpu.HBM)
            for array in (temperature, transfer, diffusivity, exchange)
        )
    )
    out = out.reshape(2, ROWS // SUBS, SUBS, SUBS, LANES).transpose(0, 1, 3, 2, 4)
    return out.reshape(2, ROWS, SUBS * LANES)


def solution(mesh):
    specs = (P(None, "solve", "cross"),) * 3 + (P("solve", "cross"),)
    return jax.shard_map(
        per_device,
        mesh=mesh,
        in_specs=specs,
        out_specs=P(None, "solve", "cross"),
        check_vma=False,
    )
```

```python
import functools

import jax
import jax.numpy as jnp
from jax import lax
from jax.experimental import pallas as pl
from jax.experimental.pallas import tpu as pltpu
from jax.sharding import PartitionSpec as P

MESH = pl.DeviceIdType.MESH
ROWS, SUBS, LANES = 16, 8, 128
GROUP = 16
HALF = LANES // 2
FLAT = 2 * ROWS * SUBS
NFIELD = 14


def spin(value, shift):
    return pltpu.roll(value, shift % LANES, 1)


def tile(ref, block, column):
    return ref[pl.ds((block * SUBS + column) * SUBS, SUBS), :]


def row(ref, plane, i):
    start = (plane * 2 + i // SUBS) * SUBS * SUBS + i % SUBS
    return ref[pl.ds(start, SUBS, stride=SUBS), :]


def lanes():
    return lax.broadcasted_iota(jnp.int32, (SUBS, LANES), 1)


def inverse(coupling, first, second):
    scale = 1.0 / (coupling * (first + second) + first * second)
    return (coupling + second) * scale, coupling * scale, (coupling + first) * scale


def merge(left, right):
    ea1, ea2, sa, n11, n12, n21, n22, ec1, ec2, sc = left
    fa1, fa2, fs, m11, m12, m21, m22, fc1, fc2, gs = right
    eb1, eb2, sb = ec1 + fa1, ec2 + fa2, sc + fs
    r1 = eb1 + ((n11 + n21) + (m11 + m12))
    r2 = eb2 + ((n12 + n22) + (m21 + m22))
    i11, i12, i22 = inverse(sb, r1, r2)
    g11, g12 = n11 * i11 + n12 * i12, n11 * i12 + n12 * i22
    g21, g22 = n21 * i11 + n22 * i12, n21 * i12 + n22 * i22
    h11, h12 = i11 * m11 + i12 * m21, i11 * m12 + i12 * m22
    h21, h22 = i12 * m11 + i22 * m21, i12 * m12 + i22 * m22
    joined = (
        ea1 + (g11 * eb1 + g12 * eb2),
        ea2 + (g21 * eb1 + g22 * eb2),
        sa + (g11 * n21 + g12 * n22),
        g11 * m11 + g12 * m21,
        g11 * m12 + g12 * m22,
        g21 * m11 + g22 * m21,
        g21 * m12 + g22 * m22,
        fc1 + (h11 * eb1 + h21 * eb2),
        fc2 + (h12 * eb1 + h22 * eb2),
        gs + (m11 * h12 + m21 * h22),
    )
    return joined, (i11, i12, i22, g11, g12, g21, g22, h11, h12, h21, h22)


def merge_leaf(sa, sb, n1, n2, m1, m2):
    r1, r2 = 1.0 + (n1 + m1), 1.0 + (n2 + m2)
    i11, i12, i22 = inverse(sb, r1, r2)
    g11, g12, g21, g22 = n1 * i11, n1 * i12, n2 * i12, n2 * i22
    h11, h12, h21, h22 = i11 * m1, i12 * m2, i12 * m1, i22 * m2
    joined = (
        1.0 + (g11 + g12),
        1.0 + (g21 + g22),
        sa + g12 * n2,
        g11 * m1,
        g12 * m2,
        g21 * m1,
        g22 * m2,
        h11 + h21,
        h12 + h22,
        m1 * h12,
    )
    return joined, (i11, i12, i22, g11, g12, g21, g22, h11, h12, h21, h22)


def merge_loads(back, left, right):
    i11, i12, i22, g11, g12, g21, g22, h11, h12, h21, h22 = back
    a1, a2, b1, b2 = left
    c1, c2, d1, d2 = right
    b1, b2 = b1 + c1, b2 + c2
    loads = (
        a1 + (g11 * b1 + g12 * b2),
        a2 + (g21 * b1 + g22 * b2),
        d1 + (h11 * b1 + h21 * b2),
        d2 + (h12 * b1 + h22 * b2),
    )
    return loads, (i11 * b1 + i12 * b2, i12 * b1 + i22 * b2)


def merge_leaf_loads(back, a, b):
    i11, i12, i22, g11, g12, g21, g22, h11, h12, h21, h22 = back
    a1, a2 = a
    b1, b2 = b
    loads = (
        a1 + (g11 * b1 + g12 * b2),
        a2 + (g21 * b1 + g22 * b2),
        h11 * b1 + h21 * b2,
        h12 * b1 + h22 * b2,
    )
    return loads, (i11 * b1 + i12 * b2, i12 * b1 + i22 * b2)


def middle(back, own, before, after):
    g11, g12, g21, g22, h11, h12, h21, h22 = back[3:]
    a1, a2 = before
    c1, c2 = after
    return (
        own[0] + ((g11 * a1 + g21 * a2) + (h11 * c1 + h12 * c2)),
        own[1] + ((g12 * a1 + g22 * a2) + (h21 * c1 + h22 * c2)),
    )


def eliminate(
    temp_hbm,
    face_hbm,
    diff_hbm,
    sheet_hbm,
    element_ref,
    ways_ref,
    source,
    edge_ref,
    temp,
    face,
    diff,
    sheet,
    in_sem,
):
    loads_in = [
        pltpu.make_async_copy(src, dst, in_sem.at[i])
        for i, (src, dst) in enumerate(
            ((temp_hbm, temp), (diff_hbm, diff), (face_hbm, face), (sheet_hbm, sheet))
        )
    ]
    for copy in loads_in:
        copy.start()

    lane = lanes()
    loads_in[0].wait()
    loads_in[1].wait()
    edges = []
    for column, shift in ((0, 0), (SUBS - 1, 1)):
        packed = jnp.zeros((SUBS, LANES), jnp.float32)
        for j in range(8):
            part = tile(temp if j < 4 else diff, j % 4, column)
            packed = jnp.where(lane == j, spin(part, j + shift), packed)
        edges.append(packed)
    edge_ref[0] = edges[0]
    edge_ref[1] = edges[1]

    zero = jnp.zeros((SUBS, LANES), jnp.float32)
    for block in range(4):
        heat = [tile(temp, block, t) for t in range(SUBS)]
        cond = [tile(diff, block, t) for t in range(SUBS)]
        heat_turned = [spin(v, -1) for v in heat] + [zero]
        cond_turned = [spin(v, -1) for v in cond] + [zero]
        last = lane == LANES - 1
        before = zero
        for t in range(SUBS):
            next_heat = jnp.where(last, heat_turned[t + 1], heat_turned[t])
            next_cond = jnp.where(last, cond_turned[t + 1], cond_turned[t])
            flux = 0.5 * (cond[t] + next_cond) * (next_heat - heat[t])
            if t == SUBS - 1:
                flux = jnp.where(last, 0.0, flux)
            turned = spin(flux, 1)
            previous = jnp.where(lane == 0, before, turned)
            before = turned
            source[pl.ds((block * SUBS + t) * SUBS, SUBS), :] = heat[t] + flux - previous

    loads_in[2].wait()
    loads_in[3].wait()
    backs = []
    level = []
    back = []
    for m in range(ROWS // 2):
        element, way = merge_leaf(
            row(sheet, 0, 2 * m),
            row(sheet, 0, 2 * m + 1),
            row(face, 0, 2 * m),
            row(face, 1, 2 * m),
            row(face, 0, 2 * m + 1),
            row(face, 1, 2 * m + 1),
        )
        level.append(element)
        back.append(way)
    backs.append(back)
    while len(level) > 1:
        pairs = [merge(level[2 * m], level[2 * m + 1]) for m in range(len(level) // 2)]
        level = [pair[0] for pair in pairs]
        backs.append([pair[1] for pair in pairs])
    element = level[0]

    for j in range(10):
        element_ref[j] = element[j]
    for n, way in enumerate(way for back in backs for way in back):
        for j in range(11):
            ways_ref[n * 11 + j] = way[j]


def exchange(
    groups,
    element_ref,
    ways_ref,
    source_ref,
    edge_send,
    out_ref,
    source,
    edge_recv,
    part_send,
    part_recv,
    line_send,
    line_recv,
    pick,
    node_send,
    node_recv,
    edge_ssem,
    edge_rsem,
    part_ssem,
    part_rsem,
    line_ssem,
    line_rsem,
    node_ssem,
    node_rsem,
):
    solve = lax.axis_index("solve")
    cross = lax.axis_index("cross")
    n_cross = lax.axis_size("cross")
    place = lax.rem(solve, GROUP)
    group = lax.div(solve, GROUP)
    base = solve - place

    order = [8, 9, 7, 10, 6, 11, 5, 12, 4, 13, 3, 14, 2, 15, 1]
    mates = [lax.rem(place + step, GROUP) for step in order]
    others = [lax.rem(group + step, groups) for step in range(1, groups)]
    right = lax.rem(cross + 1, n_cross)
    left = lax.rem(cross + n_cross - 1, n_cross)

    barrier = pltpu.get_barrier_semaphore()
    for side in (left, right):
        pl.semaphore_signal(barrier, 1, device_id={"cross": side}, device_id_type=MESH)
    for mate in mates:
        pl.semaphore_signal(barrier, 1, device_id={"solve": base + mate}, device_id_type=MESH)
    for other in others:
        pl.semaphore_signal(
            barrier, 1, device_id={"solve": other * GROUP + place}, device_id_type=MESH
        )

    lane = lanes()
    zero = jnp.zeros((SUBS, LANES), jnp.float32)
    sub = lax.broadcasted_iota(jnp.int32, (SUBS, LANES), 0)
    low = lane < HALF

    pl.semaphore_wait(barrier, 2 + len(mates) + len(others))
    edge_copies = [
        pltpu.make_async_remote_copy(
            src_ref=edge_send.at[i],
            dst_ref=edge_recv.at[i],
            send_sem=edge_ssem.at[i],
            recv_sem=edge_rsem.at[i],
            device_id={"cross": side},
            device_id_type=MESH,
        )
        for i, side in enumerate((left, right))
    ]
    for copy in edge_copies:
        copy.start()

    backs = []
    for start, count in ((0, 8), (8, 4), (12, 2), (14, 1)):
        backs.append(
            [
                tuple(ways_ref[(start + m) * 11 + j] for j in range(11))
                for m in range(count)
            ]
        )
    element = tuple(element_ref[j] for j in range(10))
    edges = (edge_send[0], edge_send[1])
    for block in range(2 * ROWS):
        where = pl.ds(block * SUBS, SUBS)
        source[where, :] = source_ref[where, :]

    for i in (0, 1):
        edge_copies[i].wait_recv()
    for column, own, got, inside in (
        (0, edges[0], edge_recv[1], cross > 0),
        (SUBS - 1, edges[1], edge_recv[0], cross < n_cross - 1),
    ):
        got = jnp.where(inside, got, 0.0)
        flux = 0.5 * spin(own + got, -4) * (got - own)
        at = 0 if column == 0 else LANES - 1
        for j in range(4):
            where = pl.ds((j * SUBS + column) * SUBS, SUBS)
            source[where, :] += jnp.where(lane == at, spin(flux, at - j), 0.0)

    owns = []
    level = []
    own = []
    for m in range(ROWS // 2):
        loads, value = merge_leaf_loads(
            backs[0][m],
            (row(source, 0, 2 * m), row(source, 1, 2 * m)),
            (row(source, 0, 2 * m + 1), row(source, 1, 2 * m + 1)),
        )
        level.append(loads)
        own.append(value)
    owns.append(own)
    for back in backs[1:]:
        pairs = [
            merge_loads(back[m], level[2 * m], level[2 * m + 1]) for m in range(len(back))
        ]
        level = [pair[0] for pair in pairs]
        owns.append([pair[1] for pair in pairs])

    fields = element + level[0]
    for j in range(NFIELD // 2):
        lo, hi = fields[j], fields[j + NFIELD // 2]
        part_send[pl.ds(j, SUBS, stride=2 * SUBS), :] = jnp.where(low, lo, spin(hi, HALF))
        part_send[pl.ds(SUBS + j, SUBS, stride=2 * SUBS), :] = jnp.where(low, spin(lo, HALF), hi)
    for half in (0, SUBS):
        part_send[pl.ds(half + SUBS - 1, SUBS, stride=2 * SUBS), :] = zero

    def slot(ref, index, rows):
        return ref.at[pl.ds(pl.multiple_of(index * rows, rows), rows)]

    part_copies = [
        pltpu.make_async_remote_copy(
            src_ref=slot(part_send, mate, SUBS),
            dst_ref=slot(part_recv, place, SUBS),
            send_sem=part_ssem,
            recv_sem=part_rsem,
            device_id={"solve": base + mate},
            device_id_type=MESH,
        )
        for mate in mates
    ]
    for copy in part_copies:
        copy.start()
    here = pl.ds(pl.multiple_of(place * SUBS, SUBS), SUBS)
    part_recv[here, :] = part_send[here, :]
    everything = part_recv.at[pl.ds(0, (GROUP - 1) * SUBS)]
    pltpu.make_async_copy(everything, everything, part_rsem).wait()

    def unpack(offset):
        rows = [
            part_recv[pl.ds(offset + j, SUBS, stride=2 * SUBS), :] for j in range(NFIELD // 2)
        ]
        return tuple(rows) + tuple(spin(value, HALF) for value in rows)

    def climb(left_fields, right_fields):
        element, way = merge(left_fields[:10], right_fields[:10])
        loads, value = merge_loads(way, left_fields[10:], right_fields[10:])
        return element + loads, way, value

    def lift(value, shift):
        return pltpu.roll(value, SUBS - shift, 0)

    def drop(value, shift):
        return pltpu.roll(value, shift, 0)

    trail = []
    fields, way, value = climb(unpack(0), unpack(SUBS))
    trail.append((way, value, 0))
    for shift in (1, 2, 4):
        fields, way, value = climb(fields, tuple(lift(v, shift) for v in fields))
        trail.append((way, value, shift))

    for j in range(NFIELD):
        line_send[pl.ds(j, 1), :] = fields[j][0:1, :]
    line_send[pl.ds(NFIELD, 2), :] = zero[0:2, :]
    line_copies = [
        pltpu.make_async_remote_copy(
            src_ref=line_send,
            dst_ref=slot(line_recv, group, 2 * SUBS),
            send_sem=line_ssem,
            recv_sem=line_rsem,
            device_id={"solve": other * GROUP + place},
            device_id_type=MESH,
        )
        for other in others
    ]
    for copy in line_copies:
        copy.start()
    line_recv[pl.ds(pl.multiple_of(group * 2 * SUBS, 2 * SUBS), 2 * SUBS), :] = line_send[...]
    everything = line_recv.at[pl.ds(0, (groups - 1) * 2 * SUBS)]
    pltpu.make_async_copy(everything, everything, line_rsem).wait()

    chain = []
    for g in range(groups):
        chain.append(
            tuple(line_recv[pl.ds(g * 2 * SUBS + j, 1), :] for j in range(NFIELD))
        )
    steps = []
    while len(chain) > 1:
        joined = [climb(chain[2 * m], chain[2 * m + 1]) for m in range(len(chain) // 2)]
        steps.append([item[1:] for item in joined])
        chain = [item[0] for item in joined]
    ea1, ea2, sa, n11, n12, n21, n22, _, _, _, f1, f2, _, _ = chain[0]
    i11, i12, i22 = inverse(sa, ea1 + (n11 + n12), ea2 + (n21 + n22))
    nothing = jnp.zeros_like(f1)
    nodes = [(i11 * f1 + i12 * f2, i12 * f1 + i22 * f2), (nothing, nothing)]
    for step in reversed(steps):
        finer = []
        for m, (way, value) in enumerate(step):
            finer += [nodes[m], middle(way, value, nodes[m], nodes[m + 1])]
        nodes = finer + [nodes[-1]]
    for plane in (0, 1):
        for g in range(groups + 1):
            pick[plane, pl.ds(g, 1), :] = nodes[g][plane]
    ends = []
    for step in (0, 1):
        ends.append(
            tuple(
                jnp.broadcast_to(pick[plane, pl.ds(group + step, 1), :], (SUBS, LANES))
                for plane in (0, 1)
            )
        )
    before, after = ends

    for way, value, shift in reversed(trail):
        inner = middle(way, value, before, after)
        if shift == 0:
            break
        first = (sub & shift) == 0
        before = tuple(jnp.where(first, b, drop(v, shift)) for b, v in zip(before, inner))
        after = tuple(jnp.where(first, v, drop(a, shift)) for v, a in zip(inner, after))

    def both(pair):
        return jnp.where(low, pair[0], spin(pair[1], HALF))

    start_row, inner_row, end_row = both(before), both(inner), both(after)
    for j, value in enumerate((start_row, inner_row, inner_row, end_row)):
        node_send[pl.ds(j, SUBS, stride=4), :] = value
    node_copies = [
        pltpu.make_async_remote_copy(
            src_ref=slot(node_send, mate, 2),
            dst_ref=slot(node_recv, place, 2),
            send_sem=node_ssem,
            recv_sem=node_rsem,
            device_id={"solve": base + mate},
            device_id_type=MESH,
        )
        for mate in mates
    ]
    for copy in node_copies:
        copy.start()
    here = pl.ds(pl.multiple_of(place * 2, 2), 2)
    node_recv[here, :] = node_send[here, :]
    everything = node_recv.at[pl.ds(0, (GROUP - 1) * 2)]
    pltpu.make_async_copy(everything, everything, node_rsem).wait()

    ends = []
    for j in (0, 1):
        lower_half = node_recv[pl.ds(j, SUBS, stride=4), :]
        upper_half = node_recv[pl.ds(2 + j, SUBS, stride=4), :]
        ends.append(
            (
                jnp.where(low, lower_half, spin(upper_half, HALF)),
                jnp.where(low, spin(lower_half, HALF), upper_half),
            )
        )

    nodes = ends
    for back, own in zip(reversed(backs), reversed(owns)):
        finer = []
        for m in range(len(back)):
            finer += [nodes[m], middle(back[m], own[m], nodes[m], nodes[m + 1])]
        nodes = finer + [nodes[-1]]
    for i in range(ROWS):
        for plane in (0, 1):
            start = (plane * 2 + i // SUBS) * SUBS * SUBS + i % SUBS
            out_ref[pl.ds(start, SUBS, stride=SUBS), :] = nodes[i][plane]

    for copy in edge_copies:
        copy.wait_send()
    sent = part_send.at[pl.ds(0, (GROUP - 1) * SUBS)]
    pltpu.make_async_copy(sent, sent, part_ssem).wait()
    sent = line_recv.at[pl.ds(0, (groups - 1) * 2 * SUBS)]
    pltpu.make_async_copy(sent, sent, line_ssem).wait()
    sent = node_send.at[pl.ds(0, (GROUP - 1) * 2)]
    pltpu.make_async_copy(sent, sent, node_ssem).wait()


def tiles(array):
    array = array.reshape(-1, ROWS // SUBS, SUBS, SUBS, LANES)
    return array.transpose(0, 1, 3, 2, 4).reshape(-1, LANES)


def per_device(temperature, transfer, diffusivity, exchange_map):
    groups = lax.axis_size("solve") // GROUP
    vmem = lambda *shape: pltpu.VMEM(shape, jnp.float32)
    dma = pltpu.SemaphoreType.DMA
    f32 = lambda *shape: jax.ShapeDtypeStruct(shape, jnp.float32)
    local = pl.pallas_call(
        eliminate,
        out_shape=(
            f32(10, SUBS, LANES),
            f32(165, SUBS, LANES),
            f32(FLAT, LANES),
            f32(2, SUBS, LANES),
        ),
        in_specs=[pl.BlockSpec(memory_space=pltpu.HBM)] * 4,
        out_specs=[pl.BlockSpec(memory_space=pltpu.VMEM)] * 4,
        scratch_shapes=[
            vmem(FLAT, LANES),
            vmem(FLAT, LANES),
            vmem(FLAT, LANES),
            vmem(FLAT // 2, LANES),
            dma((4,)),
        ],
        compiler_params=pltpu.CompilerParams(vmem_limit_bytes=16 * 1024 * 1024),
        name="eliminate",
    )(
        *(
            pltpu.with_memory_space_constraint(tiles(array), pltpu.HBM)
            for array in (temperature, transfer, diffusivity, exchange_map)
        )
    )
    out = pl.pallas_call(
        functools.partial(exchange, groups),
        out_shape=f32(FLAT, LANES),
        in_specs=[pl.BlockSpec(memory_space=pltpu.VMEM)] * 4,
        out_specs=pl.BlockSpec(memory_space=pltpu.VMEM),
        scratch_shapes=[
            vmem(FLAT, LANES),
            vmem(2, SUBS, LANES),
            vmem(GROUP * SUBS, LANES),
            vmem(GROUP * SUBS, LANES),
            vmem(2 * SUBS, LANES),
            vmem(groups * 2 * SUBS, LANES),
            vmem(2, SUBS, LANES),
            vmem(GROUP * 2, LANES),
            vmem(GROUP * 2, LANES),
            dma((2,)),
            dma((2,)),
            dma,
            dma,
            dma,
            dma,
            dma,
            dma,
        ],
        compiler_params=pltpu.CompilerParams(
            collective_id=0, has_side_effects=True, vmem_limit_bytes=16 * 1024 * 1024
        ),
        name="exchange",
    )(*local)
    out = out.reshape(2, ROWS // SUBS, SUBS, SUBS, LANES).transpose(0, 1, 3, 2, 4)
    return out.reshape(2, ROWS, SUBS * LANES)


def solution(mesh):
    specs = (P(None, "solve", "cross"),) * 3 + (P("solve", "cross"),)
    return jax.shard_map(
        per_device,
        mesh=mesh,
        in_specs=specs,
        out_specs=P(None, "solve", "cross"),
        check_vma=False,
    )
```

```python
import functools

import jax
import jax.numpy as jnp
from jax import lax
from jax.experimental import pallas as pl
from jax.experimental.pallas import tpu as pltpu
from jax.sharding import PartitionSpec as P

MESH = pl.DeviceIdType.MESH
ROWS, SUBS, LANES = 16, 8, 128
GROUP = 16
HALF = LANES // 2
LOADS, USED = 2, 7
FLAT = 2 * ROWS * SUBS


def inverse(coupling, first, second):
    scale = 1.0 / (coupling * (first + second) + first * second)
    return (coupling + second) * scale, coupling * scale, (coupling + first) * scale


def merge(left, right):
    ea1, ea2, sa, n11, n12, n21, n22, ec1, ec2, sc = left
    fa1, fa2, fs, m11, m12, m21, m22, fc1, fc2, gs = right
    eb1, eb2, sb = ec1 + fa1, ec2 + fa2, sc + fs
    r1 = eb1 + ((n11 + n21) + (m11 + m12))
    r2 = eb2 + ((n12 + n22) + (m21 + m22))
    i11, i12, i22 = inverse(sb, r1, r2)
    g11, g12 = n11 * i11 + n12 * i12, n11 * i12 + n12 * i22
    g21, g22 = n21 * i11 + n22 * i12, n21 * i12 + n22 * i22
    h11, h12 = i11 * m11 + i12 * m21, i11 * m12 + i12 * m22
    h21, h22 = i12 * m11 + i22 * m21, i12 * m12 + i22 * m22
    joined = (
        ea1 + (g11 * eb1 + g12 * eb2),
        ea2 + (g21 * eb1 + g22 * eb2),
        sa + (g11 * n21 + g12 * n22),
        g11 * m11 + g12 * m21,
        g11 * m12 + g12 * m22,
        g21 * m11 + g22 * m21,
        g21 * m12 + g22 * m22,
        fc1 + (h11 * eb1 + h21 * eb2),
        fc2 + (h12 * eb1 + h22 * eb2),
        gs + (m11 * h12 + m21 * h22),
    )
    return joined, (i11, i12, i22, g11, g12, g21, g22, h11, h12, h21, h22)


def merge_leaf(sa, sb, n1, n2, m1, m2):
    r1, r2 = 1.0 + (n1 + m1), 1.0 + (n2 + m2)
    i11, i12, i22 = inverse(sb, r1, r2)
    g11, g12, g21, g22 = n1 * i11, n1 * i12, n2 * i12, n2 * i22
    h11, h12, h21, h22 = i11 * m1, i12 * m2, i12 * m1, i22 * m2
    joined = (
        1.0 + (g11 + g12),
        1.0 + (g21 + g22),
        sa + g12 * n2,
        g11 * m1,
        g12 * m2,
        g21 * m1,
        g22 * m2,
        h11 + h21,
        h12 + h22,
        m1 * h12,
    )
    return joined, (i11, i12, i22, g11, g12, g21, g22, h11, h12, h21, h22)


def merge_loads(back, left, right):
    i11, i12, i22, g11, g12, g21, g22, h11, h12, h21, h22 = back
    a1, a2, b1, b2 = left
    c1, c2, d1, d2 = right
    b1, b2 = b1 + c1, b2 + c2
    loads = (
        a1 + (g11 * b1 + g12 * b2),
        a2 + (g21 * b1 + g22 * b2),
        d1 + (h11 * b1 + h21 * b2),
        d2 + (h12 * b1 + h22 * b2),
    )
    return loads, (i11 * b1 + i12 * b2, i12 * b1 + i22 * b2)


def merge_leaf_loads(back, a, b):
    i11, i12, i22, g11, g12, g21, g22, h11, h12, h21, h22 = back
    a1, a2 = a
    b1, b2 = b
    loads = (
        a1 + (g11 * b1 + g12 * b2),
        a2 + (g21 * b1 + g22 * b2),
        h11 * b1 + h21 * b2,
        h12 * b1 + h22 * b2,
    )
    return loads, (i11 * b1 + i12 * b2, i12 * b1 + i22 * b2)


def middle(back, own, before, after):
    g11, g12, g21, g22, h11, h12, h21, h22 = back[3:]
    a1, a2 = before
    c1, c2 = after
    return (
        own[0] + ((g11 * a1 + g21 * a2) + (h11 * c1 + h12 * c2)),
        own[1] + ((g12 * a1 + g22 * a2) + (h21 * c1 + h22 * c2)),
    )


def kernel(
    groups,
    temp_hbm,
    face_hbm,
    diff_hbm,
    sheet_hbm,
    out_ref,
    temp,
    face,
    diff,
    sheet,
    source,
    edge_send,
    edge_recv,
    part_send,
    part_recv,
    late_send,
    line_send,
    line_recv,
    pick,
    node_send,
    node_recv,
    in_sem,
    edge_ssem,
    edge_rsem,
    part_ssem,
    part_rsem,
    line_ssem,
    line_rsem,
    node_ssem,
    node_rsem,
):
    solve = lax.axis_index("solve")
    cross = lax.axis_index("cross")
    n_cross = lax.axis_size("cross")
    place = lax.rem(solve, GROUP)
    group = lax.div(solve, GROUP)
    base = solve - place

    loads_in = [
        pltpu.make_async_copy(src, dst, in_sem.at[i])
        for i, (src, dst) in enumerate(
            ((temp_hbm, temp), (diff_hbm, diff), (face_hbm, face), (sheet_hbm, sheet))
        )
    ]
    for copy in loads_in:
        copy.start()

    order = [8, 9, 7, 10, 6, 11, 5, 12, 4, 13, 3, 14, 2, 15, 1]
    mates = [lax.rem(place + step, GROUP) for step in order]
    others = [lax.rem(group + step, groups) for step in range(1, groups)]
    right = lax.rem(cross + 1, n_cross)
    left = lax.rem(cross + n_cross - 1, n_cross)

    barrier = pltpu.get_barrier_semaphore()
    for side in (left, right):
        pl.semaphore_signal(barrier, 1, device_id={"cross": side}, device_id_type=MESH)
    for mate in mates:
        pl.semaphore_signal(barrier, 1, device_id={"solve": base + mate}, device_id_type=MESH)
    for other in others:
        pl.semaphore_signal(
            barrier, 1, device_id={"solve": other * GROUP + place}, device_id_type=MESH
        )

    lane = lax.broadcasted_iota(jnp.int32, (SUBS, LANES), 1)
    sub = lax.broadcasted_iota(jnp.int32, (SUBS, LANES), 0)
    low = lane < HALF

    def spin(value, shift):
        return pltpu.roll(value, shift % LANES, 1)

    def tile(ref, block, column):
        return ref[pl.ds((block * SUBS + column) * SUBS, SUBS), :]

    loads_in[0].wait()
    loads_in[1].wait()
    edges = []
    for column, shift in ((0, 0), (SUBS - 1, 1)):
        packed = jnp.zeros((SUBS, LANES), jnp.float32)
        for j in range(8):
            part = tile(temp if j < 4 else diff, j % 4, column)
            packed = jnp.where(lane == j, spin(part, j + shift), packed)
        edges.append(packed)
    edge_send[0] = edges[0]
    edge_send[1] = edges[1]

    zero = jnp.zeros((SUBS, LANES), jnp.float32)
    for block in range(4):
        heat = [tile(temp, block, t) for t in range(SUBS)]
        cond = [tile(diff, block, t) for t in range(SUBS)]
        heat_turned = [spin(v, -1) for v in heat] + [zero]
        cond_turned = [spin(v, -1) for v in cond] + [zero]
        last = lane == LANES - 1
        before = zero
        for t in range(SUBS):
            next_heat = jnp.where(last, heat_turned[t + 1], heat_turned[t])
            next_cond = jnp.where(last, cond_turned[t + 1], cond_turned[t])
            flux = 0.5 * (cond[t] + next_cond) * (next_heat - heat[t])
            if t == SUBS - 1:
                flux = jnp.where(last, 0.0, flux)
            turned = spin(flux, 1)
            previous = jnp.where(lane == 0, before, turned)
            before = turned
            source[pl.ds((block * SUBS + t) * SUBS, SUBS), :] = heat[t] + flux - previous

    def row(ref, plane, i):
        start = (plane * 2 + i // SUBS) * SUBS * SUBS + i % SUBS
        return ref[pl.ds(start, SUBS, stride=SUBS), :]

    loads_in[2].wait()
    loads_in[3].wait()
    backs = []
    level = []
    back = []
    for m in range(ROWS // 2):
        element, way = merge_leaf(
            row(sheet, 0, 2 * m),
            row(sheet, 0, 2 * m + 1),
            row(face, 0, 2 * m),
            row(face, 1, 2 * m),
            row(face, 0, 2 * m + 1),
            row(face, 1, 2 * m + 1),
        )
        level.append(element)
        back.append(way)
    backs.append(back)
    while len(level) > 1:
        pairs = [merge(level[2 * m], level[2 * m + 1]) for m in range(len(level) // 2)]
        level = [pair[0] for pair in pairs]
        backs.append([pair[1] for pair in pairs])
    element = level[0]

    def climb_loads():
        owns = []
        level = []
        own = []
        for m in range(ROWS // 2):
            loads, value = merge_leaf_loads(
                backs[0][m],
                (row(source, 0, 2 * m), row(source, 1, 2 * m)),
                (row(source, 0, 2 * m + 1), row(source, 1, 2 * m + 1)),
            )
            level.append(loads)
            own.append(value)
        owns.append(own)
        for back in backs[1:]:
            pairs = [
                merge_loads(back[m], level[2 * m], level[2 * m + 1]) for m in range(len(back))
            ]
            level = [pair[0] for pair in pairs]
            owns.append([pair[1] for pair in pairs])
        return level[0], owns

    def halves(lo, hi):
        return jnp.where(low, lo, spin(hi, HALF)), jnp.where(low, spin(lo, HALF), hi)

    def slot(ref, index, rows, used, skip=0):
        return ref.at[pl.ds(pl.multiple_of(index * rows, rows) + skip, used)]

    loads, _ = climb_loads()
    packed = [halves(loads[0], loads[1]), halves(loads[2], loads[3])]
    packed += [halves(element[j], element[j + 5]) for j in range(5)]
    for j, (even, odd) in enumerate(packed):
        part_send[pl.ds(j, SUBS, stride=2 * SUBS), :] = even
        part_send[pl.ds(SUBS + j, SUBS, stride=2 * SUBS), :] = odd

    pl.semaphore_wait(barrier, 2 + len(mates) + len(others))
    edge_copies = [
        pltpu.make_async_remote_copy(
            src_ref=edge_send.at[i],
            dst_ref=edge_recv.at[i],
            send_sem=edge_ssem.at[i],
            recv_sem=edge_rsem.at[i],
            device_id={"cross": side},
            device_id_type=MESH,
        )
        for i, side in enumerate((left, right))
    ]
    for copy in edge_copies:
        copy.start()

    def part_copy(mate, skip, used):
        return pltpu.make_async_remote_copy(
            src_ref=slot(part_send, mate, SUBS, used, skip),
            dst_ref=slot(part_recv, place, SUBS, used, skip),
            send_sem=part_ssem,
            recv_sem=part_rsem,
            device_id={"solve": base + mate},
            device_id_type=MESH,
        )

    for mate in mates:
        outer = (mate == 0) | (mate == GROUP - 1)

        @pl.when(outer)
        def _():
            part_copy(mate, LOADS, USED - LOADS).start()

        @pl.when(jnp.logical_not(outer))
        def _():
            part_copy(mate, 0, USED).start()

    here = pl.ds(pl.multiple_of(place * SUBS, SUBS), USED)
    part_recv[here, :] = part_send[here, :]

    for i in (0, 1):
        edge_copies[i].wait_recv()
    for column, own, got, inside in (
        (0, edges[0], edge_recv[1], cross > 0),
        (SUBS - 1, edges[1], edge_recv[0], cross < n_cross - 1),
    ):
        got = jnp.where(inside, got, 0.0)
        flux = 0.5 * spin(own + got, -4) * (got - own)
        at = 0 if column == 0 else LANES - 1
        for j in range(4):
            where = pl.ds((j * SUBS + column) * SUBS, SUBS)
            source[where, :] += jnp.where(lane == at, spin(flux, at - j), 0.0)

    loads, owns = climb_loads()
    rows = [halves(loads[0], loads[1]), halves(loads[2], loads[3])]
    for j in range(LOADS):
        late_send[pl.ds(j, 1), :] = rows[j][0][0:1, :]
        late_send[pl.ds(LOADS + j, 1), :] = rows[j][1][SUBS - 1 : SUBS, :]
    for i, mate in enumerate((0, GROUP - 1)):
        ready = pl.ds(i * LOADS, LOADS)

        @pl.when(place != mate)
        def _():
            pltpu.make_async_remote_copy(
                src_ref=late_send.at[ready],
                dst_ref=slot(part_recv, place, SUBS, LOADS),
                send_sem=part_ssem,
                recv_sem=part_rsem,
                device_id={"solve": base + mate},
                device_id_type=MESH,
            ).start()

        @pl.when(place == mate)
        def _():
            part_recv[pl.ds(mate * SUBS, LOADS), :] = late_send[ready, :]

    everything = part_recv.at[pl.ds(0, (GROUP - 1) * USED)]
    pltpu.make_async_copy(everything, everything, part_rsem).wait()

    def fields_of(rows):
        turned = [spin(value, HALF) for value in rows]
        return tuple(rows[LOADS:] + turned[LOADS:]) + (rows[0], turned[0], rows[1], turned[1])

    def unpack(offset):
        return fields_of(
            [part_recv[pl.ds(offset + j, SUBS, stride=2 * SUBS), :] for j in range(USED)]
        )

    def climb(left_fields, right_fields):
        element, way = merge(left_fields[:10], right_fields[:10])
        loads, value = merge_loads(way, left_fields[10:], right_fields[10:])
        return element + loads, way, value

    def lift(value, shift):
        return pltpu.roll(value, SUBS - shift, 0)

    def drop(value, shift):
        return pltpu.roll(value, shift, 0)

    def both(pair):
        return jnp.where(low, pair[0], spin(pair[1], HALF))

    trail = []
    fields, way, value = climb(unpack(0), unpack(SUBS))
    trail.append((way, value, 0))
    for shift in (1, 2, 4):
        fields, way, value = climb(fields, tuple(lift(v, shift) for v in fields))
        trail.append((way, value, shift))

    chain_rows = [(fields[10], fields[11]), (fields[12], fields[13])]
    chain_rows += [(fields[j], fields[j + 5]) for j in range(5)]
    for j, pair in enumerate(chain_rows):
        line_send[pl.ds(j, 1), :] = both(pair)[0:1, :]
    line_copies = [
        pltpu.make_async_remote_copy(
            src_ref=line_send.at[pl.ds(0, USED)],
            dst_ref=slot(line_recv, group, SUBS, USED),
            send_sem=line_ssem,
            recv_sem=line_rsem,
            device_id={"solve": other * GROUP + place},
            device_id_type=MESH,
        )
        for other in others
    ]
    for copy in line_copies:
        copy.start()
    here = pl.ds(pl.multiple_of(group * SUBS, SUBS), USED)
    line_recv[here, :] = line_send[pl.ds(0, USED), :]
    everything = line_recv.at[pl.ds(0, (groups - 1) * USED)]
    pltpu.make_async_copy(everything, everything, line_rsem).wait()

    chain = []
    for g in range(groups):
        chain.append(fields_of([line_recv[pl.ds(g * SUBS + j, 1), :] for j in range(USED)]))
    steps = []
    while len(chain) > 1:
        joined = [climb(chain[2 * m], chain[2 * m + 1]) for m in range(len(chain) // 2)]
        steps.append([item[1:] for item in joined])
        chain = [item[0] for item in joined]
    ea1, ea2, sa, n11, n12, n21, n22, _, _, _, f1, f2, _, _ = chain[0]
    i11, i12, i22 = inverse(sa, ea1 + (n11 + n12), ea2 + (n21 + n22))
    nothing = jnp.zeros_like(f1)
    nodes = [(i11 * f1 + i12 * f2, i12 * f1 + i22 * f2), (nothing, nothing)]
    for step in reversed(steps):
        finer = []
        for m, (way, value) in enumerate(step):
            finer += [nodes[m], middle(way, value, nodes[m], nodes[m + 1])]
        nodes = finer + [nodes[-1]]
    for plane in (0, 1):
        for g in range(groups + 1):
            pick[plane, pl.ds(g, 1), :] = nodes[g][plane]
    ends = []
    for step in (0, 1):
        ends.append(
            tuple(
                jnp.broadcast_to(pick[plane, pl.ds(group + step, 1), :], (SUBS, LANES))
                for plane in (0, 1)
            )
        )
    before, after = ends

    for way, value, shift in reversed(trail):
        inner = middle(way, value, before, after)
        if shift == 0:
            break
        first = (sub & shift) == 0
        before = tuple(jnp.where(first, b, drop(v, shift)) for b, v in zip(before, inner))
        after = tuple(jnp.where(first, v, drop(a, shift)) for v, a in zip(inner, after))

    start_row, inner_row, end_row = both(before), both(inner), both(after)
    for j, value in enumerate((start_row, inner_row, inner_row, end_row)):
        node_send[pl.ds(j, SUBS, stride=4), :] = value
    node_copies = [
        pltpu.make_async_remote_copy(
            src_ref=slot(node_send, mate, 2, 2),
            dst_ref=slot(node_recv, place, 2, 2),
            send_sem=node_ssem,
            recv_sem=node_rsem,
            device_id={"solve": base + mate},
            device_id_type=MESH,
        )
        for mate in mates
    ]
    for copy in node_copies:
        copy.start()
    here = pl.ds(pl.multiple_of(place * 2, 2), 2)
    node_recv[here, :] = node_send[here, :]
    everything = node_recv.at[pl.ds(0, (GROUP - 1) * 2)]
    pltpu.make_async_copy(everything, everything, node_rsem).wait()

    ends = []
    for j in (0, 1):
        lower_half = node_recv[pl.ds(j, SUBS, stride=4), :]
        upper_half = node_recv[pl.ds(2 + j, SUBS, stride=4), :]
        ends.append(
            (
                jnp.where(low, lower_half, spin(upper_half, HALF)),
                jnp.where(low, spin(lower_half, HALF), upper_half),
            )
        )

    nodes = ends
    for back, own in zip(reversed(backs), reversed(owns)):
        finer = []
        for m in range(len(back)):
            finer += [nodes[m], middle(back[m], own[m], nodes[m], nodes[m + 1])]
        nodes = finer + [nodes[-1]]
    for i in range(ROWS):
        for plane in (0, 1):
            start = (plane * 2 + i // SUBS) * SUBS * SUBS + i % SUBS
            out_ref[pl.ds(start, SUBS, stride=SUBS), :] = nodes[i][plane]

    for copy in edge_copies:
        copy.wait_send()
    sent = part_send.at[pl.ds(0, (GROUP - 1) * USED)]
    pltpu.make_async_copy(sent, sent, part_ssem).wait()
    sent = line_recv.at[pl.ds(0, (groups - 1) * USED)]
    pltpu.make_async_copy(sent, sent, line_ssem).wait()
    sent = node_send.at[pl.ds(0, (GROUP - 1) * 2)]
    pltpu.make_async_copy(sent, sent, node_ssem).wait()


def tiles(array):
    array = array.reshape(-1, ROWS // SUBS, SUBS, SUBS, LANES)
    return array.transpose(0, 1, 3, 2, 4).reshape(-1, LANES)


def per_device(temperature, transfer, diffusivity, exchange):
    groups = lax.axis_size("solve") // GROUP
    vmem = lambda *shape: pltpu.VMEM(shape, jnp.float32)
    dma = pltpu.SemaphoreType.DMA
    out = pl.pallas_call(
        functools.partial(kernel, groups),
        out_shape=jax.ShapeDtypeStruct((FLAT, LANES), jnp.float32),
        in_specs=[pl.BlockSpec(memory_space=pltpu.HBM)] * 4,
        out_specs=pl.BlockSpec(memory_space=pltpu.VMEM),
        scratch_shapes=[
            vmem(FLAT, LANES),
            vmem(FLAT, LANES),
            vmem(FLAT, LANES),
            vmem(FLAT // 2, LANES),
            vmem(FLAT, LANES),
            vmem(2, SUBS, LANES),
            vmem(2, SUBS, LANES),
            vmem(GROUP * SUBS, LANES),
            vmem(GROUP * SUBS, LANES),
            vmem(SUBS, LANES),
            vmem(SUBS, LANES),
            vmem(groups * SUBS, LANES),
            vmem(2, SUBS, LANES),
            vmem(GROUP * 2, LANES),
            vmem(GROUP * 2, LANES),
            dma((4,)),
            dma((2,)),
            dma((2,)),
            dma,
            dma,
            dma,
            dma,
            dma,
            dma,
        ],
        compiler_params=pltpu.CompilerParams(
            collective_id=0, has_side_effects=True, vmem_limit_bytes=16 * 1024 * 1024
        ),
        cost_estimate=pl.CostEstimate(
            flops=4_000_000, bytes_accessed=600_000, transcendentals=0
        ),
        name="line_step",
    )(
        *(
            pltpu.with_memory_space_constraint(tiles(array), pltpu.HBM)
            for array in (temperature, transfer, diffusivity, exchange)
        )
    )
    out = out.reshape(2, ROWS // SUBS, SUBS, SUBS, LANES).transpose(0, 1, 3, 2, 4)
    return out.reshape(2, ROWS, SUBS * LANES)


def solution(mesh):
    specs = (P(None, "solve", "cross"),) * 3 + (P("solve", "cross"),)
    return jax.shard_map(
        per_device,
        mesh=mesh,
        in_specs=specs,
        out_specs=P(None, "solve", "cross"),
        check_vma=False,
    )
```

```python
import functools

import jax
import jax.numpy as jnp
from jax import lax
from jax.experimental import pallas as pl
from jax.experimental.pallas import tpu as pltpu
from jax.sharding import PartitionSpec as P

MESH = pl.DeviceIdType.MESH
ROWS, SUBS, LANES = 16, 8, 128
GROUP, OWNERS = 16, 8
LOADS, USED, SLOT = 4, 14, 16
FLAT = 2 * ROWS * SUBS


def inverse(coupling, first, second):
    scale = 1.0 / (coupling * (first + second) + first * second)
    return (coupling + second) * scale, coupling * scale, (coupling + first) * scale


def merge(left, right):
    ea1, ea2, sa, n11, n12, n21, n22, ec1, ec2, sc = left
    fa1, fa2, fs, m11, m12, m21, m22, fc1, fc2, gs = right
    eb1, eb2, sb = ec1 + fa1, ec2 + fa2, sc + fs
    r1 = eb1 + ((n11 + n21) + (m11 + m12))
    r2 = eb2 + ((n12 + n22) + (m21 + m22))
    i11, i12, i22 = inverse(sb, r1, r2)
    g11, g12 = n11 * i11 + n12 * i12, n11 * i12 + n12 * i22
    g21, g22 = n21 * i11 + n22 * i12, n21 * i12 + n22 * i22
    h11, h12 = i11 * m11 + i12 * m21, i11 * m12 + i12 * m22
    h21, h22 = i12 * m11 + i22 * m21, i12 * m12 + i22 * m22
    joined = (
        ea1 + (g11 * eb1 + g12 * eb2),
        ea2 + (g21 * eb1 + g22 * eb2),
        sa + (g11 * n21 + g12 * n22),
        g11 * m11 + g12 * m21,
        g11 * m12 + g12 * m22,
        g21 * m11 + g22 * m21,
        g21 * m12 + g22 * m22,
        fc1 + (h11 * eb1 + h21 * eb2),
        fc2 + (h12 * eb1 + h22 * eb2),
        gs + (m11 * h12 + m21 * h22),
    )
    return joined, (i11, i12, i22, g11, g12, g21, g22, h11, h12, h21, h22)


def merge_leaf(sa, sb, n1, n2, m1, m2):
    r1, r2 = 1.0 + (n1 + m1), 1.0 + (n2 + m2)
    i11, i12, i22 = inverse(sb, r1, r2)
    g11, g12, g21, g22 = n1 * i11, n1 * i12, n2 * i12, n2 * i22
    h11, h12, h21, h22 = i11 * m1, i12 * m2, i12 * m1, i22 * m2
    joined = (
        1.0 + (g11 + g12),
        1.0 + (g21 + g22),
        sa + g12 * n2,
        g11 * m1,
        g12 * m2,
        g21 * m1,
        g22 * m2,
        h11 + h21,
        h12 + h22,
        m1 * h12,
    )
    return joined, (i11, i12, i22, g11, g12, g21, g22, h11, h12, h21, h22)


def merge_loads(back, left, right):
    i11, i12, i22, g11, g12, g21, g22, h11, h12, h21, h22 = back
    a1, a2, b1, b2 = left
    c1, c2, d1, d2 = right
    b1, b2 = b1 + c1, b2 + c2
    loads = (
        a1 + (g11 * b1 + g12 * b2),
        a2 + (g21 * b1 + g22 * b2),
        d1 + (h11 * b1 + h21 * b2),
        d2 + (h12 * b1 + h22 * b2),
    )
    return loads, (i11 * b1 + i12 * b2, i12 * b1 + i22 * b2)


def merge_leaf_loads(back, a, b):
    i11, i12, i22, g11, g12, g21, g22, h11, h12, h21, h22 = back
    a1, a2 = a
    b1, b2 = b
    loads = (
        a1 + (g11 * b1 + g12 * b2),
        a2 + (g21 * b1 + g22 * b2),
        h11 * b1 + h21 * b2,
        h12 * b1 + h22 * b2,
    )
    return loads, (i11 * b1 + i12 * b2, i12 * b1 + i22 * b2)


def middle(back, own, before, after):
    g11, g12, g21, g22, h11, h12, h21, h22 = back[3:]
    a1, a2 = before
    c1, c2 = after
    return (
        own[0] + ((g11 * a1 + g21 * a2) + (h11 * c1 + h12 * c2)),
        own[1] + ((g12 * a1 + g22 * a2) + (h21 * c1 + h22 * c2)),
    )


def kernel(
    groups,
    temp_hbm,
    face_hbm,
    diff_hbm,
    sheet_hbm,
    out_ref,
    temp,
    face,
    diff,
    sheet,
    source,
    edge_send,
    edge_recv,
    part_send,
    part_recv,
    late_send,
    line_send,
    line_recv,
    pick,
    node_send,
    node_recv,
    in_sem,
    edge_ssem,
    edge_rsem,
    part_ssem,
    part_rsem,
    line_ssem,
    line_rsem,
    node_ssem,
    node_rsem,
):
    solve = lax.axis_index("solve")
    cross = lax.axis_index("cross")
    n_cross = lax.axis_size("cross")
    place = lax.rem(solve, GROUP)
    group = lax.div(solve, GROUP)
    base = solve - place

    loads_in = [
        pltpu.make_async_copy(src, dst, in_sem.at[i])
        for i, (src, dst) in enumerate(
            ((temp_hbm, temp), (diff_hbm, diff), (face_hbm, face), (sheet_hbm, sheet))
        )
    ]
    for copy in loads_in:
        copy.start()

    owner = place < OWNERS
    owners = [lax.rem(place + step, OWNERS) for step in (4, 5, 3, 6, 2, 7, 1, 0)]
    order = [8, 9, 7, 10, 6, 11, 5, 12, 4, 13, 3, 14, 2, 15, 1]
    mates = [lax.rem(place + step, GROUP) for step in order]
    others = [lax.rem(group + step, groups) for step in range(1, groups)]
    right = lax.rem(cross + 1, n_cross)
    left = lax.rem(cross + n_cross - 1, n_cross)

    barrier = pltpu.get_barrier_semaphore()
    for side in (left, right):
        pl.semaphore_signal(barrier, 1, device_id={"cross": side}, device_id_type=MESH)

    @pl.when(owner)
    def _():
        for mate in mates:
            pl.semaphore_signal(
                barrier, 1, device_id={"solve": base + mate}, device_id_type=MESH
            )
        for other in others:
            pl.semaphore_signal(
                barrier, 1, device_id={"solve": other * GROUP + place}, device_id_type=MESH
            )

    lane = lax.broadcasted_iota(jnp.int32, (SUBS, LANES), 1)
    sub = lax.broadcasted_iota(jnp.int32, (SUBS, LANES), 0)

    def spin(value, shift):
        return pltpu.roll(value, shift % LANES, 1)

    def tile(ref, block, column):
        return ref[pl.ds((block * SUBS + column) * SUBS, SUBS), :]

    loads_in[0].wait()
    loads_in[1].wait()
    edges = []
    for column, shift in ((0, 0), (SUBS - 1, 1)):
        packed = jnp.zeros((SUBS, LANES), jnp.float32)
        for j in range(8):
            part = tile(temp if j < 4 else diff, j % 4, column)
            packed = jnp.where(lane == j, spin(part, j + shift), packed)
        edges.append(packed)
    edge_send[0] = edges[0]
    edge_send[1] = edges[1]

    zero = jnp.zeros((SUBS, LANES), jnp.float32)
    for block in range(4):
        heat = [tile(temp, block, t) for t in range(SUBS)]
        cond = [tile(diff, block, t) for t in range(SUBS)]
        heat_turned = [spin(v, -1) for v in heat] + [zero]
        cond_turned = [spin(v, -1) for v in cond] + [zero]
        last = lane == LANES - 1
        before = zero
        for t in range(SUBS):
            next_heat = jnp.where(last, heat_turned[t + 1], heat_turned[t])
            next_cond = jnp.where(last, cond_turned[t + 1], cond_turned[t])
            flux = 0.5 * (cond[t] + next_cond) * (next_heat - heat[t])
            if t == SUBS - 1:
                flux = jnp.where(last, 0.0, flux)
            turned = spin(flux, 1)
            previous = jnp.where(lane == 0, before, turned)
            before = turned
            source[pl.ds((block * SUBS + t) * SUBS, SUBS), :] = heat[t] + flux - previous

    def row(ref, plane, i):
        start = (plane * 2 + i // SUBS) * SUBS * SUBS + i % SUBS
        return ref[pl.ds(start, SUBS, stride=SUBS), :]

    loads_in[2].wait()
    loads_in[3].wait()
    backs = []
    level = []
    back = []
    for m in range(ROWS // 2):
        element, way = merge_leaf(
            row(sheet, 0, 2 * m),
            row(sheet, 0, 2 * m + 1),
            row(face, 0, 2 * m),
            row(face, 1, 2 * m),
            row(face, 0, 2 * m + 1),
            row(face, 1, 2 * m + 1),
        )
        level.append(element)
        back.append(way)
    backs.append(back)
    while len(level) > 1:
        pairs = [merge(level[2 * m], level[2 * m + 1]) for m in range(len(level) // 2)]
        level = [pair[0] for pair in pairs]
        backs.append([pair[1] for pair in pairs])
    element = level[0]

    def climb_loads():
        owns = []
        level = []
        own = []
        for m in range(ROWS // 2):
            loads, value = merge_leaf_loads(
                backs[0][m],
                (row(source, 0, 2 * m), row(source, 1, 2 * m)),
                (row(source, 0, 2 * m + 1), row(source, 1, 2 * m + 1)),
            )
            level.append(loads)
            own.append(value)
        owns.append(own)
        for back in backs[1:]:
            pairs = [
                merge_loads(back[m], level[2 * m], level[2 * m + 1]) for m in range(len(back))
            ]
            level = [pair[0] for pair in pairs]
            owns.append([pair[1] for pair in pairs])
        return level[0], owns

    def slot(ref, index, rows, used, skip=0):
        return ref.at[pl.ds(pl.multiple_of(index * rows, rows) + skip, used)]

    loads, _ = climb_loads()
    for j, value in enumerate(loads + element):
        part_send[pl.ds(j, SUBS, stride=SLOT), :] = value

    @pl.when(owner)
    def _():
        pl.semaphore_wait(barrier, 2 + OWNERS - 1 + len(others))

    @pl.when(jnp.logical_not(owner))
    def _():
        pl.semaphore_wait(barrier, 2 + OWNERS)

    edge_copies = [
        pltpu.make_async_remote_copy(
            src_ref=edge_send.at[i],
            dst_ref=edge_recv.at[i],
            send_sem=edge_ssem.at[i],
            recv_sem=edge_rsem.at[i],
            device_id={"cross": side},
            device_id_type=MESH,
        )
        for i, side in enumerate((left, right))
    ]
    for copy in edge_copies:
        copy.start()

    def part_copy(mate, skip, used):
        return pltpu.make_async_remote_copy(
            src_ref=slot(part_send, mate, SLOT, used, skip),
            dst_ref=slot(part_recv, place, SLOT, used, skip),
            send_sem=part_ssem,
            recv_sem=part_rsem,
            device_id={"solve": base + mate},
            device_id_type=MESH,
        )

    for mate in owners:
        outer = (mate == 0) | (mate == OWNERS - 1)

        @pl.when(outer & (mate != place))
        def _():
            part_copy(mate, LOADS, USED - LOADS).start()

        @pl.when(jnp.logical_not(outer) & (mate != place))
        def _():
            part_copy(mate, 0, USED).start()

    @pl.when(owner)
    def _():
        here = pl.ds(pl.multiple_of(place * SLOT, SLOT), USED)
        part_recv[here, :] = part_send[here, :]

    for i in (0, 1):
        edge_copies[i].wait_recv()
    for column, own, got, inside in (
        (0, edges[0], edge_recv[1], cross > 0),
        (SUBS - 1, edges[1], edge_recv[0], cross < n_cross - 1),
    ):
        got = jnp.where(inside, got, 0.0)
        flux = 0.5 * spin(own + got, -4) * (got - own)
        at = 0 if column == 0 else LANES - 1
        for j in range(4):
            where = pl.ds((j * SUBS + column) * SUBS, SUBS)
            source[where, :] += jnp.where(lane == at, spin(flux, at - j), 0.0)

    loads, owns = climb_loads()
    for j in range(LOADS):
        late_send[pl.ds(j, 1), :] = loads[j][0:1, :]
        late_send[pl.ds(LOADS + j, 1), :] = loads[j][SUBS - 1 : SUBS, :]
    for i, mate in enumerate((0, OWNERS - 1)):
        ready = pl.ds(i * LOADS, LOADS)

        @pl.when(place != mate)
        def _():
            pltpu.make_async_remote_copy(
                src_ref=late_send.at[ready],
                dst_ref=slot(part_recv, place, SLOT, LOADS),
                send_sem=part_ssem,
                recv_sem=part_rsem,
                device_id={"solve": base + mate},
                device_id_type=MESH,
            ).start()

        @pl.when(place == mate)
        def _():
            part_recv[pl.ds(mate * SLOT, LOADS), :] = late_send[ready, :]

    def climb(left_fields, right_fields):
        element, way = merge(left_fields[LOADS:], right_fields[LOADS:])
        loads, value = merge_loads(way, left_fields[:LOADS], right_fields[:LOADS])
        return loads + element, way, value

    @pl.when(owner)
    def _():
        everything = part_recv.at[pl.ds(0, (GROUP - 1) * USED)]
        pltpu.make_async_copy(everything, everything, part_rsem).wait()

        evens, odds = (
            tuple(part_recv[pl.ds(at + j, SUBS, stride=2 * SLOT), :] for j in range(USED))
            for at in (0, SLOT)
        )
        fields, way, value = climb(evens, odds)
        trail = [(way, value, 0)]
        for shift in (1, 2, 4):
            raised = tuple(pltpu.roll(v, SUBS - shift, 0) for v in fields)
            fields, way, value = climb(fields, raised)
            trail.append((way, value, shift))

        for j in range(USED):
            line_send[pl.ds(j, 1), :] = fields[j][0:1, :]
        line_copies = [
            pltpu.make_async_remote_copy(
                src_ref=line_send.at[pl.ds(0, USED)],
                dst_ref=slot(line_recv, group, SLOT, USED),
                send_sem=line_ssem,
                recv_sem=line_rsem,
                device_id={"solve": other * GROUP + place},
                device_id_type=MESH,
            )
            for other in others
        ]
        for copy in line_copies:
            copy.start()
        here = pl.ds(pl.multiple_of(group * SLOT, SLOT), USED)
        line_recv[here, :] = line_send[pl.ds(0, USED), :]
        everything = line_recv.at[pl.ds(0, (groups - 1) * USED)]
        pltpu.make_async_copy(everything, everything, line_rsem).wait()

        chain = []
        for g in range(groups):
            chain.append(tuple(line_recv[pl.ds(g * SLOT + j, 1), :] for j in range(USED)))
        steps = []
        while len(chain) > 1:
            joined = [climb(chain[2 * m], chain[2 * m + 1]) for m in range(len(chain) // 2)]
            steps.append([item[1:] for item in joined])
            chain = [item[0] for item in joined]
        f1, f2, _, _, ea1, ea2, sa, n11, n12, n21, n22, _, _, _ = chain[0]
        i11, i12, i22 = inverse(sa, ea1 + (n11 + n12), ea2 + (n21 + n22))
        nothing = jnp.zeros_like(f1)
        nodes = [(i11 * f1 + i12 * f2, i12 * f1 + i22 * f2), (nothing, nothing)]
        for step in reversed(steps):
            finer = []
            for m, (way, value) in enumerate(step):
                finer += [nodes[m], middle(way, value, nodes[m], nodes[m + 1])]
            nodes = finer + [nodes[-1]]
        for plane in (0, 1):
            for g in range(groups + 1):
                pick[plane, pl.ds(g, 1), :] = nodes[g][plane]
        before, after = (
            tuple(
                jnp.broadcast_to(pick[plane, pl.ds(group + step, 1), :], (SUBS, LANES))
                for plane in (0, 1)
            )
            for step in (0, 1)
        )

        for way, value, shift in reversed(trail):
            inner = middle(way, value, before, after)
            if shift == 0:
                break
            first = (sub & shift) == 0
            before = tuple(
                jnp.where(first, b, pltpu.roll(v, shift, 0)) for b, v in zip(before, inner)
            )
            after = tuple(
                jnp.where(first, v, pltpu.roll(a, shift, 0)) for v, a in zip(inner, after)
            )
        for j, value in enumerate(before + inner + inner + after):
            node_send[pl.ds(j, SUBS, stride=2 * LOADS), :] = value
        node_copies = [
            pltpu.make_async_remote_copy(
                src_ref=slot(node_send, mate, LOADS, LOADS),
                dst_ref=slot(node_recv, place, LOADS, LOADS),
                send_sem=node_ssem,
                recv_sem=node_rsem,
                device_id={"solve": base + mate},
                device_id_type=MESH,
            )
            for mate in mates
        ]
        for copy in node_copies:
            copy.start()
        here = pl.ds(pl.multiple_of(place * LOADS, LOADS), LOADS)
        node_recv[here, :] = node_send[here, :]

    def wait_for(ref, rows, sem):
        part = ref.at[pl.ds(0, rows)]
        pltpu.make_async_copy(part, part, sem).wait()

    @pl.when(owner)
    def _():
        wait_for(node_recv, (OWNERS - 1) * LOADS, node_rsem)

    @pl.when(jnp.logical_not(owner))
    def _():
        wait_for(node_recv, OWNERS * LOADS, node_rsem)

    values = [node_recv[pl.ds(j, SUBS, stride=LOADS), :] for j in range(LOADS)]
    ends = [tuple(values[:2]), tuple(values[2:])]

    nodes = ends
    for back, own in zip(reversed(backs), reversed(owns)):
        finer = []
        for m in range(len(back)):
            finer += [nodes[m], middle(back[m], own[m], nodes[m], nodes[m + 1])]
        nodes = finer + [nodes[-1]]
    for i in range(ROWS):
        for plane in (0, 1):
            start = (plane * 2 + i // SUBS) * SUBS * SUBS + i % SUBS
            out_ref[pl.ds(start, SUBS, stride=SUBS), :] = nodes[i][plane]

    for copy in edge_copies:
        copy.wait_send()
    @pl.when(owner)
    def _():
        wait_for(part_send, (OWNERS - 1) * USED, part_ssem)
        wait_for(line_recv, (groups - 1) * USED, line_ssem)
        wait_for(node_send, (GROUP - 1) * LOADS, node_ssem)

    @pl.when(jnp.logical_not(owner))
    def _():
        wait_for(part_send, OWNERS * USED, part_ssem)


def tiles(array):
    array = array.reshape(-1, ROWS // SUBS, SUBS, SUBS, LANES)
    return array.transpose(0, 1, 3, 2, 4).reshape(-1, LANES)


def per_device(temperature, transfer, diffusivity, exchange):
    groups = lax.axis_size("solve") // GROUP
    vmem = lambda *shape: pltpu.VMEM(shape, jnp.float32)
    dma = pltpu.SemaphoreType.DMA
    out = pl.pallas_call(
        functools.partial(kernel, groups),
        out_shape=jax.ShapeDtypeStruct((FLAT, LANES), jnp.float32),
        in_specs=[pl.BlockSpec(memory_space=pltpu.HBM)] * 4,
        out_specs=pl.BlockSpec(memory_space=pltpu.VMEM),
        scratch_shapes=[
            vmem(FLAT, LANES),
            vmem(FLAT, LANES),
            vmem(FLAT, LANES),
            vmem(FLAT // 2, LANES),
            vmem(FLAT, LANES),
            vmem(2, SUBS, LANES),
            vmem(2, SUBS, LANES),
            vmem(OWNERS * SLOT, LANES),
            vmem(GROUP * SLOT, LANES),
            vmem(2 * LOADS, LANES),
            vmem(SLOT, LANES),
            vmem(groups * SLOT, LANES),
            vmem(2, SUBS, LANES),
            vmem(GROUP * LOADS, LANES),
            vmem(OWNERS * LOADS, LANES),
            dma((4,)),
            dma((2,)),
            dma((2,)),
            dma,
            dma,
            dma,
            dma,
            dma,
            dma,
        ],
        compiler_params=pltpu.CompilerParams(
            collective_id=0, has_side_effects=True, vmem_limit_bytes=16 * 1024 * 1024
        ),
        cost_estimate=pl.CostEstimate(
            flops=4_000_000, bytes_accessed=600_000, transcendentals=0
        ),
        name="line_step",
    )(
        *(
            pltpu.with_memory_space_constraint(tiles(array), pltpu.HBM)
            for array in (temperature, transfer, diffusivity, exchange)
        )
    )
    out = out.reshape(2, ROWS // SUBS, SUBS, SUBS, LANES).transpose(0, 1, 3, 2, 4)
    return out.reshape(2, ROWS, SUBS * LANES)


def solution(mesh):
    specs = (P(None, "solve", "cross"),) * 3 + (P("solve", "cross"),)
    return jax.shard_map(
        per_device,
        mesh=mesh,
        in_specs=specs,
        out_specs=P(None, "solve", "cross"),
        check_vma=False,
    )
```

```python
import functools

import jax
import jax.numpy as jnp
from jax import lax
from jax.experimental import pallas as pl
from jax.experimental.pallas import tpu as pltpu
from jax.sharding import PartitionSpec as P

MESH = pl.DeviceIdType.MESH
ROWS, SUBS, LANES = 16, 8, 128
GROUP, OWNERS = 16, 8
LOADS, USED, SLOT = 4, 14, 16
FLAT = 2 * ROWS * SUBS


def inverse(coupling, first, second):
    scale = 1.0 / (coupling * (first + second) + first * second)
    return (coupling + second) * scale, coupling * scale, (coupling + first) * scale


def merge(left, right):
    ea1, ea2, sa, n11, n12, n21, n22, ec1, ec2, sc = left
    fa1, fa2, fs, m11, m12, m21, m22, fc1, fc2, gs = right
    eb1, eb2, sb = ec1 + fa1, ec2 + fa2, sc + fs
    r1 = eb1 + ((n11 + n21) + (m11 + m12))
    r2 = eb2 + ((n12 + n22) + (m21 + m22))
    i11, i12, i22 = inverse(sb, r1, r2)
    g11, g12 = n11 * i11 + n12 * i12, n11 * i12 + n12 * i22
    g21, g22 = n21 * i11 + n22 * i12, n21 * i12 + n22 * i22
    h11, h12 = i11 * m11 + i12 * m21, i11 * m12 + i12 * m22
    h21, h22 = i12 * m11 + i22 * m21, i12 * m12 + i22 * m22
    joined = (
        ea1 + (g11 * eb1 + g12 * eb2),
        ea2 + (g21 * eb1 + g22 * eb2),
        sa + (g11 * n21 + g12 * n22),
        g11 * m11 + g12 * m21,
        g11 * m12 + g12 * m22,
        g21 * m11 + g22 * m21,
        g21 * m12 + g22 * m22,
        fc1 + (h11 * eb1 + h21 * eb2),
        fc2 + (h12 * eb1 + h22 * eb2),
        gs + (m11 * h12 + m21 * h22),
    )
    return joined, (i11, i12, i22, g11, g12, g21, g22, h11, h12, h21, h22)


def merge_leaf(sa, sb, n1, n2, m1, m2):
    r1, r2 = 1.0 + (n1 + m1), 1.0 + (n2 + m2)
    i11, i12, i22 = inverse(sb, r1, r2)
    g11, g12, g21, g22 = n1 * i11, n1 * i12, n2 * i12, n2 * i22
    h11, h12, h21, h22 = i11 * m1, i12 * m2, i12 * m1, i22 * m2
    joined = (
        1.0 + (g11 + g12),
        1.0 + (g21 + g22),
        sa + g12 * n2,
        g11 * m1,
        g12 * m2,
        g21 * m1,
        g22 * m2,
        h11 + h21,
        h12 + h22,
        m1 * h12,
    )
    return joined, (i11, i12, i22, g11, g12, g21, g22, h11, h12, h21, h22)


def merge_loads(back, left, right):
    i11, i12, i22, g11, g12, g21, g22, h11, h12, h21, h22 = back
    a1, a2, b1, b2 = left
    c1, c2, d1, d2 = right
    b1, b2 = b1 + c1, b2 + c2
    loads = (
        a1 + (g11 * b1 + g12 * b2),
        a2 + (g21 * b1 + g22 * b2),
        d1 + (h11 * b1 + h21 * b2),
        d2 + (h12 * b1 + h22 * b2),
    )
    return loads, (i11 * b1 + i12 * b2, i12 * b1 + i22 * b2)


def merge_leaf_loads(back, a, b):
    i11, i12, i22, g11, g12, g21, g22, h11, h12, h21, h22 = back
    a1, a2 = a
    b1, b2 = b
    loads = (
        a1 + (g11 * b1 + g12 * b2),
        a2 + (g21 * b1 + g22 * b2),
        h11 * b1 + h21 * b2,
        h12 * b1 + h22 * b2,
    )
    return loads, (i11 * b1 + i12 * b2, i12 * b1 + i22 * b2)


def middle(back, own, before, after):
    g11, g12, g21, g22, h11, h12, h21, h22 = back[3:]
    a1, a2 = before
    c1, c2 = after
    return (
        own[0] + ((g11 * a1 + g21 * a2) + (h11 * c1 + h12 * c2)),
        own[1] + ((g12 * a1 + g22 * a2) + (h21 * c1 + h22 * c2)),
    )


def kernel(
    groups,
    temp_hbm,
    face_hbm,
    diff_hbm,
    sheet_hbm,
    out_ref,
    temp,
    face,
    diff,
    sheet,
    source,
    edge_send,
    edge_own,
    edge_far,
    flux_send,
    flux_recv,
    flipped,
    part_send,
    part_recv,
    line_send,
    line_recv,
    pick,
    node_send,
    node_recv,
    in_sem,
    edge_ssem,
    own_rsem,
    far_rsem,
    flux_ssem,
    flux_rsem,
    part_ssem,
    part_rsem,
    line_ssem,
    line_rsem,
    node_ssem,
    node_rsem,
):
    solve = lax.axis_index("solve")
    cross = lax.axis_index("cross")
    n_cross = lax.axis_size("cross")
    place = lax.rem(solve, GROUP)
    group = lax.div(solve, GROUP)
    base = solve - place

    loads_in = [
        pltpu.make_async_copy(src, dst, in_sem.at[i])
        for i, (src, dst) in enumerate(
            ((temp_hbm, temp), (diff_hbm, diff), (face_hbm, face), (sheet_hbm, sheet))
        )
    ]
    for copy in loads_in:
        copy.start()

    owner = place < OWNERS
    outer = (place == 0) | (place == OWNERS - 1)
    owners = [lax.rem(place + step, OWNERS) for step in (4, 5, 3, 6, 2, 7, 1, 0)]
    order = [8, 9, 7, 10, 6, 11, 5, 12, 4, 13, 3, 14, 2, 15, 1]
    mates = [lax.rem(place + step, GROUP) for step in order]
    others = [lax.rem(group + step, groups) for step in range(1, groups)]
    right = lax.rem(cross + 1, n_cross)
    left = lax.rem(cross + n_cross - 1, n_cross)

    barrier = pltpu.get_barrier_semaphore()
    for column, side in ((0, left), (OWNERS - 1, right)):

        @pl.when(place == column)
        def _():
            for mate in range(GROUP):
                pl.semaphore_signal(
                    barrier,
                    1,
                    device_id={"solve": base + mate, "cross": side},
                    device_id_type=MESH,
                )

    @pl.when(owner)
    def _():
        for mate in mates:
            pl.semaphore_signal(
                barrier, 1, device_id={"solve": base + mate}, device_id_type=MESH
            )
        for other in others:
            pl.semaphore_signal(
                barrier, 1, device_id={"solve": other * GROUP + place}, device_id_type=MESH
            )

    lane = lax.broadcasted_iota(jnp.int32, (SUBS, LANES), 1)
    sub = lax.broadcasted_iota(jnp.int32, (SUBS, LANES), 0)

    def spin(value, shift):
        return pltpu.roll(value, shift % LANES, 1)

    def tile(ref, block, column):
        return ref[pl.ds((block * SUBS + column) * SUBS, SUBS), :]

    def slot(ref, index, rows, used, skip=0):
        return ref.at[pl.ds(pl.multiple_of(index * rows, rows) + skip, used)]

    for copy in loads_in:
        copy.wait()
    tracks = [(ref, j) for ref in (temp, diff, face) for j in range(4)]
    tracks += [(sheet, 0), (sheet, 1)]
    for i, (column, shift) in enumerate(((0, 0), (SUBS - 1, 1))):
        packed = jnp.zeros((SUBS, LANES), jnp.float32)
        for j, (ref, block) in enumerate(tracks):
            packed = jnp.where(lane == j, spin(tile(ref, block, column), j + shift), packed)
        edge_send[pl.ds(i * SUBS, SUBS), :] = packed

    @pl.when(owner)
    def _():
        pl.semaphore_wait(barrier, 2 + OWNERS - 1 + len(others))

    @pl.when(jnp.logical_not(owner))
    def _():
        pl.semaphore_wait(barrier, 2 + OWNERS)

    for i, (mine, theirs, side) in enumerate(
        ((0, OWNERS - 1, left), (OWNERS - 1, 0, right))
    ):
        edge = edge_send.at[pl.ds(i * SUBS, SUBS)]
        pltpu.make_async_remote_copy(
            src_ref=edge,
            dst_ref=slot(edge_far, place, SUBS, SUBS),
            send_sem=edge_ssem,
            recv_sem=far_rsem,
            device_id={"solve": base + theirs, "cross": side},
            device_id_type=MESH,
        ).start()

        @pl.when(place != mine)
        def _():
            pltpu.make_async_remote_copy(
                src_ref=edge,
                dst_ref=slot(edge_own, place, SUBS, SUBS),
                send_sem=edge_ssem,
                recv_sem=own_rsem,
                device_id={"solve": base + mine},
                device_id_type=MESH,
            ).start()

        @pl.when(place == mine)
        def _():
            edge_own[pl.ds(mine * SUBS, SUBS), :] = edge_send[pl.ds(i * SUBS, SUBS), :]

    zero = jnp.zeros((SUBS, LANES), jnp.float32)
    for block in range(4):
        heat = [tile(temp, block, t) for t in range(SUBS)]
        cond = [tile(diff, block, t) for t in range(SUBS)]
        heat_turned = [spin(v, -1) for v in heat] + [zero]
        cond_turned = [spin(v, -1) for v in cond] + [zero]
        last = lane == LANES - 1
        before = zero
        for t in range(SUBS):
            next_heat = jnp.where(last, heat_turned[t + 1], heat_turned[t])
            next_cond = jnp.where(last, cond_turned[t + 1], cond_turned[t])
            flux = 0.5 * (cond[t] + next_cond) * (next_heat - heat[t])
            if t == SUBS - 1:
                flux = jnp.where(last, 0.0, flux)
            turned = spin(flux, 1)
            previous = jnp.where(lane == 0, before, turned)
            before = turned
            source[pl.ds((block * SUBS + t) * SUBS, SUBS), :] = heat[t] + flux - previous

    def row(ref, plane, i):
        start = (plane * 2 + i // SUBS) * SUBS * SUBS + i % SUBS
        return ref[pl.ds(start, SUBS, stride=SUBS), :]

    backs = []
    level = []
    back = []
    for m in range(ROWS // 2):
        element, way = merge_leaf(
            row(sheet, 0, 2 * m),
            row(sheet, 0, 2 * m + 1),
            row(face, 0, 2 * m),
            row(face, 1, 2 * m),
            row(face, 0, 2 * m + 1),
            row(face, 1, 2 * m + 1),
        )
        level.append(element)
        back.append(way)
    backs.append(back)
    while len(level) > 1:
        pairs = [merge(level[2 * m], level[2 * m + 1]) for m in range(len(level) // 2)]
        level = [pair[0] for pair in pairs]
        backs.append([pair[1] for pair in pairs])
    element = level[0]

    def climb_loads():
        owns = []
        level = []
        own = []
        for m in range(ROWS // 2):
            loads, value = merge_leaf_loads(
                backs[0][m],
                (row(source, 0, 2 * m), row(source, 1, 2 * m)),
                (row(source, 0, 2 * m + 1), row(source, 1, 2 * m + 1)),
            )
            level.append(loads)
            own.append(value)
        owns.append(own)
        for back in backs[1:]:
            pairs = [
                merge_loads(back[m], level[2 * m], level[2 * m + 1]) for m in range(len(back))
            ]
            level = [pair[0] for pair in pairs]
            owns.append([pair[1] for pair in pairs])
        return level[0], owns

    loads, _ = climb_loads()
    for j, value in enumerate(loads + element):
        part_send[pl.ds(j, SUBS, stride=SLOT), :] = value

    for mate in owners:

        @pl.when(mate != place)
        def _():
            pltpu.make_async_remote_copy(
                src_ref=slot(part_send, mate, SLOT, USED),
                dst_ref=slot(part_recv, place, SLOT, USED),
                send_sem=part_ssem,
                recv_sem=part_rsem,
                device_id={"solve": base + mate},
                device_id_type=MESH,
            ).start()

    @pl.when(owner)
    def _():
        here = pl.ds(pl.multiple_of(place * SLOT, SLOT), USED)
        part_recv[here, :] = part_send[here, :]

    def climb(left_fields, right_fields):
        element, way = merge(left_fields[LOADS:], right_fields[LOADS:])
        loads, value = merge_loads(way, left_fields[:LOADS], right_fields[:LOADS])
        return loads + element, way, value

    def wait_for(ref, rows, sem):
        part = ref.at[pl.ds(0, rows)]
        pltpu.make_async_copy(part, part, sem).wait()

    @pl.when(outer)
    def _():
        wait_for(edge_own, (GROUP - 1) * SUBS, own_rsem)
        wait_for(edge_far, GROUP * SUBS, far_rsem)
        inside = jnp.where(place == 0, cross > 0, cross < n_cross - 1)
        for mate in range(GROUP):
            where = pl.ds(mate * SUBS, SUBS)
            own = edge_own[where, :]
            far = jnp.where(inside, edge_far[where, :], 0.0)
            flux_send[where, :] = 0.5 * spin(own + far, -4) * (far - own)
        flipped[pl.ds(0, 32), :] = edge_own[...].T[:32]
        flipped[pl.ds(32, 32), :] = flux_send[...].T[:32]
        side1, side2, first1, first2, second = (
            flipped[pl.ds(at, SUBS), :] for at in (32, 34, 8, 10, 12)
        )
        element, way = merge_leaf(
            second, spin(second, -1), first1, first2, spin(first1, -1), spin(first2, -1)
        )
        loads, _ = merge_leaf_loads(way, (side1, side2), (spin(side1, -1), spin(side2, -1)))
        fields = loads + element
        for shift in (2, 4):
            fields, _, _ = climb(fields, tuple(spin(v, -shift) for v in fields))
        fields, _, _ = climb(fields, tuple(pltpu.roll(v, SUBS - 1, 0) for v in fields))
        rows = [fields[j][0:1, :] for j in range(LOADS)]
        rows.append(jnp.zeros((LANES - LOADS, LANES), jnp.float32))
        flipped[...] = jnp.concatenate(rows, axis=0).T

    @pl.when(owner)
    def _():
        wait_for(part_recv, (GROUP - 1) * USED, part_rsem)

        @pl.when(outer)
        def _():
            for half in (0, 1):
                got = flipped[pl.ds(half * SUBS * SUBS, SUBS, stride=SUBS), :]
                for j in range(LOADS):
                    rows = pl.ds(half * SUBS * SLOT + j, SUBS, stride=SLOT)
                    start_lane = jnp.where(lane == 0, spin(got, -j), 0.0)
                    end_lane = jnp.where(lane == LANES - 1, spin(got, -1 - j), 0.0)
                    part_recv[rows, :] += jnp.where(place == 0, start_lane, end_lane)

        evens, odds = (
            tuple(part_recv[pl.ds(at + j, SUBS, stride=2 * SLOT), :] for j in range(USED))
            for at in (0, SLOT)
        )
        fields, way, value = climb(evens, odds)
        trail = [(way, value, 0)]
        for shift in (1, 2, 4):
            raised = tuple(pltpu.roll(v, SUBS - shift, 0) for v in fields)
            fields, way, value = climb(fields, raised)
            trail.append((way, value, shift))

        for j in range(USED):
            line_send[pl.ds(j, 1), :] = fields[j][0:1, :]
        line_copies = [
            pltpu.make_async_remote_copy(
                src_ref=line_send.at[pl.ds(0, USED)],
                dst_ref=slot(line_recv, group, SLOT, USED),
                send_sem=line_ssem,
                recv_sem=line_rsem,
                device_id={"solve": other * GROUP + place},
                device_id_type=MESH,
            )
            for other in others
        ]
        for copy in line_copies:
            copy.start()
        here = pl.ds(pl.multiple_of(group * SLOT, SLOT), USED)
        line_recv[here, :] = line_send[pl.ds(0, USED), :]

        for i, column in enumerate((0, OWNERS - 1)):

            @pl.when(place == column)
            def _():
                for mate in mates:
                    pltpu.make_async_remote_copy(
                        src_ref=slot(flux_send, mate, SUBS, SUBS),
                        dst_ref=flux_recv.at[pl.ds(i * SUBS, SUBS)],
                        send_sem=flux_ssem,
                        recv_sem=flux_rsem,
                        device_id={"solve": base + mate},
                        device_id_type=MESH,
                    ).start()
                flux_recv[pl.ds(i * SUBS, SUBS), :] = flux_send[pl.ds(column * SUBS, SUBS), :]

        everything = line_recv.at[pl.ds(0, (groups - 1) * USED)]
        pltpu.make_async_copy(everything, everything, line_rsem).wait()

        chain = []
        for g in range(groups):
            chain.append(tuple(line_recv[pl.ds(g * SLOT + j, 1), :] for j in range(USED)))
        steps = []
        while len(chain) > 1:
            joined = [climb(chain[2 * m], chain[2 * m + 1]) for m in range(len(chain) // 2)]
            steps.append([item[1:] for item in joined])
            chain = [item[0] for item in joined]
        f1, f2, _, _, ea1, ea2, sa, n11, n12, n21, n22, _, _, _ = chain[0]
        i11, i12, i22 = inverse(sa, ea1 + (n11 + n12), ea2 + (n21 + n22))
        nothing = jnp.zeros_like(f1)
        nodes = [(i11 * f1 + i12 * f2, i12 * f1 + i22 * f2), (nothing, nothing)]
        for step in reversed(steps):
            finer = []
            for m, (way, value) in enumerate(step):
                finer += [nodes[m], middle(way, value, nodes[m], nodes[m + 1])]
            nodes = finer + [nodes[-1]]
        for plane in (0, 1):
            for g in range(groups + 1):
                pick[plane, pl.ds(g, 1), :] = nodes[g][plane]
        before, after = (
            tuple(
                jnp.broadcast_to(pick[plane, pl.ds(group + step, 1), :], (SUBS, LANES))
                for plane in (0, 1)
            )
            for step in (0, 1)
        )

        for way, value, shift in reversed(trail):
            inner = middle(way, value, before, after)
            if shift == 0:
                break
            first = (sub & shift) == 0
            before = tuple(
                jnp.where(first, b, pltpu.roll(v, shift, 0)) for b, v in zip(before, inner)
            )
            after = tuple(
                jnp.where(first, v, pltpu.roll(a, shift, 0)) for v, a in zip(inner, after)
            )
        for j, value in enumerate(before + inner + inner + after):
            node_send[pl.ds(j, SUBS, stride=2 * LOADS), :] = value
        node_copies = [
            pltpu.make_async_remote_copy(
                src_ref=slot(node_send, mate, LOADS, LOADS),
                dst_ref=slot(node_recv, place, LOADS, LOADS),
                send_sem=node_ssem,
                recv_sem=node_rsem,
                device_id={"solve": base + mate},
                device_id_type=MESH,
            )
            for mate in mates
        ]
        for copy in node_copies:
            copy.start()
        here = pl.ds(pl.multiple_of(place * LOADS, LOADS), LOADS)
        node_recv[here, :] = node_send[here, :]

    @pl.when(outer)
    def _():
        wait_for(flux_recv, SUBS, flux_rsem)

    @pl.when(jnp.logical_not(outer))
    def _():
        wait_for(flux_recv, 2 * SUBS, flux_rsem)

    for i, (column, at) in enumerate(((0, 0), (SUBS - 1, LANES - 1))):
        flux = flux_recv[pl.ds(i * SUBS, SUBS), :]
        for j in range(4):
            where = pl.ds((j * SUBS + column) * SUBS, SUBS)
            source[where, :] += jnp.where(lane == at, spin(flux, at - j), 0.0)
    _, owns = climb_loads()

    @pl.when(owner)
    def _():
        wait_for(node_recv, (OWNERS - 1) * LOADS, node_rsem)

    @pl.when(jnp.logical_not(owner))
    def _():
        wait_for(node_recv, OWNERS * LOADS, node_rsem)

    values = [node_recv[pl.ds(j, SUBS, stride=LOADS), :] for j in range(LOADS)]
    ends = [tuple(values[:2]), tuple(values[2:])]

    nodes = ends
    for back, own in zip(reversed(backs), reversed(owns)):
        finer = []
        for m in range(len(back)):
            finer += [nodes[m], middle(back[m], own[m], nodes[m], nodes[m + 1])]
        nodes = finer + [nodes[-1]]
    for i in range(ROWS):
        for plane in (0, 1):
            start = (plane * 2 + i // SUBS) * SUBS * SUBS + i % SUBS
            out_ref[pl.ds(start, SUBS, stride=SUBS), :] = nodes[i][plane]

    @pl.when(outer)
    def _():
        wait_for(edge_own, 3 * SUBS, edge_ssem)
        wait_for(flux_send, (GROUP - 1) * SUBS, flux_ssem)

    @pl.when(jnp.logical_not(outer))
    def _():
        wait_for(edge_own, 4 * SUBS, edge_ssem)

    @pl.when(owner)
    def _():
        wait_for(part_send, (OWNERS - 1) * USED, part_ssem)
        wait_for(line_recv, (groups - 1) * USED, line_ssem)
        wait_for(node_send, (GROUP - 1) * LOADS, node_ssem)

    @pl.when(jnp.logical_not(owner))
    def _():
        wait_for(part_send, OWNERS * USED, part_ssem)


def tiles(array):
    array = array.reshape(-1, ROWS // SUBS, SUBS, SUBS, LANES)
    return array.transpose(0, 1, 3, 2, 4).reshape(-1, LANES)


def per_device(temperature, transfer, diffusivity, exchange):
    groups = lax.axis_size("solve") // GROUP
    vmem = lambda *shape: pltpu.VMEM(shape, jnp.float32)
    dma = pltpu.SemaphoreType.DMA
    out = pl.pallas_call(
        functools.partial(kernel, groups),
        out_shape=jax.ShapeDtypeStruct((FLAT, LANES), jnp.float32),
        in_specs=[pl.BlockSpec(memory_space=pltpu.HBM)] * 4,
        out_specs=pl.BlockSpec(memory_space=pltpu.VMEM),
        scratch_shapes=[
            vmem(FLAT, LANES),
            vmem(FLAT, LANES),
            vmem(FLAT, LANES),
            vmem(FLAT // 2, LANES),
            vmem(FLAT, LANES),
            vmem(2 * SUBS, LANES),
            vmem(GROUP * SUBS, LANES),
            vmem(GROUP * SUBS, LANES),
            vmem(GROUP * SUBS, LANES),
            vmem(2 * SUBS, LANES),
            vmem(LANES, LANES),
            vmem(OWNERS * SLOT, LANES),
            vmem(GROUP * SLOT, LANES),
            vmem(SLOT, LANES),
            vmem(groups * SLOT, LANES),
            vmem(2, SUBS, LANES),
            vmem(GROUP * LOADS, LANES),
            vmem(OWNERS * LOADS, LANES),
            dma((4,)),
            dma,
            dma,
            dma,
            dma,
            dma,
            dma,
            dma,
            dma,
            dma,
            dma,
            dma,
        ],
        compiler_params=pltpu.CompilerParams(
            collective_id=0, has_side_effects=True, vmem_limit_bytes=16 * 1024 * 1024
        ),
        cost_estimate=pl.CostEstimate(
            flops=4_000_000, bytes_accessed=600_000, transcendentals=0
        ),
        name="line_step",
    )(
        *(
            pltpu.with_memory_space_constraint(tiles(array), pltpu.HBM)
            for array in (temperature, transfer, diffusivity, exchange)
        )
    )
    out = out.reshape(2, ROWS // SUBS, SUBS, SUBS, LANES).transpose(0, 1, 3, 2, 4)
    return out.reshape(2, ROWS, SUBS * LANES)


def solution(mesh):
    specs = (P(None, "solve", "cross"),) * 3 + (P("solve", "cross"),)
    return jax.shard_map(
        per_device,
        mesh=mesh,
        in_specs=specs,
        out_specs=P(None, "solve", "cross"),
        check_vma=False,
    )
```

```python
import functools

import jax
import jax.numpy as jnp
from jax import lax
from jax.experimental import pallas as pl
from jax.experimental.pallas import tpu as pltpu
from jax.sharding import PartitionSpec as P

MESH = pl.DeviceIdType.MESH
ROWS, SUBS, LANES = 16, 8, 128
GROUP, OWNERS = 16, 8
LOADS, USED, SLOT = 4, 14, 16
FLAT = 2 * ROWS * SUBS


def inverse(coupling, first, second):
    scale = 1.0 / (coupling * (first + second) + first * second)
    return (coupling + second) * scale, coupling * scale, (coupling + first) * scale


def merge(left, right):
    ea1, ea2, sa, n11, n12, n21, n22, ec1, ec2, sc = left
    fa1, fa2, fs, m11, m12, m21, m22, fc1, fc2, gs = right
    eb1, eb2, sb = ec1 + fa1, ec2 + fa2, sc + fs
    r1 = eb1 + ((n11 + n21) + (m11 + m12))
    r2 = eb2 + ((n12 + n22) + (m21 + m22))
    i11, i12, i22 = inverse(sb, r1, r2)
    g11, g12 = n11 * i11 + n12 * i12, n11 * i12 + n12 * i22
    g21, g22 = n21 * i11 + n22 * i12, n21 * i12 + n22 * i22
    h11, h12 = i11 * m11 + i12 * m21, i11 * m12 + i12 * m22
    h21, h22 = i12 * m11 + i22 * m21, i12 * m12 + i22 * m22
    joined = (
        ea1 + (g11 * eb1 + g12 * eb2),
        ea2 + (g21 * eb1 + g22 * eb2),
        sa + (g11 * n21 + g12 * n22),
        g11 * m11 + g12 * m21,
        g11 * m12 + g12 * m22,
        g21 * m11 + g22 * m21,
        g21 * m12 + g22 * m22,
        fc1 + (h11 * eb1 + h21 * eb2),
        fc2 + (h12 * eb1 + h22 * eb2),
        gs + (m11 * h12 + m21 * h22),
    )
    return joined, (i11, i12, i22, g11, g12, g21, g22, h11, h12, h21, h22)


def merge_leaf(sa, sb, n1, n2, m1, m2):
    r1, r2 = 1.0 + (n1 + m1), 1.0 + (n2 + m2)
    i11, i12, i22 = inverse(sb, r1, r2)
    g11, g12, g21, g22 = n1 * i11, n1 * i12, n2 * i12, n2 * i22
    h11, h12, h21, h22 = i11 * m1, i12 * m2, i12 * m1, i22 * m2
    joined = (
        1.0 + (g11 + g12),
        1.0 + (g21 + g22),
        sa + g12 * n2,
        g11 * m1,
        g12 * m2,
        g21 * m1,
        g22 * m2,
        h11 + h21,
        h12 + h22,
        m1 * h12,
    )
    return joined, (i11, i12, i22, g11, g12, g21, g22, h11, h12, h21, h22)


def merge_loads(back, left, right):
    i11, i12, i22, g11, g12, g21, g22, h11, h12, h21, h22 = back
    a1, a2, b1, b2 = left
    c1, c2, d1, d2 = right
    b1, b2 = b1 + c1, b2 + c2
    loads = (
        a1 + (g11 * b1 + g12 * b2),
        a2 + (g21 * b1 + g22 * b2),
        d1 + (h11 * b1 + h21 * b2),
        d2 + (h12 * b1 + h22 * b2),
    )
    return loads, (i11 * b1 + i12 * b2, i12 * b1 + i22 * b2)


def merge_leaf_loads(back, a, b):
    i11, i12, i22, g11, g12, g21, g22, h11, h12, h21, h22 = back
    a1, a2 = a
    b1, b2 = b
    loads = (
        a1 + (g11 * b1 + g12 * b2),
        a2 + (g21 * b1 + g22 * b2),
        h11 * b1 + h21 * b2,
        h12 * b1 + h22 * b2,
    )
    return loads, (i11 * b1 + i12 * b2, i12 * b1 + i22 * b2)


def middle(back, own, before, after):
    g11, g12, g21, g22, h11, h12, h21, h22 = back[3:]
    a1, a2 = before
    c1, c2 = after
    return (
        own[0] + ((g11 * a1 + g21 * a2) + (h11 * c1 + h12 * c2)),
        own[1] + ((g12 * a1 + g22 * a2) + (h21 * c1 + h22 * c2)),
    )


def kernel(
    groups,
    temp_hbm,
    face_hbm,
    diff_hbm,
    sheet_hbm,
    out_ref,
    temp,
    face,
    diff,
    sheet,
    source,
    edge_send,
    edge_own,
    edge_far,
    flux_send,
    flux_recv,
    flipped,
    part_send,
    part_recv,
    line_send,
    line_recv,
    pick,
    node_send,
    node_recv,
    in_sem,
    edge_ssem,
    own_rsem,
    far_rsem,
    flux_ssem,
    flux_rsem,
    part_ssem,
    part_rsem,
    line_ssem,
    line_rsem,
    node_ssem,
    node_rsem,
):
    solve = lax.axis_index("solve")
    cross = lax.axis_index("cross")
    n_cross = lax.axis_size("cross")
    place = lax.rem(solve, GROUP)
    group = lax.div(solve, GROUP)
    base = solve - place

    loads_in = [
        pltpu.make_async_copy(src, dst, in_sem.at[i])
        for i, (src, dst) in enumerate(
            ((temp_hbm, temp), (diff_hbm, diff), (face_hbm, face), (sheet_hbm, sheet))
        )
    ]
    for copy in loads_in:
        copy.start()

    owner = place < OWNERS
    outer = (place == 0) | (place == OWNERS - 1)
    owners = [lax.rem(place + step, OWNERS) for step in (4, 5, 3, 6, 2, 7, 1, 0)]
    order = [8, 9, 7, 10, 6, 11, 5, 12, 4, 13, 3, 14, 2, 15, 1]
    mates = [lax.rem(place + step, GROUP) for step in order]
    others = [lax.rem(group + step, groups) for step in range(1, groups)]
    right = lax.rem(cross + 1, n_cross)
    left = lax.rem(cross + n_cross - 1, n_cross)

    barrier = pltpu.get_barrier_semaphore()
    for column, side in ((0, left), (OWNERS - 1, right)):

        @pl.when(place == column)
        def _():
            for mate in range(GROUP):
                pl.semaphore_signal(
                    barrier,
                    1,
                    device_id={"solve": base + mate, "cross": side},
                    device_id_type=MESH,
                )

    @pl.when(owner)
    def _():
        for mate in mates:
            pl.semaphore_signal(
                barrier, 1, device_id={"solve": base + mate}, device_id_type=MESH
            )
        for other in others:
            pl.semaphore_signal(
                barrier, 1, device_id={"solve": other * GROUP + place}, device_id_type=MESH
            )

    lane = lax.broadcasted_iota(jnp.int32, (SUBS, LANES), 1)
    sub = lax.broadcasted_iota(jnp.int32, (SUBS, LANES), 0)

    def spin(value, shift):
        return pltpu.roll(value, shift % LANES, 1)

    def tile(ref, block, column):
        return ref[pl.ds((block * SUBS + column) * SUBS, SUBS), :]

    def slot(ref, index, rows, used):
        start = index * rows if isinstance(index, int) else pl.multiple_of(index * rows, rows)
        return ref.at[pl.ds(start, used)]

    for copy in loads_in:
        copy.wait()
    tracks = [(ref, j) for ref in (temp, diff, face) for j in range(4)]
    tracks += [(sheet, 0), (sheet, 1)]
    for i, (column, shift) in enumerate(((0, 0), (SUBS - 1, 1))):
        packed = jnp.zeros((SUBS, LANES), jnp.float32)
        for j, (ref, block) in enumerate(tracks):
            packed = jnp.where(lane == j, spin(tile(ref, block, column), j + shift), packed)
        edge_send[pl.ds(i * SUBS, SUBS), :] = packed

    @pl.when(owner)
    def _():
        pl.semaphore_wait(barrier, 2 + OWNERS - 1 + len(others))

    @pl.when(jnp.logical_not(owner))
    def _():
        pl.semaphore_wait(barrier, 2 + OWNERS)

    for i, (mine, theirs, side) in enumerate(
        ((0, OWNERS - 1, left), (OWNERS - 1, 0, right))
    ):
        edge = edge_send.at[pl.ds(i * SUBS, SUBS)]
        pltpu.make_async_remote_copy(
            src_ref=edge,
            dst_ref=slot(edge_far, place, SUBS, SUBS),
            send_sem=edge_ssem,
            recv_sem=far_rsem,
            device_id={"solve": base + theirs, "cross": side},
            device_id_type=MESH,
        ).start()

        @pl.when(place != mine)
        def _():
            pltpu.make_async_remote_copy(
                src_ref=edge,
                dst_ref=slot(edge_own, place, SUBS, SUBS),
                send_sem=edge_ssem,
                recv_sem=own_rsem,
                device_id={"solve": base + mine},
                device_id_type=MESH,
            ).start()

        @pl.when(place == mine)
        def _():
            edge_own[pl.ds(mine * SUBS, SUBS), :] = edge_send[pl.ds(i * SUBS, SUBS), :]

    zero = jnp.zeros((SUBS, LANES), jnp.float32)
    for block in range(4):
        heat = [tile(temp, block, t) for t in range(SUBS)]
        cond = [tile(diff, block, t) for t in range(SUBS)]
        heat_turned = [spin(v, -1) for v in heat] + [zero]
        cond_turned = [spin(v, -1) for v in cond] + [zero]
        last = lane == LANES - 1
        before = zero
        for t in range(SUBS):
            next_heat = jnp.where(last, heat_turned[t + 1], heat_turned[t])
            next_cond = jnp.where(last, cond_turned[t + 1], cond_turned[t])
            flux = 0.5 * (cond[t] + next_cond) * (next_heat - heat[t])
            if t == SUBS - 1:
                flux = jnp.where(last, 0.0, flux)
            turned = spin(flux, 1)
            previous = jnp.where(lane == 0, before, turned)
            before = turned
            source[pl.ds((block * SUBS + t) * SUBS, SUBS), :] = heat[t] + flux - previous

    def row(ref, plane, i):
        start = (plane * 2 + i // SUBS) * SUBS * SUBS + i % SUBS
        return ref[pl.ds(start, SUBS, stride=SUBS), :]

    backs = []
    level = []
    back = []
    for m in range(ROWS // 2):
        element, way = merge_leaf(
            row(sheet, 0, 2 * m),
            row(sheet, 0, 2 * m + 1),
            row(face, 0, 2 * m),
            row(face, 1, 2 * m),
            row(face, 0, 2 * m + 1),
            row(face, 1, 2 * m + 1),
        )
        level.append(element)
        back.append(way)
    backs.append(back)
    while len(level) > 1:
        pairs = [merge(level[2 * m], level[2 * m + 1]) for m in range(len(level) // 2)]
        level = [pair[0] for pair in pairs]
        backs.append([pair[1] for pair in pairs])
    element = level[0]

    def climb_loads():
        owns = []
        level = []
        own = []
        for m in range(ROWS // 2):
            loads, value = merge_leaf_loads(
                backs[0][m],
                (row(source, 0, 2 * m), row(source, 1, 2 * m)),
                (row(source, 0, 2 * m + 1), row(source, 1, 2 * m + 1)),
            )
            level.append(loads)
            own.append(value)
        owns.append(own)
        for back in backs[1:]:
            pairs = [
                merge_loads(back[m], level[2 * m], level[2 * m + 1]) for m in range(len(back))
            ]
            level = [pair[0] for pair in pairs]
            owns.append([pair[1] for pair in pairs])
        return level[0], owns

    loads, _ = climb_loads()
    for j, value in enumerate(loads + element):
        part_send[pl.ds(j, SUBS, stride=SLOT), :] = value

    for mate in owners:

        @pl.when(mate != place)
        def _():
            pltpu.make_async_remote_copy(
                src_ref=slot(part_send, mate, SLOT, USED),
                dst_ref=slot(part_recv, place, SLOT, USED),
                send_sem=part_ssem,
                recv_sem=part_rsem,
                device_id={"solve": base + mate},
                device_id_type=MESH,
            ).start()

    @pl.when(owner)
    def _():
        here = pl.ds(pl.multiple_of(place * SLOT, SLOT), USED)
        part_recv[here, :] = part_send[here, :]

    def climb(left_fields, right_fields):
        element, way = merge(left_fields[LOADS:], right_fields[LOADS:])
        loads, value = merge_loads(way, left_fields[:LOADS], right_fields[:LOADS])
        return loads + element, way, value

    def wait_for(ref, rows, sem):
        part = ref.at[pl.ds(0, rows)]
        pltpu.make_async_copy(part, part, sem).wait()

    @pl.when(outer)
    def _():
        wait_for(edge_own, (GROUP - 1) * SUBS, own_rsem)
        wait_for(edge_far, GROUP * SUBS, far_rsem)
        inside = jnp.where(place == 0, cross > 0, cross < n_cross - 1)
        for mate in range(GROUP):
            where = pl.ds(mate * SUBS, SUBS)
            own = edge_own[where, :]
            far = jnp.where(inside, edge_far[where, :], 0.0)
            flux_send[where, :] = 0.5 * spin(own + far, -4) * (far - own)
        flipped[pl.ds(0, 32), :] = edge_own[...].T[:32]
        flipped[pl.ds(32, 32), :] = flux_send[...].T[:32]
        side1, side2, first1, first2, second = (
            flipped[pl.ds(at, SUBS), :] for at in (32, 34, 8, 10, 12)
        )
        element, way = merge_leaf(
            second, spin(second, -1), first1, first2, spin(first1, -1), spin(first2, -1)
        )
        loads, _ = merge_leaf_loads(way, (side1, side2), (spin(side1, -1), spin(side2, -1)))
        fields = loads + element
        for shift in (2, 4):
            fields, _, _ = climb(fields, tuple(spin(v, -shift) for v in fields))
        fields, _, _ = climb(fields, tuple(pltpu.roll(v, SUBS - 1, 0) for v in fields))
        rows = [fields[j][0:1, :] for j in range(LOADS)]
        rows.append(jnp.zeros((LANES - LOADS, LANES), jnp.float32))
        flipped[...] = jnp.concatenate(rows, axis=0).T

    @pl.when(owner)
    def _():
        wait_for(part_recv, (GROUP - 1) * USED, part_rsem)

        @pl.when(outer)
        def _():
            for half in (0, 1):
                got = flipped[pl.ds(half * SUBS * SUBS, SUBS, stride=SUBS), :]
                for j in range(LOADS):
                    rows = pl.ds(half * SUBS * SLOT + j, SUBS, stride=SLOT)
                    start_lane = jnp.where(lane == 0, spin(got, -j), 0.0)
                    end_lane = jnp.where(lane == LANES - 1, spin(got, -1 - j), 0.0)
                    part_recv[rows, :] += jnp.where(place == 0, start_lane, end_lane)

        evens, odds = (
            tuple(part_recv[pl.ds(at + j, SUBS, stride=2 * SLOT), :] for j in range(USED))
            for at in (0, SLOT)
        )
        fields, way, value = climb(evens, odds)
        trail = [(way, value, 0)]
        for shift in (1, 2, 4):
            raised = tuple(pltpu.roll(v, SUBS - shift, 0) for v in fields)
            fields, way, value = climb(fields, raised)
            trail.append((way, value, shift))

        for j in range(USED):
            line_send[pl.ds(j, 1), :] = fields[j][0:1, :]
        line_copies = [
            pltpu.make_async_remote_copy(
                src_ref=line_send.at[pl.ds(0, USED)],
                dst_ref=slot(line_recv, group, SLOT, USED),
                send_sem=line_ssem,
                recv_sem=line_rsem,
                device_id={"solve": other * GROUP + place},
                device_id_type=MESH,
            )
            for other in others
        ]
        for copy in line_copies:
            copy.start()
        here = pl.ds(pl.multiple_of(group * SLOT, SLOT), USED)
        line_recv[here, :] = line_send[pl.ds(0, USED), :]

        for i, column in enumerate((0, OWNERS - 1)):

            @pl.when(place == column)
            def _():
                for mate in mates:
                    pltpu.make_async_remote_copy(
                        src_ref=slot(flux_send, mate, SUBS, SUBS),
                        dst_ref=flux_recv.at[pl.ds(i * SUBS, SUBS)],
                        send_sem=flux_ssem,
                        recv_sem=flux_rsem,
                        device_id={"solve": base + mate},
                        device_id_type=MESH,
                    ).start()
                flux_recv[pl.ds(i * SUBS, SUBS), :] = flux_send[pl.ds(column * SUBS, SUBS), :]

        everything = line_recv.at[pl.ds(0, (groups - 1) * USED)]
        pltpu.make_async_copy(everything, everything, line_rsem).wait()

        chain = []
        for g in range(groups):
            chain.append(tuple(line_recv[pl.ds(g * SLOT + j, 1), :] for j in range(USED)))
        steps = []
        while len(chain) > 1:
            joined = [climb(chain[2 * m], chain[2 * m + 1]) for m in range(len(chain) // 2)]
            steps.append([item[1:] for item in joined])
            chain = [item[0] for item in joined]
        f1, f2, _, _, ea1, ea2, sa, n11, n12, n21, n22, _, _, _ = chain[0]
        i11, i12, i22 = inverse(sa, ea1 + (n11 + n12), ea2 + (n21 + n22))
        nothing = jnp.zeros_like(f1)
        nodes = [(i11 * f1 + i12 * f2, i12 * f1 + i22 * f2), (nothing, nothing)]
        for step in reversed(steps):
            finer = []
            for m, (way, value) in enumerate(step):
                finer += [nodes[m], middle(way, value, nodes[m], nodes[m + 1])]
            nodes = finer + [nodes[-1]]
        for plane in (0, 1):
            for g in range(groups + 1):
                pick[plane, pl.ds(g, 1), :] = nodes[g][plane]
        before, after = (
            tuple(
                jnp.broadcast_to(pick[plane, pl.ds(group + step, 1), :], (SUBS, LANES))
                for plane in (0, 1)
            )
            for step in (0, 1)
        )

        for way, value, shift in reversed(trail):
            inner = middle(way, value, before, after)
            if shift == 0:
                break
            first = (sub & shift) == 0
            before = tuple(
                jnp.where(first, b, pltpu.roll(v, shift, 0)) for b, v in zip(before, inner)
            )
            after = tuple(
                jnp.where(first, v, pltpu.roll(a, shift, 0)) for v, a in zip(inner, after)
            )
        for j, value in enumerate(before + inner + inner + after):
            node_send[pl.ds(j, SUBS, stride=2 * LOADS), :] = value
        for mate in [1, 0] + list(range(2, GROUP)):

            @pl.when(place != mate)
            def _():
                pltpu.make_async_remote_copy(
                    src_ref=slot(node_send, mate, LOADS, LOADS),
                    dst_ref=slot(node_recv, place, LOADS, LOADS),
                    send_sem=node_ssem,
                    recv_sem=node_rsem,
                    device_id={"solve": base + mate},
                    device_id_type=MESH,
                ).start()

        here = pl.ds(pl.multiple_of(place * LOADS, LOADS), LOADS)
        node_recv[here, :] = node_send[here, :]

    @pl.when(outer)
    def _():
        wait_for(flux_recv, SUBS, flux_rsem)

    @pl.when(jnp.logical_not(outer))
    def _():
        wait_for(flux_recv, 2 * SUBS, flux_rsem)

    for i, (column, at) in enumerate(((0, 0), (SUBS - 1, LANES - 1))):
        flux = flux_recv[pl.ds(i * SUBS, SUBS), :]
        for j in range(4):
            where = pl.ds((j * SUBS + column) * SUBS, SUBS)
            source[where, :] += jnp.where(lane == at, spin(flux, at - j), 0.0)
    _, owns = climb_loads()

    @pl.when(owner)
    def _():
        wait_for(node_recv, (OWNERS - 1) * LOADS, node_rsem)

    @pl.when(jnp.logical_not(owner))
    def _():
        wait_for(node_recv, OWNERS * LOADS, node_rsem)

    values = [node_recv[pl.ds(j, SUBS, stride=LOADS), :] for j in range(LOADS)]
    ends = [tuple(values[:2]), tuple(values[2:])]

    nodes = ends
    for back, own in zip(reversed(backs), reversed(owns)):
        finer = []
        for m in range(len(back)):
            finer += [nodes[m], middle(back[m], own[m], nodes[m], nodes[m + 1])]
        nodes = finer + [nodes[-1]]
    for i in range(ROWS):
        for plane in (0, 1):
            start = (plane * 2 + i // SUBS) * SUBS * SUBS + i % SUBS
            out_ref[pl.ds(start, SUBS, stride=SUBS), :] = nodes[i][plane]

    @pl.when(outer)
    def _():
        wait_for(edge_own, 3 * SUBS, edge_ssem)
        wait_for(flux_send, (GROUP - 1) * SUBS, flux_ssem)

    @pl.when(jnp.logical_not(outer))
    def _():
        wait_for(edge_own, 4 * SUBS, edge_ssem)

    @pl.when(owner)
    def _():
        wait_for(part_send, (OWNERS - 1) * USED, part_ssem)
        wait_for(line_recv, (groups - 1) * USED, line_ssem)
        wait_for(node_send, (GROUP - 1) * LOADS, node_ssem)

    @pl.when(jnp.logical_not(owner))
    def _():
        wait_for(part_send, OWNERS * USED, part_ssem)


def tiles(array):
    array = array.reshape(-1, ROWS // SUBS, SUBS, SUBS, LANES)
    return array.transpose(0, 1, 3, 2, 4).reshape(-1, LANES)


def per_device(temperature, transfer, diffusivity, exchange):
    groups = lax.axis_size("solve") // GROUP
    vmem = lambda *shape: pltpu.VMEM(shape, jnp.float32)
    dma = pltpu.SemaphoreType.DMA
    out = pl.pallas_call(
        functools.partial(kernel, groups),
        out_shape=jax.ShapeDtypeStruct((FLAT, LANES), jnp.float32),
        in_specs=[pl.BlockSpec(memory_space=pltpu.HBM)] * 4,
        out_specs=pl.BlockSpec(memory_space=pltpu.VMEM),
        scratch_shapes=[
            vmem(FLAT, LANES),
            vmem(FLAT, LANES),
            vmem(FLAT, LANES),
            vmem(FLAT // 2, LANES),
            vmem(FLAT, LANES),
            vmem(2 * SUBS, LANES),
            vmem(GROUP * SUBS, LANES),
            vmem(GROUP * SUBS, LANES),
            vmem(GROUP * SUBS, LANES),
            vmem(2 * SUBS, LANES),
            vmem(LANES, LANES),
            vmem(OWNERS * SLOT, LANES),
            vmem(GROUP * SLOT, LANES),
            vmem(SLOT, LANES),
            vmem(groups * SLOT, LANES),
            vmem(2, SUBS, LANES),
            vmem(GROUP * LOADS, LANES),
            vmem(OWNERS * LOADS, LANES),
            dma((4,)),
            dma,
            dma,
            dma,
            dma,
            dma,
            dma,
            dma,
            dma,
            dma,
            dma,
            dma,
        ],
        compiler_params=pltpu.CompilerParams(
            collective_id=0, has_side_effects=True, vmem_limit_bytes=16 * 1024 * 1024
        ),
        cost_estimate=pl.CostEstimate(
            flops=4_000_000, bytes_accessed=600_000, transcendentals=0
        ),
        name="line_step",
    )(
        *(
            pltpu.with_memory_space_constraint(tiles(array), pltpu.HBM)
            for array in (temperature, transfer, diffusivity, exchange)
        )
    )
    out = out.reshape(2, ROWS // SUBS, SUBS, SUBS, LANES).transpose(0, 1, 3, 2, 4)
    return out.reshape(2, ROWS, SUBS * LANES)


def solution(mesh):
    specs = (P(None, "solve", "cross"),) * 3 + (P("solve", "cross"),)
    return jax.shard_map(
        per_device,
        mesh=mesh,
        in_specs=specs,
        out_specs=P(None, "solve", "cross"),
        check_vma=False,
    )
```

```python
import jax
import jax.numpy as jnp
from jax import lax
from jax.experimental import pallas as pl
from jax.experimental.pallas import tpu as pltpu
from jax.sharding import PartitionSpec as P

MESH = pl.DeviceIdType.MESH
ROWS, SUBS, LANES = 16, 8, 128
GROUP, OWNERS, PARTS = 16, 8, 64
FIRST, LAST = 0, 49
LOADS, USED, SLOT = 4, 14, 16
FLAT = 2 * ROWS * SUBS


def inverse(coupling, first, second):
    scale = 1.0 / (coupling * (first + second) + first * second)
    return (coupling + second) * scale, coupling * scale, (coupling + first) * scale


def merge(left, right):
    ea1, ea2, sa, n11, n12, n21, n22, ec1, ec2, sc = left
    fa1, fa2, fs, m11, m12, m21, m22, fc1, fc2, gs = right
    eb1, eb2, sb = ec1 + fa1, ec2 + fa2, sc + fs
    r1 = eb1 + ((n11 + n21) + (m11 + m12))
    r2 = eb2 + ((n12 + n22) + (m21 + m22))
    i11, i12, i22 = inverse(sb, r1, r2)
    g11, g12 = n11 * i11 + n12 * i12, n11 * i12 + n12 * i22
    g21, g22 = n21 * i11 + n22 * i12, n21 * i12 + n22 * i22
    h11, h12 = i11 * m11 + i12 * m21, i11 * m12 + i12 * m22
    h21, h22 = i12 * m11 + i22 * m21, i12 * m12 + i22 * m22
    joined = (
        ea1 + (g11 * eb1 + g12 * eb2),
        ea2 + (g21 * eb1 + g22 * eb2),
        sa + (g11 * n21 + g12 * n22),
        g11 * m11 + g12 * m21,
        g11 * m12 + g12 * m22,
        g21 * m11 + g22 * m21,
        g21 * m12 + g22 * m22,
        fc1 + (h11 * eb1 + h21 * eb2),
        fc2 + (h12 * eb1 + h22 * eb2),
        gs + (m11 * h12 + m21 * h22),
    )
    return joined, (i11, i12, i22, g11, g12, g21, g22, h11, h12, h21, h22)


def merge_leaf(sa, sb, n1, n2, m1, m2):
    r1, r2 = 1.0 + (n1 + m1), 1.0 + (n2 + m2)
    i11, i12, i22 = inverse(sb, r1, r2)
    g11, g12, g21, g22 = n1 * i11, n1 * i12, n2 * i12, n2 * i22
    h11, h12, h21, h22 = i11 * m1, i12 * m2, i12 * m1, i22 * m2
    joined = (
        1.0 + (g11 + g12),
        1.0 + (g21 + g22),
        sa + g12 * n2,
        g11 * m1,
        g12 * m2,
        g21 * m1,
        g22 * m2,
        h11 + h21,
        h12 + h22,
        m1 * h12,
    )
    return joined, (i11, i12, i22, g11, g12, g21, g22, h11, h12, h21, h22)


def merge_loads(back, left, right):
    i11, i12, i22, g11, g12, g21, g22, h11, h12, h21, h22 = back
    a1, a2, b1, b2 = left
    c1, c2, d1, d2 = right
    b1, b2 = b1 + c1, b2 + c2
    loads = (
        a1 + (g11 * b1 + g12 * b2),
        a2 + (g21 * b1 + g22 * b2),
        d1 + (h11 * b1 + h21 * b2),
        d2 + (h12 * b1 + h22 * b2),
    )
    return loads, (i11 * b1 + i12 * b2, i12 * b1 + i22 * b2)


def merge_leaf_loads(back, a, b):
    i11, i12, i22, g11, g12, g21, g22, h11, h12, h21, h22 = back
    a1, a2 = a
    b1, b2 = b
    loads = (
        a1 + (g11 * b1 + g12 * b2),
        a2 + (g21 * b1 + g22 * b2),
        h11 * b1 + h21 * b2,
        h12 * b1 + h22 * b2,
    )
    return loads, (i11 * b1 + i12 * b2, i12 * b1 + i22 * b2)


def middle(back, own, before, after):
    g11, g12, g21, g22, h11, h12, h21, h22 = back[3:]
    a1, a2 = before
    c1, c2 = after
    return (
        own[0] + ((g11 * a1 + g21 * a2) + (h11 * c1 + h12 * c2)),
        own[1] + ((g12 * a1 + g22 * a2) + (h21 * c1 + h22 * c2)),
    )


def kernel(
    temp_hbm,
    face_hbm,
    diff_hbm,
    sheet_hbm,
    out_ref,
    temp,
    face,
    diff,
    sheet,
    source,
    edge_send,
    edge_own,
    edge_far,
    flux_send,
    flux_recv,
    flipped,
    lined,
    part_send,
    part_recv,
    extra,
    node_send,
    node_recv,
    in_sem,
    edge_ssem,
    own_rsem,
    far_rsem,
    flux_ssem,
    flux_rsem,
    part_ssem,
    part_rsem,
    node_ssem,
    node_rsem,
):
    solve = lax.axis_index("solve")
    cross = lax.axis_index("cross")
    n_cross = lax.axis_size("cross")
    place = lax.rem(solve, GROUP)
    group = lax.div(solve, GROUP)

    loads_in = [
        pltpu.make_async_copy(src, dst, in_sem.at[i])
        for i, (src, dst) in enumerate(
            ((temp_hbm, temp), (diff_hbm, diff), (face_hbm, face), (sheet_hbm, sheet))
        )
    ]
    for copy in loads_in:
        copy.start()

    owner = place < 2
    column_row = group * 2 + place
    outer = (solve == FIRST) | (solve == LAST)
    rows_of = [lax.rem(solve + step, OWNERS) for step in range(OWNERS)]

    def device_of(index):
        return lax.div(index, 2) * GROUP + lax.rem(index, 2)

    right = lax.rem(cross + 1, n_cross)
    left = lax.rem(cross + n_cross - 1, n_cross)

    barrier = pltpu.get_barrier_semaphore()
    for column, side in ((FIRST, left), (LAST, right)):

        @pl.when(solve == column)
        def _():
            def greet(index, _):
                pl.semaphore_signal(
                    barrier,
                    1,
                    device_id={"solve": index, "cross": side},
                    device_id_type=MESH,
                )
                return 0

            lax.fori_loop(0, PARTS, greet, 0)

    @pl.when(owner)
    def _():
        def greet(step, _):
            pl.semaphore_signal(
                barrier,
                1,
                device_id={"solve": lax.rem(solve + step, PARTS)},
                device_id_type=MESH,
            )
            return 0

        lax.fori_loop(1, PARTS, greet, 0)
        extra[...] = jnp.zeros((PARTS * LOADS, LANES), jnp.float32)

    lane = lax.broadcasted_iota(jnp.int32, (SUBS, LANES), 1)
    sub = lax.broadcasted_iota(jnp.int32, (SUBS, LANES), 0)

    def spin(value, shift):
        return pltpu.roll(value, shift % LANES, 1)

    def tile(ref, block, column):
        return ref[pl.ds((block * SUBS + column) * SUBS, SUBS), :]

    def slot(ref, index, rows, used):
        start = index * rows if isinstance(index, int) else pl.multiple_of(index * rows, rows)
        return ref.at[pl.ds(start, used)]

    for copy in loads_in:
        copy.wait()
    tracks = [(ref, j) for ref in (temp, diff, face) for j in range(4)]
    tracks += [(sheet, 0), (sheet, 1)]
    for i, (column, shift) in enumerate(((0, 0), (SUBS - 1, 1))):
        packed = jnp.zeros((SUBS, LANES), jnp.float32)
        for j, (ref, block) in enumerate(tracks):
            packed = jnp.where(lane == j, spin(tile(ref, block, column), j + shift), packed)
        edge_send[pl.ds(i * SUBS, SUBS), :] = packed

    @pl.when(owner)
    def _():
        pl.semaphore_wait(barrier, 2 + OWNERS - 1)

    @pl.when(jnp.logical_not(owner))
    def _():
        pl.semaphore_wait(barrier, 2 + OWNERS)

    for i, (mine, theirs, side) in enumerate(
        ((FIRST, LAST, left), (LAST, FIRST, right))
    ):
        edge = edge_send.at[pl.ds(i * SUBS, SUBS)]
        pltpu.make_async_remote_copy(
            src_ref=edge,
            dst_ref=slot(edge_far, solve, SUBS, SUBS),
            send_sem=edge_ssem,
            recv_sem=far_rsem,
            device_id={"solve": theirs, "cross": side},
            device_id_type=MESH,
        ).start()

        @pl.when(solve != mine)
        def _():
            pltpu.make_async_remote_copy(
                src_ref=edge,
                dst_ref=slot(edge_own, solve, SUBS, SUBS),
                send_sem=edge_ssem,
                recv_sem=own_rsem,
                device_id={"solve": mine},
                device_id_type=MESH,
            ).start()

        @pl.when(solve == mine)
        def _():
            edge_own[pl.ds(mine * SUBS, SUBS), :] = edge_send[pl.ds(i * SUBS, SUBS), :]

    zero = jnp.zeros((SUBS, LANES), jnp.float32)
    for block in range(4):
        heat = [tile(temp, block, t) for t in range(SUBS)]
        cond = [tile(diff, block, t) for t in range(SUBS)]
        heat_turned = [spin(v, -1) for v in heat] + [zero]
        cond_turned = [spin(v, -1) for v in cond] + [zero]
        last = lane == LANES - 1
        before = zero
        for t in range(SUBS):
            next_heat = jnp.where(last, heat_turned[t + 1], heat_turned[t])
            next_cond = jnp.where(last, cond_turned[t + 1], cond_turned[t])
            flux = 0.5 * (cond[t] + next_cond) * (next_heat - heat[t])
            if t == SUBS - 1:
                flux = jnp.where(last, 0.0, flux)
            turned = spin(flux, 1)
            previous = jnp.where(lane == 0, before, turned)
            before = turned
            source[pl.ds((block * SUBS + t) * SUBS, SUBS), :] = heat[t] + flux - previous

    def row(ref, plane, i):
        start = (plane * 2 + i // SUBS) * SUBS * SUBS + i % SUBS
        return ref[pl.ds(start, SUBS, stride=SUBS), :]

    backs = []
    level = []
    back = []
    for m in range(ROWS // 2):
        element, way = merge_leaf(
            row(sheet, 0, 2 * m),
            row(sheet, 0, 2 * m + 1),
            row(face, 0, 2 * m),
            row(face, 1, 2 * m),
            row(face, 0, 2 * m + 1),
            row(face, 1, 2 * m + 1),
        )
        level.append(element)
        back.append(way)
    backs.append(back)
    while len(level) > 1:
        pairs = [merge(level[2 * m], level[2 * m + 1]) for m in range(len(level) // 2)]
        level = [pair[0] for pair in pairs]
        backs.append([pair[1] for pair in pairs])
    element = level[0]

    def climb_loads():
        owns = []
        level = []
        own = []
        for m in range(ROWS // 2):
            loads, value = merge_leaf_loads(
                backs[0][m],
                (row(source, 0, 2 * m), row(source, 1, 2 * m)),
                (row(source, 0, 2 * m + 1), row(source, 1, 2 * m + 1)),
            )
            level.append(loads)
            own.append(value)
        owns.append(own)
        for back in backs[1:]:
            pairs = [
                merge_loads(back[m], level[2 * m], level[2 * m + 1]) for m in range(len(back))
            ]
            level = [pair[0] for pair in pairs]
            owns.append([pair[1] for pair in pairs])
        return level[0], owns

    loads, _ = climb_loads()
    for j, value in enumerate(loads + element):
        part_send[pl.ds(j, SUBS, stride=SLOT), :] = value

    for index in rows_of:

        @pl.when(device_of(index) != solve)
        def _():
            pltpu.make_async_remote_copy(
                src_ref=slot(part_send, index, SLOT, USED),
                dst_ref=slot(part_recv, solve, SLOT, USED),
                send_sem=part_ssem,
                recv_sem=part_rsem,
                device_id={"solve": device_of(index)},
                device_id_type=MESH,
            ).start()

    @pl.when(owner)
    def _():
        here = pl.ds(pl.multiple_of(solve * SLOT, SLOT), USED)
        there = pl.ds(pl.multiple_of(column_row * SLOT, SLOT), USED)
        part_recv[here, :] = part_send[there, :]

    def climb(left_fields, right_fields):
        element, way = merge(left_fields[LOADS:], right_fields[LOADS:])
        loads, value = merge_loads(way, left_fields[:LOADS], right_fields[:LOADS])
        return loads + element, way, value

    def wait_for(ref, rows, sem):
        part = ref.at[pl.ds(0, rows)]
        pltpu.make_async_copy(part, part, sem).wait()

    def to_all(first, last, send):
        def one(n, _):
            part = lax.rem(lax.div(n, 2), 4) * GROUP + lax.div(n, 8) * 2 + lax.rem(n, 2)

            @pl.when(part != solve)
            def _():
                send(part)

            return 0

        lax.fori_loop(first, last, one, 0)

    def flux_to(i):
        def send(part):
            pltpu.make_async_remote_copy(
                src_ref=slot(flux_send, lax.div(part, GROUP), 4, 4),
                dst_ref=flux_recv.at[pl.ds(i * 4, 4)],
                send_sem=flux_ssem,
                recv_sem=flux_rsem,
                device_id={"solve": part},
                device_id_type=MESH,
            ).start()

        return send

    for i, (column, at, inside) in enumerate(
        ((FIRST, 0, cross > 0), (LAST, LANES - 1, cross < n_cross - 1))
    ):

        @pl.when(solve == column)
        def _():
            wait_for(edge_own, (PARTS - 1) * SUBS, own_rsem)
            wait_for(edge_far, PARTS * SUBS, far_rsem)
            for g in range(PARTS // GROUP):
                where = pl.ds(g * LANES, LANES)
                own = edge_own[where, :]
                far = jnp.where(inside, edge_far[where, :], 0.0)
                flux = 0.5 * spin(own + far, -4) * (far - own)
                flipped[pl.ds(0, SUBS), :] = flux.T[:SUBS]
                flipped[pl.ds(SUBS, 2 * SUBS), :] = own.T[: 2 * SUBS]
                flux_send[pl.ds(g * 4, 4), :] = flipped[pl.ds(0, 4), :]
                for f, row_at in enumerate((0, 2, 16, 18, 20)):
                    lined[pl.ds(f * SUBS + 2 * g, 2), :] = flipped[pl.ds(row_at, 2), :]
            side1, side2, first1, first2, second = (
                lined[pl.ds(f * SUBS, SUBS), :] for f in range(5)
            )
            element, way = merge_leaf(
                second, spin(second, -1), first1, first2, spin(first1, -1), spin(first2, -1)
            )
            loads, _ = merge_leaf_loads(
                way, (side1, side2), (spin(side1, -1), spin(side2, -1))
            )
            fields = loads + element
            for shift in (2, 4):
                fields, _, _ = climb(fields, tuple(spin(v, -shift) for v in fields))
            fields, _, _ = climb(fields, tuple(pltpu.roll(v, SUBS - 1, 0) for v in fields))
            rows = list(fields[:LOADS])
            rows.append(jnp.zeros((LANES - LOADS * SUBS, LANES), jnp.float32))
            flipped[...] = jnp.concatenate(rows, axis=0).T
            for half in (0, 1):
                got = flipped[pl.ds(half * SUBS * SUBS, SUBS, stride=SUBS), :]
                for g in range(PARTS // GROUP):
                    for j in range(LOADS):
                        moved = spin(got, at - j * SUBS - 2 * g)
                        at_rows = pl.ds(
                            (g * GROUP + half * SUBS) * LOADS + j, SUBS, stride=LOADS
                        )
                        extra[at_rows, :] = jnp.where(lane == at, moved, 0.0)
            to_all(0, 16, flux_to(i))
            flux_recv[pl.ds(i * 4, 4), :] = flux_send[pl.ds((column // GROUP) * 4, 4), :]

    @pl.when(owner)
    def _():
        wait_for(part_recv, (PARTS - 1) * USED, part_rsem)

        level = []
        for k in range(SUBS):
            loads = tuple(
                part_recv[pl.ds(k * SLOT + j, SUBS, stride=SUBS * SLOT), :]
                + extra[pl.ds(k * LOADS + j, SUBS, stride=SUBS * LOADS), :]
                for j in range(LOADS)
            )
            rest = tuple(
                part_recv[pl.ds(k * SLOT + j, SUBS, stride=SUBS * SLOT), :]
                for j in range(LOADS, USED)
            )
            level.append(loads + rest)
        steps = []
        while len(level) > 1:
            joined = [climb(level[2 * m], level[2 * m + 1]) for m in range(len(level) // 2)]
            steps.append([item[1:] for item in joined])
            level = [item[0] for item in joined]
        fields = level[0]
        trail = []
        for shift in (1, 2, 4):
            raised = tuple(pltpu.roll(v, SUBS - shift, 0) for v in fields)
            fields, way, value = climb(fields, raised)
            trail.append((way, value, shift))
        f1, f2, _, _, ea1, ea2, sa, n11, n12, n21, n22, _, _, _ = fields
        i11, i12, i22 = inverse(sa, ea1 + (n11 + n12), ea2 + (n21 + n22))
        before = (i11 * f1 + i12 * f2, i12 * f1 + i22 * f2)
        after = (zero, zero)

        for way, value, shift in reversed(trail):
            inner = middle(way, value, before, after)
            first = (sub & shift) == 0
            before = tuple(
                jnp.where(first, b, pltpu.roll(v, shift, 0)) for b, v in zip(before, inner)
            )
            after = tuple(
                jnp.where(first, v, pltpu.roll(a, shift, 0)) for v, a in zip(inner, after)
            )
        nodes = [before, after]
        for step in reversed(steps):
            finer = []
            for m, (way, value) in enumerate(step):
                finer += [nodes[m], middle(way, value, nodes[m], nodes[m + 1])]
            nodes = finer + [nodes[-1]]
        for k in range(SUBS):
            for j, value in enumerate(nodes[k] + nodes[k + 1]):
                node_send[pl.ds(k * LOADS + j, SUBS, stride=SUBS * LOADS), :] = value

        def values_to(part):
            pltpu.make_async_remote_copy(
                src_ref=slot(node_send, part, LOADS, LOADS),
                dst_ref=slot(node_recv, column_row, LOADS, LOADS),
                send_sem=node_ssem,
                recv_sem=node_rsem,
                device_id={"solve": part},
                device_id_type=MESH,
            ).start()

        to_all(0, PARTS, values_to)
        here = pl.ds(pl.multiple_of(column_row * LOADS, LOADS), LOADS)
        there = pl.ds(pl.multiple_of(solve * LOADS, LOADS), LOADS)
        node_recv[here, :] = node_send[there, :]

    for i, column in enumerate((FIRST, LAST)):

        @pl.when(solve == column)
        def _():
            to_all(16, PARTS, flux_to(i))

    @pl.when(outer)
    def _():
        wait_for(flux_recv, 4, flux_rsem)

    @pl.when(jnp.logical_not(outer))
    def _():
        wait_for(flux_recv, 8, flux_rsem)

    flux = pltpu.roll(flux_recv[...], lax.rem(LANES - place * SUBS, LANES), 1)
    flux = jnp.concatenate([flux, jnp.zeros((LANES - SUBS, LANES), jnp.float32)], axis=0).T
    flux = flux[:SUBS]
    for i, (column, at) in enumerate(((0, 0), (SUBS - 1, LANES - 1))):
        for j in range(4):
            where = pl.ds((j * SUBS + column) * SUBS, SUBS)
            source[where, :] += jnp.where(lane == at, spin(flux, at - j - 4 * i), 0.0)
    _, owns = climb_loads()

    @pl.when(owner)
    def _():
        wait_for(node_recv, (OWNERS - 1) * LOADS, node_rsem)

    @pl.when(jnp.logical_not(owner))
    def _():
        wait_for(node_recv, OWNERS * LOADS, node_rsem)

    values = [node_recv[pl.ds(j, SUBS, stride=LOADS), :] for j in range(LOADS)]
    ends = [tuple(values[:2]), tuple(values[2:])]

    nodes = ends
    for back, own in zip(reversed(backs), reversed(owns)):
        finer = []
        for m in range(len(back)):
            finer += [nodes[m], middle(back[m], own[m], nodes[m], nodes[m + 1])]
        nodes = finer + [nodes[-1]]
    for i in range(ROWS):
        for plane in (0, 1):
            start = (plane * 2 + i // SUBS) * SUBS * SUBS + i % SUBS
            out_ref[pl.ds(start, SUBS, stride=SUBS), :] = nodes[i][plane]

    @pl.when(outer)
    def _():
        wait_for(edge_own, 3 * SUBS, edge_ssem)
        wait_for(node_send, (PARTS - 1) * 4, flux_ssem)

    @pl.when(jnp.logical_not(outer))
    def _():
        wait_for(edge_own, 4 * SUBS, edge_ssem)

    @pl.when(owner)
    def _():
        wait_for(part_send, (OWNERS - 1) * USED, part_ssem)
        wait_for(node_send, (PARTS - 1) * LOADS, node_ssem)

    @pl.when(jnp.logical_not(owner))
    def _():
        wait_for(part_send, OWNERS * USED, part_ssem)


def tiles(array):
    array = array.reshape(-1, ROWS // SUBS, SUBS, SUBS, LANES)
    return array.transpose(0, 1, 3, 2, 4).reshape(-1, LANES)


def per_device(temperature, transfer, diffusivity, exchange):
    vmem = lambda *shape: pltpu.VMEM(shape, jnp.float32)
    dma = pltpu.SemaphoreType.DMA
    out = pl.pallas_call(
        kernel,
        out_shape=jax.ShapeDtypeStruct((FLAT, LANES), jnp.float32),
        in_specs=[pl.BlockSpec(memory_space=pltpu.HBM)] * 4,
        out_specs=pl.BlockSpec(memory_space=pltpu.VMEM),
        scratch_shapes=[
            vmem(FLAT, LANES),
            vmem(FLAT, LANES),
            vmem(FLAT, LANES),
            vmem(FLAT // 2, LANES),
            vmem(FLAT, LANES),
            vmem(2 * SUBS, LANES),
            vmem(PARTS * SUBS, LANES),
            vmem(PARTS * SUBS, LANES),
            vmem(2 * SUBS, LANES),
            vmem(SUBS, LANES),
            vmem(LANES, LANES),
            vmem(5 * SUBS, LANES),
            vmem(OWNERS * SLOT, LANES),
            vmem(PARTS * SLOT, LANES),
            vmem(PARTS * LOADS, LANES),
            vmem(PARTS * LOADS, LANES),
            vmem(OWNERS * LOADS, LANES),
            dma((4,)),
            dma,
            dma,
            dma,
            dma,
            dma,
            dma,
            dma,
            dma,
            dma,
        ],
        compiler_params=pltpu.CompilerParams(
            collective_id=0, has_side_effects=True, vmem_limit_bytes=16 * 1024 * 1024
        ),
        cost_estimate=pl.CostEstimate(
            flops=4_000_000, bytes_accessed=600_000, transcendentals=0
        ),
        name="line_step",
    )(
        *(
            pltpu.with_memory_space_constraint(tiles(array), pltpu.HBM)
            for array in (temperature, transfer, diffusivity, exchange)
        )
    )
    out = out.reshape(2, ROWS // SUBS, SUBS, SUBS, LANES).transpose(0, 1, 3, 2, 4)
    return out.reshape(2, ROWS, SUBS * LANES)


def solution(mesh):
    specs = (P(None, "solve", "cross"),) * 3 + (P("solve", "cross"),)
    return jax.shard_map(
        per_device,
        mesh=mesh,
        in_specs=specs,
        out_specs=P(None, "solve", "cross"),
        check_vma=False,
    )
```

```python
import jax
import jax.numpy as jnp
from jax import lax
from jax.experimental import pallas as pl
from jax.experimental.pallas import tpu as pltpu
from jax.sharding import PartitionSpec as P

MESH = pl.DeviceIdType.MESH
ROWS, SUBS, LANES = 16, 8, 128
GROUP, OWNERS, PARTS = 16, 8, 64
FIRST, LAST = 0, 49
LOADS, USED, SLOT = 4, 14, 16
FLAT = 2 * ROWS * SUBS


def inverse(coupling, first, second):
    scale = 1.0 / (coupling * (first + second) + first * second)
    return (coupling + second) * scale, coupling * scale, (coupling + first) * scale


def merge(left, right):
    ea1, ea2, sa, n11, n12, n21, n22, ec1, ec2, sc = left
    fa1, fa2, fs, m11, m12, m21, m22, fc1, fc2, gs = right
    eb1, eb2, sb = ec1 + fa1, ec2 + fa2, sc + fs
    r1 = eb1 + ((n11 + n21) + (m11 + m12))
    r2 = eb2 + ((n12 + n22) + (m21 + m22))
    i11, i12, i22 = inverse(sb, r1, r2)
    g11, g12 = n11 * i11 + n12 * i12, n11 * i12 + n12 * i22
    g21, g22 = n21 * i11 + n22 * i12, n21 * i12 + n22 * i22
    h11, h12 = i11 * m11 + i12 * m21, i11 * m12 + i12 * m22
    h21, h22 = i12 * m11 + i22 * m21, i12 * m12 + i22 * m22
    joined = (
        ea1 + (g11 * eb1 + g12 * eb2),
        ea2 + (g21 * eb1 + g22 * eb2),
        sa + (g11 * n21 + g12 * n22),
        g11 * m11 + g12 * m21,
        g11 * m12 + g12 * m22,
        g21 * m11 + g22 * m21,
        g21 * m12 + g22 * m22,
        fc1 + (h11 * eb1 + h21 * eb2),
        fc2 + (h12 * eb1 + h22 * eb2),
        gs + (m11 * h12 + m21 * h22),
    )
    return joined, (i11, i12, i22, g11, g12, g21, g22, h11, h12, h21, h22)


def merge_leaf(sa, sb, n1, n2, m1, m2):
    r1, r2 = 1.0 + (n1 + m1), 1.0 + (n2 + m2)
    i11, i12, i22 = inverse(sb, r1, r2)
    g11, g12, g21, g22 = n1 * i11, n1 * i12, n2 * i12, n2 * i22
    h11, h12, h21, h22 = i11 * m1, i12 * m2, i12 * m1, i22 * m2
    joined = (
        1.0 + (g11 + g12),
        1.0 + (g21 + g22),
        sa + g12 * n2,
        g11 * m1,
        g12 * m2,
        g21 * m1,
        g22 * m2,
        h11 + h21,
        h12 + h22,
        m1 * h12,
    )
    return joined, (i11, i12, i22, g11, g12, g21, g22, h11, h12, h21, h22)


def merge_loads(back, left, right):
    i11, i12, i22, g11, g12, g21, g22, h11, h12, h21, h22 = back
    a1, a2, b1, b2 = left
    c1, c2, d1, d2 = right
    b1, b2 = b1 + c1, b2 + c2
    loads = (
        a1 + (g11 * b1 + g12 * b2),
        a2 + (g21 * b1 + g22 * b2),
        d1 + (h11 * b1 + h21 * b2),
        d2 + (h12 * b1 + h22 * b2),
    )
    return loads, (i11 * b1 + i12 * b2, i12 * b1 + i22 * b2)


def merge_leaf_loads(back, a, b):
    i11, i12, i22, g11, g12, g21, g22, h11, h12, h21, h22 = back
    a1, a2 = a
    b1, b2 = b
    loads = (
        a1 + (g11 * b1 + g12 * b2),
        a2 + (g21 * b1 + g22 * b2),
        h11 * b1 + h21 * b2,
        h12 * b1 + h22 * b2,
    )
    return loads, (i11 * b1 + i12 * b2, i12 * b1 + i22 * b2)


def middle(back, own, before, after):
    g11, g12, g21, g22, h11, h12, h21, h22 = back[3:]
    a1, a2 = before
    c1, c2 = after
    return (
        own[0] + ((g11 * a1 + g21 * a2) + (h11 * c1 + h12 * c2)),
        own[1] + ((g12 * a1 + g22 * a2) + (h21 * c1 + h22 * c2)),
    )


def kernel(
    temp_hbm,
    face_hbm,
    diff_hbm,
    sheet_hbm,
    out_ref,
    temp,
    face,
    diff,
    sheet,
    source,
    edge_send,
    edge_own,
    edge_far,
    flux_send,
    flux_recv,
    part_send,
    part_recv,
    extra,
    node_send,
    node_recv,
    in_sem,
    edge_ssem,
    own_rsem,
    far_rsem,
    flux_ssem,
    flux_rsem,
    part_ssem,
    part_rsem,
    node_ssem,
    node_rsem,
):
    solve = lax.axis_index("solve")
    cross = lax.axis_index("cross")
    n_cross = lax.axis_size("cross")
    place = lax.rem(solve, GROUP)
    group = lax.div(solve, GROUP)

    loads_in = [
        pltpu.make_async_copy(src, dst, in_sem.at[i])
        for i, (src, dst) in enumerate(
            ((temp_hbm, temp), (diff_hbm, diff), (face_hbm, face), (sheet_hbm, sheet))
        )
    ]
    for copy in loads_in:
        copy.start()

    owner = place < 2
    column_row = group * 2 + place
    outer = (solve == FIRST) | (solve == LAST)
    rows_of = [lax.rem(solve + step, OWNERS) for step in range(OWNERS)]

    def device_of(index):
        return lax.div(index, 2) * GROUP + lax.rem(index, 2)

    right = lax.rem(cross + 1, n_cross)
    left = lax.rem(cross + n_cross - 1, n_cross)

    barrier = pltpu.get_barrier_semaphore()
    for column, side in ((FIRST, left), (LAST, right)):

        @pl.when(solve == column)
        def _():
            def greet(index, _):
                pl.semaphore_signal(
                    barrier,
                    1,
                    device_id={"solve": index, "cross": side},
                    device_id_type=MESH,
                )
                return 0

            lax.fori_loop(0, PARTS, greet, 0)

    @pl.when(owner)
    def _():
        def greet(step, _):
            pl.semaphore_signal(
                barrier,
                1,
                device_id={"solve": lax.rem(solve + step, PARTS)},
                device_id_type=MESH,
            )
            return 0

        lax.fori_loop(1, PARTS, greet, 0)
        extra[...] = jnp.zeros((PARTS * LOADS, LANES), jnp.float32)

    lane = lax.broadcasted_iota(jnp.int32, (SUBS, LANES), 1)
    sub = lax.broadcasted_iota(jnp.int32, (SUBS, LANES), 0)

    zero = jnp.zeros((SUBS, LANES), jnp.float32)

    def spin(value, shift):
        return pltpu.roll(value, shift % LANES, 1)

    def tile(ref, block, column):
        return ref[pl.ds((block * SUBS + column) * SUBS, SUBS), :]

    def slot(ref, index, rows, used):
        start = index * rows if isinstance(index, int) else pl.multiple_of(index * rows, rows)
        return ref.at[pl.ds(start, used)]

    for copy in loads_in:
        copy.wait()
    tracks = [(ref, j) for ref in (temp, diff, face) for j in range(4)]
    tracks += [(sheet, 0), (sheet, 1)]
    for i, (column, shift) in enumerate(((0, 0), (SUBS - 1, 1))):
        packed = jnp.zeros((SUBS, LANES), jnp.float32)
        for j, (ref, block) in enumerate(tracks):
            at = j * SUBS
            packed = jnp.where(lane == at, spin(tile(ref, block, column), at + shift), packed)
        for step in (1, 2, 4):
            packed = packed + spin(pltpu.roll(packed, SUBS - step, 0), step)
        edge_send[pl.ds(i, 1), :] = packed[0:1, :]
    flux_recv[pl.ds(4, 4), :] = zero[0:4, :]

    @pl.when(owner)
    def _():
        pl.semaphore_wait(barrier, 2 + OWNERS - 1)

    @pl.when(jnp.logical_not(owner))
    def _():
        pl.semaphore_wait(barrier, 2 + OWNERS)

    for i, (mine, theirs, side) in enumerate(
        ((FIRST, LAST, left), (LAST, FIRST, right))
    ):
        edge = edge_send.at[pl.ds(i, 1)]
        pltpu.make_async_remote_copy(
            src_ref=edge,
            dst_ref=slot(edge_far, solve, 1, 1),
            send_sem=edge_ssem,
            recv_sem=far_rsem,
            device_id={"solve": theirs, "cross": side},
            device_id_type=MESH,
        ).start()

        @pl.when(solve != mine)
        def _():
            pltpu.make_async_remote_copy(
                src_ref=edge,
                dst_ref=slot(edge_own, solve, 1, 1),
                send_sem=edge_ssem,
                recv_sem=own_rsem,
                device_id={"solve": mine},
                device_id_type=MESH,
            ).start()

        @pl.when(solve == mine)
        def _():
            edge_own[pl.ds(mine, 1), :] = edge_send[pl.ds(i, 1), :]

    for block in range(4):
        heat = [tile(temp, block, t) for t in range(SUBS)]
        cond = [tile(diff, block, t) for t in range(SUBS)]
        heat_turned = [spin(v, -1) for v in heat] + [zero]
        cond_turned = [spin(v, -1) for v in cond] + [zero]
        last = lane == LANES - 1
        before = zero
        for t in range(SUBS):
            next_heat = jnp.where(last, heat_turned[t + 1], heat_turned[t])
            next_cond = jnp.where(last, cond_turned[t + 1], cond_turned[t])
            flux = 0.5 * (cond[t] + next_cond) * (next_heat - heat[t])
            if t == SUBS - 1:
                flux = jnp.where(last, 0.0, flux)
            turned = spin(flux, 1)
            previous = jnp.where(lane == 0, before, turned)
            before = turned
            source[pl.ds((block * SUBS + t) * SUBS, SUBS), :] = heat[t] + flux - previous

    def row(ref, plane, i):
        start = (plane * 2 + i // SUBS) * SUBS * SUBS + i % SUBS
        return ref[pl.ds(start, SUBS, stride=SUBS), :]

    backs = []
    level = []
    back = []
    for m in range(ROWS // 2):
        element, way = merge_leaf(
            row(sheet, 0, 2 * m),
            row(sheet, 0, 2 * m + 1),
            row(face, 0, 2 * m),
            row(face, 1, 2 * m),
            row(face, 0, 2 * m + 1),
            row(face, 1, 2 * m + 1),
        )
        level.append(element)
        back.append(way)
    backs.append(back)
    while len(level) > 1:
        pairs = [merge(level[2 * m], level[2 * m + 1]) for m in range(len(level) // 2)]
        level = [pair[0] for pair in pairs]
        backs.append([pair[1] for pair in pairs])
    element = level[0]

    def climb_loads():
        owns = []
        level = []
        own = []
        for m in range(ROWS // 2):
            loads, value = merge_leaf_loads(
                backs[0][m],
                (row(source, 0, 2 * m), row(source, 1, 2 * m)),
                (row(source, 0, 2 * m + 1), row(source, 1, 2 * m + 1)),
            )
            level.append(loads)
            own.append(value)
        owns.append(own)
        for back in backs[1:]:
            pairs = [
                merge_loads(back[m], level[2 * m], level[2 * m + 1]) for m in range(len(back))
            ]
            level = [pair[0] for pair in pairs]
            owns.append([pair[1] for pair in pairs])
        return level[0], owns

    loads, _ = climb_loads()
    for j, value in enumerate(loads + element):
        part_send[pl.ds(j, SUBS, stride=SLOT), :] = value

    for index in rows_of:

        @pl.when(device_of(index) != solve)
        def _():
            pltpu.make_async_remote_copy(
                src_ref=slot(part_send, index, SLOT, USED),
                dst_ref=slot(part_recv, solve, SLOT, USED),
                send_sem=part_ssem,
                recv_sem=part_rsem,
                device_id={"solve": device_of(index)},
                device_id_type=MESH,
            ).start()

    @pl.when(owner)
    def _():
        here = pl.ds(pl.multiple_of(solve * SLOT, SLOT), USED)
        there = pl.ds(pl.multiple_of(column_row * SLOT, SLOT), USED)
        part_recv[here, :] = part_send[there, :]

    def climb(left_fields, right_fields):
        element, way = merge(left_fields[LOADS:], right_fields[LOADS:])
        loads, value = merge_loads(way, left_fields[:LOADS], right_fields[:LOADS])
        return loads + element, way, value

    def wait_for(ref, rows, sem):
        part = ref.at[pl.ds(0, rows)]
        pltpu.make_async_copy(part, part, sem).wait()

    def to_all(first, last, send):
        def one(n, _):
            part = lax.rem(lax.div(n, 2), 4) * GROUP + lax.div(n, 8) * 2 + lax.rem(n, 2)

            @pl.when(part != solve)
            def _():
                send(part)

            return 0

        lax.fori_loop(first, last, one, 0)

    def flux_to(i):
        def send(part):
            pltpu.make_async_remote_copy(
                src_ref=slot(flux_send, lax.rem(part, SUBS), 2, 2),
                dst_ref=flux_recv.at[pl.ds(i * 2, 2)],
                send_sem=flux_ssem,
                recv_sem=flux_rsem,
                device_id={"solve": part},
                device_id_type=MESH,
            ).start()

        return send

    def along(ref, at, inside=None):
        value = zero
        for a in range(SUBS):
            part = spin(ref[pl.ds(a * SUBS, SUBS), :], a * ROWS - at)
            value = jnp.where(lax.div(lane, ROWS) == a, part, value)
        return value if inside is None else jnp.where(inside, value, 0.0)

    for i, (column, at, inside) in enumerate(
        ((FIRST, 0, cross > 0), (LAST, LANES - 1, cross < n_cross - 1))
    ):

        @pl.when(solve == column)
        def _():
            wait_for(edge_own, PARTS - 1, own_rsem)
            wait_for(edge_far, PARTS, far_rsem)
            sides = []
            for plane in (0, 1):
                warm, cond = plane * ROWS, (2 + plane) * ROWS
                total = along(edge_own, cond) + along(edge_far, cond, inside)
                step = along(edge_far, warm, inside) - along(edge_own, warm)
                sides.append(0.5 * total * step)
                flux_send[pl.ds(plane, SUBS, stride=2), :] = sides[plane]
            first1, first2, second = (along(edge_own, f * ROWS) for f in (4, 5, 6))
            element, way = merge_leaf(
                second, spin(second, -1), first1, first2, spin(first1, -1), spin(first2, -1)
            )
            loads, _ = merge_leaf_loads(way, sides, [spin(v, -1) for v in sides])
            fields = loads + element
            for shift in (2, 4, 8):
                fields, _, _ = climb(fields, tuple(spin(v, -shift) for v in fields))
            for a in range(SUBS):
                for j in range(LOADS):
                    at_rows = pl.ds(a * SUBS * LOADS + j, SUBS, stride=LOADS)
                    moved = spin(fields[j], at - a * ROWS)
                    extra[at_rows, :] = jnp.where(lane == at, moved, 0.0)
            to_all(0, 16, flux_to(i))
            flux_recv[pl.ds(i * 2, 2), :] = flux_send[pl.ds((column % SUBS) * 2, 2), :]

    @pl.when(owner)
    def _():
        wait_for(part_recv, (PARTS - 1) * USED, part_rsem)

        level = []
        for k in range(SUBS):
            loads = tuple(
                part_recv[pl.ds(k * SLOT + j, SUBS, stride=SUBS * SLOT), :]
                + extra[pl.ds(k * LOADS + j, SUBS, stride=SUBS * LOADS), :]
                for j in range(LOADS)
            )
            rest = tuple(
                part_recv[pl.ds(k * SLOT + j, SUBS, stride=SUBS * SLOT), :]
                for j in range(LOADS, USED)
            )
            level.append(loads + rest)
        steps = []
        while len(level) > 1:
            joined = [climb(level[2 * m], level[2 * m + 1]) for m in range(len(level) // 2)]
            steps.append([item[1:] for item in joined])
            level = [item[0] for item in joined]
        fields = level[0]
        trail = []
        for shift in (1, 2, 4):
            raised = tuple(pltpu.roll(v, SUBS - shift, 0) for v in fields)
            fields, way, value = climb(fields, raised)
            trail.append((way, value, shift))
        f1, f2, _, _, ea1, ea2, sa, n11, n12, n21, n22, _, _, _ = fields
        i11, i12, i22 = inverse(sa, ea1 + (n11 + n12), ea2 + (n21 + n22))
        before = (i11 * f1 + i12 * f2, i12 * f1 + i22 * f2)
        after = (zero, zero)

        for way, value, shift in reversed(trail):
            inner = middle(way, value, before, after)
            first = (sub & shift) == 0
            before = tuple(
                jnp.where(first, b, pltpu.roll(v, shift, 0)) for b, v in zip(before, inner)
            )
            after = tuple(
                jnp.where(first, v, pltpu.roll(a, shift, 0)) for v, a in zip(inner, after)
            )
        nodes = [before, after]
        for step in reversed(steps):
            finer = []
            for m, (way, value) in enumerate(step):
                finer += [nodes[m], middle(way, value, nodes[m], nodes[m + 1])]
            nodes = finer + [nodes[-1]]
        for k in range(SUBS):
            for j, value in enumerate(nodes[k] + nodes[k + 1]):
                node_send[pl.ds(k * LOADS + j, SUBS, stride=SUBS * LOADS), :] = value

        def values_to(part):
            pltpu.make_async_remote_copy(
                src_ref=slot(node_send, part, LOADS, LOADS),
                dst_ref=slot(node_recv, column_row, LOADS, LOADS),
                send_sem=node_ssem,
                recv_sem=node_rsem,
                device_id={"solve": part},
                device_id_type=MESH,
            ).start()

        to_all(0, PARTS, values_to)
        here = pl.ds(pl.multiple_of(column_row * LOADS, LOADS), LOADS)
        there = pl.ds(pl.multiple_of(solve * LOADS, LOADS), LOADS)
        node_recv[here, :] = node_send[there, :]

    for i, column in enumerate((FIRST, LAST)):

        @pl.when(solve == column)
        def _():
            to_all(16, PARTS, flux_to(i))

    @pl.when(outer)
    def _():
        wait_for(flux_recv, 2, flux_rsem)

    @pl.when(jnp.logical_not(outer))
    def _():
        wait_for(flux_recv, 4, flux_rsem)

    shift = lax.rem(LANES - lax.div(solve, SUBS) * ROWS, LANES)
    flux = pltpu.roll(flux_recv[...], shift, 1)
    flux = jnp.concatenate([flux, jnp.zeros((LANES - SUBS, LANES), jnp.float32)], axis=0).T
    for i, (column, at) in enumerate(((0, 0), (SUBS - 1, LANES - 1))):
        for j in range(4):
            where = pl.ds((j * SUBS + column) * SUBS, SUBS)
            part = flux[(j % 2) * SUBS : (j % 2 + 1) * SUBS]
            moved = spin(part, at - 2 * i - j // 2)
            source[where, :] += jnp.where(lane == at, moved, 0.0)
    _, owns = climb_loads()

    @pl.when(owner)
    def _():
        wait_for(node_recv, (OWNERS - 1) * LOADS, node_rsem)

    @pl.when(jnp.logical_not(owner))
    def _():
        wait_for(node_recv, OWNERS * LOADS, node_rsem)

    values = [node_recv[pl.ds(j, SUBS, stride=LOADS), :] for j in range(LOADS)]
    ends = [tuple(values[:2]), tuple(values[2:])]

    nodes = ends
    for back, own in zip(reversed(backs), reversed(owns)):
        finer = []
        for m in range(len(back)):
            finer += [nodes[m], middle(back[m], own[m], nodes[m], nodes[m + 1])]
        nodes = finer + [nodes[-1]]
    for i in range(ROWS):
        for plane in (0, 1):
            start = (plane * 2 + i // SUBS) * SUBS * SUBS + i % SUBS
            out_ref[pl.ds(start, SUBS, stride=SUBS), :] = nodes[i][plane]

    @pl.when(outer)
    def _():
        wait_for(edge_own, 3, edge_ssem)
        wait_for(node_send, (PARTS - 1) * 2, flux_ssem)

    @pl.when(jnp.logical_not(outer))
    def _():
        wait_for(edge_own, 4, edge_ssem)

    @pl.when(owner)
    def _():
        wait_for(part_send, (OWNERS - 1) * USED, part_ssem)
        wait_for(node_send, (PARTS - 1) * LOADS, node_ssem)

    @pl.when(jnp.logical_not(owner))
    def _():
        wait_for(part_send, OWNERS * USED, part_ssem)


def tiles(array):
    array = array.reshape(-1, ROWS // SUBS, SUBS, SUBS, LANES)
    return array.transpose(0, 1, 3, 2, 4).reshape(-1, LANES)


def per_device(temperature, transfer, diffusivity, exchange):
    vmem = lambda *shape: pltpu.VMEM(shape, jnp.float32)
    dma = pltpu.SemaphoreType.DMA
    out = pl.pallas_call(
        kernel,
        out_shape=jax.ShapeDtypeStruct((FLAT, LANES), jnp.float32),
        in_specs=[pl.BlockSpec(memory_space=pltpu.HBM)] * 4,
        out_specs=pl.BlockSpec(memory_space=pltpu.VMEM),
        scratch_shapes=[
            vmem(FLAT, LANES),
            vmem(FLAT, LANES),
            vmem(FLAT, LANES),
            vmem(FLAT // 2, LANES),
            vmem(FLAT, LANES),
            vmem(SUBS, LANES),
            vmem(PARTS, LANES),
            vmem(PARTS, LANES),
            vmem(2 * SUBS, LANES),
            vmem(SUBS, LANES),
            vmem(OWNERS * SLOT, LANES),
            vmem(PARTS * SLOT, LANES),
            vmem(PARTS * LOADS, LANES),
            vmem(PARTS * LOADS, LANES),
            vmem(OWNERS * LOADS, LANES),
            dma((4,)),
            dma,
            dma,
            dma,
            dma,
            dma,
            dma,
            dma,
            dma,
            dma,
        ],
        compiler_params=pltpu.CompilerParams(
            collective_id=0, has_side_effects=True, vmem_limit_bytes=16 * 1024 * 1024
        ),
        cost_estimate=pl.CostEstimate(
            flops=4_000_000, bytes_accessed=600_000, transcendentals=0
        ),
        name="line_step",
    )(
        *(
            pltpu.with_memory_space_constraint(tiles(array), pltpu.HBM)
            for array in (temperature, transfer, diffusivity, exchange)
        )
    )
    out = out.reshape(2, ROWS // SUBS, SUBS, SUBS, LANES).transpose(0, 1, 3, 2, 4)
    return out.reshape(2, ROWS, SUBS * LANES)


def solution(mesh):
    specs = (P(None, "solve", "cross"),) * 3 + (P("solve", "cross"),)
    return jax.shard_map(
        per_device,
        mesh=mesh,
        in_specs=specs,
        out_specs=P(None, "solve", "cross"),
        check_vma=False,
    )
```

```python
import functools

import jax
import jax.numpy as jnp
from jax import lax
from jax.experimental import pallas as pl
from jax.experimental.pallas import tpu as pltpu
from jax.sharding import PartitionSpec as P

MESH = pl.DeviceIdType.MESH
ROWS, SUBS, LANES = 16, 8, 128
GROUP, OWNERS, PARTS = 16, 8, 64
FIRST, LAST = 0, 49
LOADS, USED, SLOT = 4, 14, 16
FLAT = 2 * ROWS * SUBS


def inverse(coupling, first, second):
    scale = 1.0 / (coupling * (first + second) + first * second)
    return (coupling + second) * scale, coupling * scale, (coupling + first) * scale


def merge(left, right):
    ea1, ea2, sa, n11, n12, n21, n22, ec1, ec2, sc = left
    fa1, fa2, fs, m11, m12, m21, m22, fc1, fc2, gs = right
    eb1, eb2, sb = ec1 + fa1, ec2 + fa2, sc + fs
    r1 = eb1 + ((n11 + n21) + (m11 + m12))
    r2 = eb2 + ((n12 + n22) + (m21 + m22))
    i11, i12, i22 = inverse(sb, r1, r2)
    g11, g12 = n11 * i11 + n12 * i12, n11 * i12 + n12 * i22
    g21, g22 = n21 * i11 + n22 * i12, n21 * i12 + n22 * i22
    h11, h12 = i11 * m11 + i12 * m21, i11 * m12 + i12 * m22
    h21, h22 = i12 * m11 + i22 * m21, i12 * m12 + i22 * m22
    joined = (
        ea1 + (g11 * eb1 + g12 * eb2),
        ea2 + (g21 * eb1 + g22 * eb2),
        sa + (g11 * n21 + g12 * n22),
        g11 * m11 + g12 * m21,
        g11 * m12 + g12 * m22,
        g21 * m11 + g22 * m21,
        g21 * m12 + g22 * m22,
        fc1 + (h11 * eb1 + h21 * eb2),
        fc2 + (h12 * eb1 + h22 * eb2),
        gs + (m11 * h12 + m21 * h22),
    )
    return joined, (i11, i12, i22, g11, g12, g21, g22, h11, h12, h21, h22)


def merge_leaf(sa, sb, n1, n2, m1, m2):
    r1, r2 = 1.0 + (n1 + m1), 1.0 + (n2 + m2)
    i11, i12, i22 = inverse(sb, r1, r2)
    g11, g12, g21, g22 = n1 * i11, n1 * i12, n2 * i12, n2 * i22
    h11, h12, h21, h22 = i11 * m1, i12 * m2, i12 * m1, i22 * m2
    joined = (
        1.0 + (g11 + g12),
        1.0 + (g21 + g22),
        sa + g12 * n2,
        g11 * m1,
        g12 * m2,
        g21 * m1,
        g22 * m2,
        h11 + h21,
        h12 + h22,
        m1 * h12,
    )
    return joined, (i11, i12, i22, g11, g12, g21, g22, h11, h12, h21, h22)


def merge_loads(back, left, right):
    i11, i12, i22, g11, g12, g21, g22, h11, h12, h21, h22 = back
    a1, a2, b1, b2 = left
    c1, c2, d1, d2 = right
    b1, b2 = b1 + c1, b2 + c2
    loads = (
        a1 + (g11 * b1 + g12 * b2),
        a2 + (g21 * b1 + g22 * b2),
        d1 + (h11 * b1 + h21 * b2),
        d2 + (h12 * b1 + h22 * b2),
    )
    return loads, (i11 * b1 + i12 * b2, i12 * b1 + i22 * b2)


def merge_leaf_loads(back, a, b):
    i11, i12, i22, g11, g12, g21, g22, h11, h12, h21, h22 = back
    a1, a2 = a
    b1, b2 = b
    loads = (
        a1 + (g11 * b1 + g12 * b2),
        a2 + (g21 * b1 + g22 * b2),
        h11 * b1 + h21 * b2,
        h12 * b1 + h22 * b2,
    )
    return loads, (i11 * b1 + i12 * b2, i12 * b1 + i22 * b2)


def middle(back, own, before, after):
    g11, g12, g21, g22, h11, h12, h21, h22 = back[3:]
    a1, a2 = before
    c1, c2 = after
    return (
        own[0] + ((g11 * a1 + g21 * a2) + (h11 * c1 + h12 * c2)),
        own[1] + ((g12 * a1 + g22 * a2) + (h21 * c1 + h22 * c2)),
    )


def kernel(
    temp_hbm,
    face_hbm,
    diff_hbm,
    sheet_hbm,
    out_ref,
    temp,
    face,
    diff,
    sheet,
    source,
    edge_send,
    edge_own,
    edge_far,
    flux_send,
    flux_recv,
    part_send,
    late_send,
    part_recv,
    extra,
    node_send,
    node_recv,
    in_sem,
    edge_ssem,
    own_rsem,
    far_rsem,
    flux_ssem,
    flux_rsem,
    part_ssem,
    part_rsem,
    node_ssem,
    node_rsem,
):
    solve = lax.axis_index("solve")
    cross = lax.axis_index("cross")
    n_cross = lax.axis_size("cross")
    place = lax.rem(solve, GROUP)
    group = lax.div(solve, GROUP)

    loads_in = [
        pltpu.make_async_copy(src, dst, in_sem.at[i])
        for i, (src, dst) in enumerate(
            ((temp_hbm, temp), (diff_hbm, diff), (face_hbm, face), (sheet_hbm, sheet))
        )
    ]
    for copy in loads_in:
        copy.start()

    owner = place < 2
    column_row = group * 2 + place
    outer = (solve == FIRST) | (solve == LAST)
    rows_of = [lax.rem(solve + step, OWNERS) for step in range(OWNERS)]

    def device_of(index):
        return lax.div(index, 2) * GROUP + lax.rem(index, 2)

    right = lax.rem(cross + 1, n_cross)
    left = lax.rem(cross + n_cross - 1, n_cross)

    barrier = pltpu.get_barrier_semaphore()
    for column, side in ((FIRST, left), (LAST, right)):

        @pl.when(solve == column)
        def _():
            def greet(index, _):
                pl.semaphore_signal(
                    barrier,
                    1,
                    device_id={"solve": index, "cross": side},
                    device_id_type=MESH,
                )
                return 0

            lax.fori_loop(0, PARTS, greet, 0)

    @pl.when(owner)
    def _():
        def greet(step, _):
            pl.semaphore_signal(
                barrier,
                1,
                device_id={"solve": lax.rem(solve + step, PARTS)},
                device_id_type=MESH,
            )
            return 0

        lax.fori_loop(1, PARTS, greet, 0)
        extra[...] = jnp.zeros((PARTS * LOADS, LANES), jnp.float32)

    lane = lax.broadcasted_iota(jnp.int32, (SUBS, LANES), 1)
    sub = lax.broadcasted_iota(jnp.int32, (SUBS, LANES), 0)

    zero = jnp.zeros((SUBS, LANES), jnp.float32)

    def spin(value, shift):
        return pltpu.roll(value, shift % LANES, 1)

    def tile(ref, block, column):
        return ref[pl.ds((block * SUBS + column) * SUBS, SUBS), :]

    def slot(ref, index, rows, used):
        start = index * rows if isinstance(index, int) else pl.multiple_of(index * rows, rows)
        return ref.at[pl.ds(start, used)]

    for copy in loads_in:
        copy.wait()
    tracks = [(ref, j) for ref in (temp, diff, face) for j in range(4)]
    tracks += [(sheet, 0), (sheet, 1)]
    for i, (column, shift) in enumerate(((0, 0), (SUBS - 1, 1))):
        packed = jnp.zeros((SUBS, LANES), jnp.float32)
        for j, (ref, block) in enumerate(tracks):
            at = j * SUBS
            packed = jnp.where(lane == at, spin(tile(ref, block, column), at + shift), packed)
        for step in (1, 2, 4):
            packed = packed + spin(pltpu.roll(packed, SUBS - step, 0), step)
        edge_send[pl.ds(i, 1), :] = packed[0:1, :]
    flux_recv[pl.ds(4, 4), :] = zero[0:4, :]

    @pl.when(owner)
    def _():
        pl.semaphore_wait(barrier, 2 + OWNERS - 1)

    @pl.when(jnp.logical_not(owner))
    def _():
        pl.semaphore_wait(barrier, 2 + OWNERS)

    for i, (mine, theirs, side) in enumerate(
        ((FIRST, LAST, left), (LAST, FIRST, right))
    ):
        edge = edge_send.at[pl.ds(i, 1)]
        pltpu.make_async_remote_copy(
            src_ref=edge,
            dst_ref=slot(edge_far, solve, 1, 1),
            send_sem=edge_ssem,
            recv_sem=far_rsem,
            device_id={"solve": theirs, "cross": side},
            device_id_type=MESH,
        ).start()

        @pl.when(solve != mine)
        def _():
            pltpu.make_async_remote_copy(
                src_ref=edge,
                dst_ref=slot(edge_own, solve, 1, 1),
                send_sem=edge_ssem,
                recv_sem=own_rsem,
                device_id={"solve": mine},
                device_id_type=MESH,
            ).start()

        @pl.when(solve == mine)
        def _():
            edge_own[pl.ds(mine, 1), :] = edge_send[pl.ds(i, 1), :]

    def row(ref, plane, i):
        start = (plane * 2 + i // SUBS) * SUBS * SUBS + i % SUBS
        return ref[pl.ds(start, SUBS, stride=SUBS), :]

    backs = []
    level = []
    back = []
    for m in range(ROWS // 2):
        element, way = merge_leaf(
            row(sheet, 0, 2 * m),
            row(sheet, 0, 2 * m + 1),
            row(face, 0, 2 * m),
            row(face, 1, 2 * m),
            row(face, 0, 2 * m + 1),
            row(face, 1, 2 * m + 1),
        )
        level.append(element)
        back.append(way)
    backs.append(back)
    while len(level) > 1:
        pairs = [merge(level[2 * m], level[2 * m + 1]) for m in range(len(level) // 2)]
        level = [pair[0] for pair in pairs]
        backs.append([pair[1] for pair in pairs])
    element = level[0]

    def send_parts(ref, slot_rows, skip, rows):
        def rows_at(ref, slot_rows, index):
            start = pl.multiple_of(index * slot_rows, slot_rows) + skip % slot_rows
            return ref.at[pl.ds(start, rows)]

        for index in rows_of:

            @pl.when(device_of(index) != solve)
            def _():
                pltpu.make_async_remote_copy(
                    src_ref=rows_at(ref, slot_rows, index),
                    dst_ref=rows_at(part_recv, SLOT, solve),
                    send_sem=part_ssem,
                    recv_sem=part_rsem,
                    device_id={"solve": device_of(index)},
                    device_id_type=MESH,
                ).start()

    for j, value in enumerate(element):
        part_send[pl.ds(LOADS + j, SUBS, stride=SLOT), :] = value
    send_parts(part_send, SLOT, LOADS, USED - LOADS)

    for block in range(4):
        heat = [tile(temp, block, t) for t in range(SUBS)]
        cond = [tile(diff, block, t) for t in range(SUBS)]
        heat_turned = [spin(v, -1) for v in heat] + [zero]
        cond_turned = [spin(v, -1) for v in cond] + [zero]
        last = lane == LANES - 1
        before = zero
        for t in range(SUBS):
            next_heat = jnp.where(last, heat_turned[t + 1], heat_turned[t])
            next_cond = jnp.where(last, cond_turned[t + 1], cond_turned[t])
            flux = 0.5 * (cond[t] + next_cond) * (next_heat - heat[t])
            if t == SUBS - 1:
                flux = jnp.where(last, 0.0, flux)
            turned = spin(flux, 1)
            previous = jnp.where(lane == 0, before, turned)
            before = turned
            source[pl.ds((block * SUBS + t) * SUBS, SUBS), :] = heat[t] + flux - previous


    def climb_loads():
        owns = []
        level = []
        own = []
        for m in range(ROWS // 2):
            loads, value = merge_leaf_loads(
                backs[0][m],
                (row(source, 0, 2 * m), row(source, 1, 2 * m)),
                (row(source, 0, 2 * m + 1), row(source, 1, 2 * m + 1)),
            )
            level.append(loads)
            own.append(value)
        owns.append(own)
        for back in backs[1:]:
            pairs = [
                merge_loads(back[m], level[2 * m], level[2 * m + 1]) for m in range(len(back))
            ]
            level = [pair[0] for pair in pairs]
            owns.append([pair[1] for pair in pairs])
        return level[0], owns

    loads, _ = climb_loads()
    for j, value in enumerate(loads):
        late_send[pl.ds(j, SUBS, stride=LOADS), :] = value

    send_parts(late_send, LOADS, 0, LOADS)

    @pl.when(owner)
    def _():
        here = pl.multiple_of(solve * SLOT, SLOT)
        there = pl.multiple_of(column_row * SLOT, SLOT) + LOADS
        late = pl.ds(pl.multiple_of(column_row * LOADS, LOADS), LOADS)
        part_recv[pl.ds(here, LOADS), :] = late_send[late, :]
        part_recv[pl.ds(here + LOADS, USED - LOADS), :] = part_send[
            pl.ds(there, USED - LOADS), :
        ]

    def climb(left_fields, right_fields):
        element, way = merge(left_fields[LOADS:], right_fields[LOADS:])
        loads, value = merge_loads(way, left_fields[:LOADS], right_fields[:LOADS])
        return loads + element, way, value

    def wait_for(ref, rows, sem):
        part = ref.at[pl.ds(0, rows)]
        pltpu.make_async_copy(part, part, sem).wait()

    def to_all(first, last, send):
        def one(n, _):
            part = lax.rem(lax.div(n, 2), 4) * GROUP + lax.div(n, 8) * 2 + lax.rem(n, 2)

            @pl.when(part != solve)
            def _():
                send(part)

            return 0

        lax.fori_loop(first, last, one, 0)

    def flux_to(i):
        def send(part):
            pltpu.make_async_remote_copy(
                src_ref=slot(flux_send, lax.rem(part, SUBS), 2, 2),
                dst_ref=flux_recv.at[pl.ds(i * 2, 2)],
                send_sem=flux_ssem,
                recv_sem=flux_rsem,
                device_id={"solve": part},
                device_id_type=MESH,
            ).start()

        return send

    def along(ref, at, inside=None):
        value = zero
        for a in range(SUBS):
            part = spin(ref[pl.ds(a * SUBS, SUBS), :], a * ROWS - at)
            value = jnp.where(lax.div(lane, ROWS) == a, part, value)
        return value if inside is None else jnp.where(inside, value, 0.0)

    for i, (column, at, inside) in enumerate(
        ((FIRST, 0, cross > 0), (LAST, LANES - 1, cross < n_cross - 1))
    ):

        @pl.when(solve == column)
        def _():
            wait_for(edge_own, PARTS - 1, own_rsem)
            wait_for(edge_far, PARTS, far_rsem)
            sides = []
            for plane in (0, 1):
                warm, cond = plane * ROWS, (2 + plane) * ROWS
                total = along(edge_own, cond) + along(edge_far, cond, inside)
                step = along(edge_far, warm, inside) - along(edge_own, warm)
                sides.append(0.5 * total * step)
                flux_send[pl.ds(plane, SUBS, stride=2), :] = sides[plane]
            first1, first2, second = (along(edge_own, f * ROWS) for f in (4, 5, 6))
            element, way = merge_leaf(
                second, spin(second, -1), first1, first2, spin(first1, -1), spin(first2, -1)
            )
            loads, _ = merge_leaf_loads(way, sides, [spin(v, -1) for v in sides])
            fields = loads + element
            for shift in (2, 4, 8):
                fields, _, _ = climb(fields, tuple(spin(v, -shift) for v in fields))
            for a in range(SUBS):
                for j in range(LOADS):
                    at_rows = pl.ds(a * SUBS * LOADS + j, SUBS, stride=LOADS)
                    moved = spin(fields[j], at - a * ROWS)
                    extra[at_rows, :] = jnp.where(lane == at, moved, 0.0)
            to_all(0, 16, flux_to(i))
            flux_recv[pl.ds(i * 2, 2), :] = flux_send[pl.ds((column % SUBS) * 2, 2), :]

    @pl.when(owner)
    def _():
        wait_for(part_recv, (PARTS - 1) * USED, part_rsem)

        level = []
        for k in range(SUBS):
            loads = tuple(
                part_recv[pl.ds(k * SLOT + j, SUBS, stride=SUBS * SLOT), :]
                + extra[pl.ds(k * LOADS + j, SUBS, stride=SUBS * LOADS), :]
                for j in range(LOADS)
            )
            rest = tuple(
                part_recv[pl.ds(k * SLOT + j, SUBS, stride=SUBS * SLOT), :]
                for j in range(LOADS, USED)
            )
            level.append(loads + rest)
        steps = []
        while len(level) > 1:
            joined = [climb(level[2 * m], level[2 * m + 1]) for m in range(len(level) // 2)]
            steps.append([item[1:] for item in joined])
            level = [item[0] for item in joined]
        fields = level[0]
        trail = []
        for shift in (1, 2, 4):
            raised = tuple(pltpu.roll(v, SUBS - shift, 0) for v in fields)
            fields, way, value = climb(fields, raised)
            trail.append((way, value, shift))
        f1, f2, _, _, ea1, ea2, sa, n11, n12, n21, n22, _, _, _ = fields
        i11, i12, i22 = inverse(sa, ea1 + (n11 + n12), ea2 + (n21 + n22))
        before = (i11 * f1 + i12 * f2, i12 * f1 + i22 * f2)
        after = (zero, zero)

        for way, value, shift in reversed(trail):
            inner = middle(way, value, before, after)
            first = (sub & shift) == 0
            before = tuple(
                jnp.where(first, b, pltpu.roll(v, shift, 0)) for b, v in zip(before, inner)
            )
            after = tuple(
                jnp.where(first, v, pltpu.roll(a, shift, 0)) for v, a in zip(inner, after)
            )
        nodes = [before, after]
        for step in reversed(steps):
            finer = []
            for m, (way, value) in enumerate(step):
                finer += [nodes[m], middle(way, value, nodes[m], nodes[m + 1])]
            nodes = finer + [nodes[-1]]
        for k in range(SUBS):
            for j, value in enumerate(nodes[k] + nodes[k + 1]):
                node_send[pl.ds(k * LOADS + j, SUBS, stride=SUBS * LOADS), :] = value

        def values_to(part):
            pltpu.make_async_remote_copy(
                src_ref=slot(node_send, part, LOADS, LOADS),
                dst_ref=slot(node_recv, column_row, LOADS, LOADS),
                send_sem=node_ssem,
                recv_sem=node_rsem,
                device_id={"solve": part},
                device_id_type=MESH,
            ).start()

        for n in range(PARTS):
            part = (n // 2) % 4 * GROUP + n // 8 * 2 + n % 2
            if n < OWNERS:
                pl.when(solve != part)(functools.partial(values_to, part))
            else:
                values_to(part)
        here = pl.ds(pl.multiple_of(column_row * LOADS, LOADS), LOADS)
        there = pl.ds(pl.multiple_of(solve * LOADS, LOADS), LOADS)
        node_recv[here, :] = node_send[there, :]

    for i, column in enumerate((FIRST, LAST)):

        @pl.when(solve == column)
        def _():
            to_all(16, PARTS, flux_to(i))

    @pl.when(outer)
    def _():
        wait_for(flux_recv, 2, flux_rsem)

    @pl.when(jnp.logical_not(outer))
    def _():
        wait_for(flux_recv, 4, flux_rsem)

    shift = lax.rem(LANES - lax.div(solve, SUBS) * ROWS, LANES)
    flux = pltpu.roll(flux_recv[...], shift, 1)
    flux = jnp.concatenate([flux, jnp.zeros((LANES - SUBS, LANES), jnp.float32)], axis=0).T
    for i, (column, at) in enumerate(((0, 0), (SUBS - 1, LANES - 1))):
        for j in range(4):
            where = pl.ds((j * SUBS + column) * SUBS, SUBS)
            part = flux[(j % 2) * SUBS : (j % 2 + 1) * SUBS]
            moved = spin(part, at - 2 * i - j // 2)
            source[where, :] += jnp.where(lane == at, moved, 0.0)
    _, owns = climb_loads()

    @pl.when(owner)
    def _():
        wait_for(node_recv, (OWNERS - 1) * LOADS, node_rsem)

    @pl.when(jnp.logical_not(owner))
    def _():
        wait_for(node_recv, OWNERS * LOADS, node_rsem)

    values = [node_recv[pl.ds(j, SUBS, stride=LOADS), :] for j in range(LOADS)]
    ends = [tuple(values[:2]), tuple(values[2:])]

    nodes = ends
    for back, own in zip(reversed(backs), reversed(owns)):
        finer = []
        for m in range(len(back)):
            finer += [nodes[m], middle(back[m], own[m], nodes[m], nodes[m + 1])]
        nodes = finer + [nodes[-1]]
    for i in range(ROWS):
        for plane in (0, 1):
            start = (plane * 2 + i // SUBS) * SUBS * SUBS + i % SUBS
            out_ref[pl.ds(start, SUBS, stride=SUBS), :] = nodes[i][plane]

    @pl.when(outer)
    def _():
        wait_for(edge_own, 3, edge_ssem)
        wait_for(node_send, (PARTS - 1) * 2, flux_ssem)

    @pl.when(jnp.logical_not(outer))
    def _():
        wait_for(edge_own, 4, edge_ssem)

    @pl.when(owner)
    def _():
        wait_for(part_send, (OWNERS - 1) * USED, part_ssem)
        wait_for(node_send, (PARTS - 1) * LOADS, node_ssem)

    @pl.when(jnp.logical_not(owner))
    def _():
        wait_for(part_send, OWNERS * USED, part_ssem)


def tiles(array):
    array = array.reshape(-1, ROWS // SUBS, SUBS, SUBS, LANES)
    return array.transpose(0, 1, 3, 2, 4).reshape(-1, LANES)


def per_device(temperature, transfer, diffusivity, exchange):
    vmem = lambda *shape: pltpu.VMEM(shape, jnp.float32)
    dma = pltpu.SemaphoreType.DMA
    out = pl.pallas_call(
        kernel,
        out_shape=jax.ShapeDtypeStruct((FLAT, LANES), jnp.float32),
        in_specs=[pl.BlockSpec(memory_space=pltpu.HBM)] * 4,
        out_specs=pl.BlockSpec(memory_space=pltpu.VMEM),
        scratch_shapes=[
            vmem(FLAT, LANES),
            vmem(FLAT, LANES),
            vmem(FLAT, LANES),
            vmem(FLAT // 2, LANES),
            vmem(FLAT, LANES),
            vmem(SUBS, LANES),
            vmem(PARTS, LANES),
            vmem(PARTS, LANES),
            vmem(2 * SUBS, LANES),
            vmem(SUBS, LANES),
            vmem(OWNERS * SLOT, LANES),
            vmem(OWNERS * LOADS, LANES),
            vmem(PARTS * SLOT, LANES),
            vmem(PARTS * LOADS, LANES),
            vmem(PARTS * LOADS, LANES),
            vmem(OWNERS * LOADS, LANES),
            dma((4,)),
            dma,
            dma,
            dma,
            dma,
            dma,
            dma,
            dma,
            dma,
            dma,
        ],
        compiler_params=pltpu.CompilerParams(
            collective_id=0, has_side_effects=True, vmem_limit_bytes=16 * 1024 * 1024
        ),
        cost_estimate=pl.CostEstimate(
            flops=4_000_000, bytes_accessed=600_000, transcendentals=0
        ),
        name="line_step",
    )(
        *(
            pltpu.with_memory_space_constraint(tiles(array), pltpu.HBM)
            for array in (temperature, transfer, diffusivity, exchange)
        )
    )
    out = out.reshape(2, ROWS // SUBS, SUBS, SUBS, LANES).transpose(0, 1, 3, 2, 4)
    return out.reshape(2, ROWS, SUBS * LANES)


def solution(mesh):
    specs = (P(None, "solve", "cross"),) * 3 + (P("solve", "cross"),)
    return jax.shard_map(
        per_device,
        mesh=mesh,
        in_specs=specs,
        out_specs=P(None, "solve", "cross"),
        check_vma=False,
    )
```

```python
import functools

import jax
import jax.numpy as jnp
from jax import lax
from jax.experimental import pallas as pl
from jax.experimental.pallas import tpu as pltpu
from jax.sharding import PartitionSpec as P

MESH = pl.DeviceIdType.MESH
ROWS, SUBS, LANES = 16, 8, 128
GROUP, OWNERS, PARTS = 16, 8, 64
FIRST, LAST = 0, 49
FRONT = (1, 0, 16, 17, 32, 33, 48, 49)
LOADS, USED, SLOT = 4, 14, 16
FLAT = 2 * ROWS * SUBS


def inverse(coupling, first, second):
    scale = 1.0 / (coupling * (first + second) + first * second)
    return (coupling + second) * scale, coupling * scale, (coupling + first) * scale


def merge(left, right):
    ea1, ea2, sa, n11, n12, n21, n22, ec1, ec2, sc = left
    fa1, fa2, fs, m11, m12, m21, m22, fc1, fc2, gs = right
    eb1, eb2, sb = ec1 + fa1, ec2 + fa2, sc + fs
    r1 = eb1 + ((n11 + n21) + (m11 + m12))
    r2 = eb2 + ((n12 + n22) + (m21 + m22))
    i11, i12, i22 = inverse(sb, r1, r2)
    g11, g12 = n11 * i11 + n12 * i12, n11 * i12 + n12 * i22
    g21, g22 = n21 * i11 + n22 * i12, n21 * i12 + n22 * i22
    h11, h12 = i11 * m11 + i12 * m21, i11 * m12 + i12 * m22
    h21, h22 = i12 * m11 + i22 * m21, i12 * m12 + i22 * m22
    joined = (
        ea1 + (g11 * eb1 + g12 * eb2),
        ea2 + (g21 * eb1 + g22 * eb2),
        sa + (g11 * n21 + g12 * n22),
        g11 * m11 + g12 * m21,
        g11 * m12 + g12 * m22,
        g21 * m11 + g22 * m21,
        g21 * m12 + g22 * m22,
        fc1 + (h11 * eb1 + h21 * eb2),
        fc2 + (h12 * eb1 + h22 * eb2),
        gs + (m11 * h12 + m21 * h22),
    )
    return joined, (i11, i12, i22, g11, g12, g21, g22, h11, h12, h21, h22)


def merge_leaf(sa, sb, n1, n2, m1, m2):
    r1, r2 = 1.0 + (n1 + m1), 1.0 + (n2 + m2)
    i11, i12, i22 = inverse(sb, r1, r2)
    g11, g12, g21, g22 = n1 * i11, n1 * i12, n2 * i12, n2 * i22
    h11, h12, h21, h22 = i11 * m1, i12 * m2, i12 * m1, i22 * m2
    joined = (
        1.0 + (g11 + g12),
        1.0 + (g21 + g22),
        sa + g12 * n2,
        g11 * m1,
        g12 * m2,
        g21 * m1,
        g22 * m2,
        h11 + h21,
        h12 + h22,
        m1 * h12,
    )
    return joined, (i11, i12, i22, g11, g12, g21, g22, h11, h12, h21, h22)


def merge_loads(back, left, right):
    i11, i12, i22, g11, g12, g21, g22, h11, h12, h21, h22 = back
    a1, a2, b1, b2 = left
    c1, c2, d1, d2 = right
    b1, b2 = b1 + c1, b2 + c2
    loads = (
        a1 + (g11 * b1 + g12 * b2),
        a2 + (g21 * b1 + g22 * b2),
        d1 + (h11 * b1 + h21 * b2),
        d2 + (h12 * b1 + h22 * b2),
    )
    return loads, (i11 * b1 + i12 * b2, i12 * b1 + i22 * b2)


def merge_leaf_loads(back, a, b):
    i11, i12, i22, g11, g12, g21, g22, h11, h12, h21, h22 = back
    a1, a2 = a
    b1, b2 = b
    loads = (
        a1 + (g11 * b1 + g12 * b2),
        a2 + (g21 * b1 + g22 * b2),
        h11 * b1 + h21 * b2,
        h12 * b1 + h22 * b2,
    )
    return loads, (i11 * b1 + i12 * b2, i12 * b1 + i22 * b2)


def middle(back, own, before, after):
    g11, g12, g21, g22, h11, h12, h21, h22 = back[3:]
    a1, a2 = before
    c1, c2 = after
    return (
        own[0] + ((g11 * a1 + g21 * a2) + (h11 * c1 + h12 * c2)),
        own[1] + ((g12 * a1 + g22 * a2) + (h21 * c1 + h22 * c2)),
    )


def kernel(
    temp_hbm,
    face_hbm,
    diff_hbm,
    sheet_hbm,
    out_ref,
    temp,
    face,
    diff,
    sheet,
    source,
    edge_send,
    edge_own,
    edge_far,
    flux_send,
    flux_recv,
    part_send,
    late_send,
    part_recv,
    extra,
    node_send,
    node_recv,
    in_sem,
    edge_ssem,
    own_rsem,
    far_rsem,
    flux_ssem,
    flux_rsem,
    part_ssem,
    part_rsem,
    node_ssem,
    node_rsem,
):
    solve = lax.axis_index("solve")
    cross = lax.axis_index("cross")
    n_cross = lax.axis_size("cross")
    place = lax.rem(solve, GROUP)
    group = lax.div(solve, GROUP)

    loads_in = [
        pltpu.make_async_copy(src, dst, in_sem.at[i])
        for i, (src, dst) in enumerate(
            ((temp_hbm, temp), (diff_hbm, diff), (face_hbm, face), (sheet_hbm, sheet))
        )
    ]
    for copy in loads_in:
        copy.start()

    owner = place < 2
    column_row = group * 2 + place
    outer = (solve == FIRST) | (solve == LAST)
    rows_of = [lax.rem(solve + step, OWNERS) for step in range(OWNERS)]

    def device_of(index):
        return lax.div(index, 2) * GROUP + lax.rem(index, 2)

    right = lax.rem(cross + 1, n_cross)
    left = lax.rem(cross + n_cross - 1, n_cross)

    barrier = pltpu.get_barrier_semaphore()
    for column, side in ((FIRST, left), (LAST, right)):

        @pl.when(solve == column)
        def _():
            def greet(index, _):
                pl.semaphore_signal(
                    barrier,
                    1,
                    device_id={"solve": index, "cross": side},
                    device_id_type=MESH,
                )
                return 0

            lax.fori_loop(0, PARTS, greet, 0)

    @pl.when(owner)
    def _():
        def greet(step, _):
            pl.semaphore_signal(
                barrier,
                1,
                device_id={"solve": lax.rem(solve + step, PARTS)},
                device_id_type=MESH,
            )
            return 0

        lax.fori_loop(1, PARTS, greet, 0)
        extra[...] = jnp.zeros((PARTS * LOADS, LANES), jnp.float32)

    lane = lax.broadcasted_iota(jnp.int32, (SUBS, LANES), 1)
    sub = lax.broadcasted_iota(jnp.int32, (SUBS, LANES), 0)

    zero = jnp.zeros((SUBS, LANES), jnp.float32)

    def spin(value, shift):
        return pltpu.roll(value, shift % LANES, 1)

    def tile(ref, block, column):
        return ref[pl.ds((block * SUBS + column) * SUBS, SUBS), :]

    def slot(ref, index, rows, used):
        start = index * rows if isinstance(index, int) else pl.multiple_of(index * rows, rows)
        return ref.at[pl.ds(start, used)]

    for copy in loads_in:
        copy.wait()
    tracks = [(ref, j) for ref in (temp, diff, face) for j in range(4)]
    tracks += [(sheet, 0), (sheet, 1)]
    for i, (column, shift) in enumerate(((0, 0), (SUBS - 1, 1))):
        packed = jnp.zeros((SUBS, LANES), jnp.float32)
        for j, (ref, block) in enumerate(tracks):
            at = j * SUBS
            packed = jnp.where(lane == at, spin(tile(ref, block, column), at + shift), packed)
        for step in (1, 2, 4):
            packed = packed + spin(pltpu.roll(packed, SUBS - step, 0), step)
        edge_send[pl.ds(i, 1), :] = packed[0:1, :]
    flux_recv[pl.ds(4, 4), :] = zero[0:4, :]

    @pl.when(owner)
    def _():
        pl.semaphore_wait(barrier, 2 + OWNERS - 1)

    @pl.when(jnp.logical_not(owner))
    def _():
        pl.semaphore_wait(barrier, 2 + OWNERS)

    for i, (mine, theirs, side) in enumerate(
        ((FIRST, LAST, left), (LAST, FIRST, right))
    ):
        edge = edge_send.at[pl.ds(i, 1)]
        pltpu.make_async_remote_copy(
            src_ref=edge,
            dst_ref=slot(edge_far, solve, 1, 1),
            send_sem=edge_ssem,
            recv_sem=far_rsem,
            device_id={"solve": theirs, "cross": side},
            device_id_type=MESH,
        ).start()

        @pl.when(solve != mine)
        def _():
            pltpu.make_async_remote_copy(
                src_ref=edge,
                dst_ref=slot(edge_own, solve, 1, 1),
                send_sem=edge_ssem,
                recv_sem=own_rsem,
                device_id={"solve": mine},
                device_id_type=MESH,
            ).start()

        @pl.when(solve == mine)
        def _():
            edge_own[pl.ds(mine, 1), :] = edge_send[pl.ds(i, 1), :]

    def row(ref, plane, i):
        start = (plane * 2 + i // SUBS) * SUBS * SUBS + i % SUBS
        return ref[pl.ds(start, SUBS, stride=SUBS), :]

    backs = []
    level = []
    back = []
    for m in range(ROWS // 2):
        element, way = merge_leaf(
            row(sheet, 0, 2 * m),
            row(sheet, 0, 2 * m + 1),
            row(face, 0, 2 * m),
            row(face, 1, 2 * m),
            row(face, 0, 2 * m + 1),
            row(face, 1, 2 * m + 1),
        )
        level.append(element)
        back.append(way)
    backs.append(back)
    while len(level) > 1:
        pairs = [merge(level[2 * m], level[2 * m + 1]) for m in range(len(level) // 2)]
        level = [pair[0] for pair in pairs]
        backs.append([pair[1] for pair in pairs])
    element = level[0]

    def send_parts(ref, slot_rows, skip, rows):
        def rows_at(ref, slot_rows, index):
            start = pl.multiple_of(index * slot_rows, slot_rows) + skip % slot_rows
            return ref.at[pl.ds(start, rows)]

        for index in rows_of:

            @pl.when(device_of(index) != solve)
            def _():
                pltpu.make_async_remote_copy(
                    src_ref=rows_at(ref, slot_rows, index),
                    dst_ref=rows_at(part_recv, SLOT, solve),
                    send_sem=part_ssem,
                    recv_sem=part_rsem,
                    device_id={"solve": device_of(index)},
                    device_id_type=MESH,
                ).start()

    for j, value in enumerate(element):
        part_send[pl.ds(LOADS + j, SUBS, stride=SLOT), :] = value
    send_parts(part_send, SLOT, LOADS, USED - LOADS)

    for block in range(4):
        heat = [tile(temp, block, t) for t in range(SUBS)]
        cond = [tile(diff, block, t) for t in range(SUBS)]
        heat_turned = [spin(v, -1) for v in heat] + [zero]
        cond_turned = [spin(v, -1) for v in cond] + [zero]
        last = lane == LANES - 1
        before = zero
        for t in range(SUBS):
            next_heat = jnp.where(last, heat_turned[t + 1], heat_turned[t])
            next_cond = jnp.where(last, cond_turned[t + 1], cond_turned[t])
            flux = 0.5 * (cond[t] + next_cond) * (next_heat - heat[t])
            if t == SUBS - 1:
                flux = jnp.where(last, 0.0, flux)
            turned = spin(flux, 1)
            previous = jnp.where(lane == 0, before, turned)
            before = turned
            source[pl.ds((block * SUBS + t) * SUBS, SUBS), :] = heat[t] + flux - previous


    def climb_loads():
        owns = []
        level = []
        own = []
        for m in range(ROWS // 2):
            loads, value = merge_leaf_loads(
                backs[0][m],
                (row(source, 0, 2 * m), row(source, 1, 2 * m)),
                (row(source, 0, 2 * m + 1), row(source, 1, 2 * m + 1)),
            )
            level.append(loads)
            own.append(value)
        owns.append(own)
        for back in backs[1:]:
            pairs = [
                merge_loads(back[m], level[2 * m], level[2 * m + 1]) for m in range(len(back))
            ]
            level = [pair[0] for pair in pairs]
            owns.append([pair[1] for pair in pairs])
        return level[0], owns

    loads, _ = climb_loads()
    for j, value in enumerate(loads):
        late_send[pl.ds(j, SUBS, stride=LOADS), :] = value

    send_parts(late_send, LOADS, 0, LOADS)

    @pl.when(owner)
    def _():
        here = pl.multiple_of(solve * SLOT, SLOT)
        there = pl.multiple_of(column_row * SLOT, SLOT) + LOADS
        late = pl.ds(pl.multiple_of(column_row * LOADS, LOADS), LOADS)
        part_recv[pl.ds(here, LOADS), :] = late_send[late, :]
        part_recv[pl.ds(here + LOADS, USED - LOADS), :] = part_send[
            pl.ds(there, USED - LOADS), :
        ]

    def climb(left_fields, right_fields):
        element, way = merge(left_fields[LOADS:], right_fields[LOADS:])
        loads, value = merge_loads(way, left_fields[:LOADS], right_fields[:LOADS])
        return loads + element, way, value

    def wait_for(ref, rows, sem):
        part = ref.at[pl.ds(0, rows)]
        pltpu.make_async_copy(part, part, sem).wait()

    def to_all(first, last, send):
        def one(n, _):
            part = lax.rem(lax.div(n, 2), 4) * GROUP + lax.div(n, 8) * 2 + lax.rem(n, 2)

            @pl.when(part != solve)
            def _():
                send(part)

            return 0

        lax.fori_loop(first, last, one, 0)

    def flux_to(i):
        def send(part):
            pltpu.make_async_remote_copy(
                src_ref=slot(flux_send, lax.rem(part, SUBS), 2, 2),
                dst_ref=flux_recv.at[pl.ds(i * 2, 2)],
                send_sem=flux_ssem,
                recv_sem=flux_rsem,
                device_id={"solve": part},
                device_id_type=MESH,
            ).start()

        return send

    def along(ref, at, inside=None):
        value = zero
        for a in range(SUBS):
            part = spin(ref[pl.ds(a * SUBS, SUBS), :], a * ROWS - at)
            value = jnp.where(lax.div(lane, ROWS) == a, part, value)
        return value if inside is None else jnp.where(inside, value, 0.0)

    for i, (column, at, inside) in enumerate(
        ((FIRST, 0, cross > 0), (LAST, LANES - 1, cross < n_cross - 1))
    ):

        @pl.when(solve == column)
        def _():
            wait_for(edge_own, PARTS - 1, own_rsem)
            first1, first2, second = (along(edge_own, f * ROWS) for f in (4, 5, 6))
            element, way = merge_leaf(
                second, spin(second, -1), first1, first2, spin(first1, -1), spin(first2, -1)
            )
            ways = [way]
            for shift in (2, 4, 8):
                element, way = merge(element, tuple(spin(v, -shift) for v in element))
                ways.append(way)
            own = [along(edge_own, f * ROWS) for f in range(4)]
            wait_for(edge_far, PARTS, far_rsem)
            far = [along(edge_far, f * ROWS, inside) for f in range(4)]
            sides = []
            for plane in (0, 1):
                total = own[2 + plane] + far[2 + plane]
                sides.append(0.5 * total * (far[plane] - own[plane]))
                flux_send[pl.ds(plane, SUBS, stride=2), :] = sides[plane]
            fields, _ = merge_leaf_loads(ways[0], sides, [spin(v, -1) for v in sides])
            for shift, way in zip((2, 4, 8), ways[1:]):
                fields, _ = merge_loads(way, fields, [spin(v, -shift) for v in fields])
            for a in range(SUBS):
                for j in range(LOADS):
                    at_rows = pl.ds(a * SUBS * LOADS + j, SUBS, stride=LOADS)
                    moved = spin(fields[j], at - a * ROWS)
                    extra[at_rows, :] = jnp.where(lane == at, moved, 0.0)
            for part in FRONT:
                if part != column:
                    flux_to(i)(part)
            flux_recv[pl.ds(i * 2, 2), :] = flux_send[pl.ds((column % SUBS) * 2, 2), :]

    @pl.when(owner)
    def _():
        wait_for(part_recv, (PARTS - 1) * USED, part_rsem)

        level = []
        for k in range(SUBS):
            loads = tuple(
                part_recv[pl.ds(k * SLOT + j, SUBS, stride=SUBS * SLOT), :]
                + extra[pl.ds(k * LOADS + j, SUBS, stride=SUBS * LOADS), :]
                for j in range(LOADS)
            )
            rest = tuple(
                part_recv[pl.ds(k * SLOT + j, SUBS, stride=SUBS * SLOT), :]
                for j in range(LOADS, USED)
            )
            level.append(loads + rest)
        steps = []
        while len(level) > 1:
            joined = [climb(level[2 * m], level[2 * m + 1]) for m in range(len(level) // 2)]
            steps.append([item[1:] for item in joined])
            level = [item[0] for item in joined]
        fields = level[0]
        trail = []
        for shift in (1, 2, 4):
            raised = tuple(pltpu.roll(v, SUBS - shift, 0) for v in fields)
            fields, way, value = climb(fields, raised)
            trail.append((way, value, shift))
        f1, f2, _, _, ea1, ea2, sa, n11, n12, n21, n22, _, _, _ = fields
        i11, i12, i22 = inverse(sa, ea1 + (n11 + n12), ea2 + (n21 + n22))
        before = (i11 * f1 + i12 * f2, i12 * f1 + i22 * f2)
        after = (zero, zero)

        for way, value, shift in reversed(trail):
            inner = middle(way, value, before, after)
            first = (sub & shift) == 0
            before = tuple(
                jnp.where(first, b, pltpu.roll(v, shift, 0)) for b, v in zip(before, inner)
            )
            after = tuple(
                jnp.where(first, v, pltpu.roll(a, shift, 0)) for v, a in zip(inner, after)
            )
        nodes = [before, after]
        for step in reversed(steps):
            finer = []
            for m, (way, value) in enumerate(step):
                finer += [nodes[m], middle(way, value, nodes[m], nodes[m + 1])]
            nodes = finer + [nodes[-1]]
        for k in range(SUBS):
            for j, value in enumerate(nodes[k] + nodes[k + 1]):
                node_send[pl.ds(k * LOADS + j, SUBS, stride=SUBS * LOADS), :] = value

        def values_to(part):
            pltpu.make_async_remote_copy(
                src_ref=slot(node_send, part, LOADS, LOADS),
                dst_ref=slot(node_recv, column_row, LOADS, LOADS),
                send_sem=node_ssem,
                recv_sem=node_rsem,
                device_id={"solve": part},
                device_id_type=MESH,
            ).start()

        for n in range(PARTS):
            part = (n // 2) % 4 * GROUP + n // 8 * 2 + n % 2
            if n < OWNERS:
                pl.when(solve != part)(functools.partial(values_to, part))
            else:
                values_to(part)
        here = pl.ds(pl.multiple_of(column_row * LOADS, LOADS), LOADS)
        there = pl.ds(pl.multiple_of(solve * LOADS, LOADS), LOADS)
        node_recv[here, :] = node_send[there, :]

    for i, column in enumerate((FIRST, LAST)):

        @pl.when(solve == column)
        def _():
            to_all(OWNERS, PARTS, flux_to(i))

    @pl.when(outer)
    def _():
        wait_for(flux_recv, 2, flux_rsem)

    @pl.when(jnp.logical_not(outer))
    def _():
        wait_for(flux_recv, 4, flux_rsem)

    shift = lax.rem(LANES - lax.div(solve, SUBS) * ROWS, LANES)
    flux = pltpu.roll(flux_recv[...], shift, 1)
    flux = jnp.concatenate([flux, jnp.zeros((LANES - SUBS, LANES), jnp.float32)], axis=0).T
    for i, (column, at) in enumerate(((0, 0), (SUBS - 1, LANES - 1))):
        for j in range(4):
            where = pl.ds((j * SUBS + column) * SUBS, SUBS)
            part = flux[(j % 2) * SUBS : (j % 2 + 1) * SUBS]
            moved = spin(part, at - 2 * i - j // 2)
            source[where, :] += jnp.where(lane == at, moved, 0.0)
    _, owns = climb_loads()

    @pl.when(owner)
    def _():
        wait_for(node_recv, (OWNERS - 1) * LOADS, node_rsem)

    @pl.when(jnp.logical_not(owner))
    def _():
        wait_for(node_recv, OWNERS * LOADS, node_rsem)

    values = [node_recv[pl.ds(j, SUBS, stride=LOADS), :] for j in range(LOADS)]
    ends = [tuple(values[:2]), tuple(values[2:])]

    nodes = ends
    for back, own in zip(reversed(backs), reversed(owns)):
        finer = []
        for m in range(len(back)):
            finer += [nodes[m], middle(back[m], own[m], nodes[m], nodes[m + 1])]
        nodes = finer + [nodes[-1]]
    for i in range(ROWS):
        for plane in (0, 1):
            start = (plane * 2 + i // SUBS) * SUBS * SUBS + i % SUBS
            out_ref[pl.ds(start, SUBS, stride=SUBS), :] = nodes[i][plane]

    @pl.when(outer)
    def _():
        wait_for(edge_own, 3, edge_ssem)
        wait_for(node_send, (PARTS - 1) * 2, flux_ssem)

    @pl.when(jnp.logical_not(outer))
    def _():
        wait_for(edge_own, 4, edge_ssem)

    @pl.when(owner)
    def _():
        wait_for(part_send, (OWNERS - 1) * USED, part_ssem)
        wait_for(node_send, (PARTS - 1) * LOADS, node_ssem)

    @pl.when(jnp.logical_not(owner))
    def _():
        wait_for(part_send, OWNERS * USED, part_ssem)


def tiles(array):
    array = array.reshape(-1, ROWS // SUBS, SUBS, SUBS, LANES)
    return array.transpose(0, 1, 3, 2, 4).reshape(-1, LANES)


def per_device(temperature, transfer, diffusivity, exchange):
    vmem = lambda *shape: pltpu.VMEM(shape, jnp.float32)
    dma = pltpu.SemaphoreType.DMA
    out = pl.pallas_call(
        kernel,
        out_shape=jax.ShapeDtypeStruct((FLAT, LANES), jnp.float32),
        in_specs=[pl.BlockSpec(memory_space=pltpu.HBM)] * 4,
        out_specs=pl.BlockSpec(memory_space=pltpu.VMEM),
        scratch_shapes=[
            vmem(FLAT, LANES),
            vmem(FLAT, LANES),
            vmem(FLAT, LANES),
            vmem(FLAT // 2, LANES),
            vmem(FLAT, LANES),
            vmem(SUBS, LANES),
            vmem(PARTS, LANES),
            vmem(PARTS, LANES),
            vmem(2 * SUBS, LANES),
            vmem(SUBS, LANES),
            vmem(OWNERS * SLOT, LANES),
            vmem(OWNERS * LOADS, LANES),
            vmem(PARTS * SLOT, LANES),
            vmem(PARTS * LOADS, LANES),
            vmem(PARTS * LOADS, LANES),
            vmem(OWNERS * LOADS, LANES),
            dma((4,)),
            dma,
            dma,
            dma,
            dma,
            dma,
            dma,
            dma,
            dma,
            dma,
        ],
        compiler_params=pltpu.CompilerParams(
            collective_id=0, has_side_effects=True, vmem_limit_bytes=16 * 1024 * 1024
        ),
        cost_estimate=pl.CostEstimate(
            flops=4_000_000, bytes_accessed=600_000, transcendentals=0
        ),
        name="line_step",
    )(
        *(
            pltpu.with_memory_space_constraint(tiles(array), pltpu.HBM)
            for array in (temperature, transfer, diffusivity, exchange)
        )
    )
    out = out.reshape(2, ROWS // SUBS, SUBS, SUBS, LANES).transpose(0, 1, 3, 2, 4)
    return out.reshape(2, ROWS, SUBS * LANES)


def solution(mesh):
    specs = (P(None, "solve", "cross"),) * 3 + (P("solve", "cross"),)
    return jax.shard_map(
        per_device,
        mesh=mesh,
        in_specs=specs,
        out_specs=P(None, "solve", "cross"),
        check_vma=False,
    )
```

```python
import functools

import jax
import jax.numpy as jnp
from jax import lax
from jax.experimental import pallas as pl
from jax.experimental.pallas import tpu as pltpu
from jax.sharding import PartitionSpec as P

MESH = pl.DeviceIdType.MESH
ROWS, SUBS, LANES = 16, 8, 128
GROUP, OWNERS, PARTS = 16, 8, 64
FIRST, LAST = 0, 49
LOADS, USED, SLOT = 4, 14, 16
FLAT = 2 * ROWS * SUBS


def inverse(coupling, first, second):
    scale = 1.0 / (coupling * (first + second) + first * second)
    return (coupling + second) * scale, coupling * scale, (coupling + first) * scale


def merge(left, right):
    ea1, ea2, sa, n11, n12, n21, n22, ec1, ec2, sc = left
    fa1, fa2, fs, m11, m12, m21, m22, fc1, fc2, gs = right
    eb1, eb2, sb = ec1 + fa1, ec2 + fa2, sc + fs
    r1 = eb1 + ((n11 + n21) + (m11 + m12))
    r2 = eb2 + ((n12 + n22) + (m21 + m22))
    i11, i12, i22 = inverse(sb, r1, r2)
    g11, g12 = n11 * i11 + n12 * i12, n11 * i12 + n12 * i22
    g21, g22 = n21 * i11 + n22 * i12, n21 * i12 + n22 * i22
    h11, h12 = i11 * m11 + i12 * m21, i11 * m12 + i12 * m22
    h21, h22 = i12 * m11 + i22 * m21, i12 * m12 + i22 * m22
    joined = (
        ea1 + (g11 * eb1 + g12 * eb2),
        ea2 + (g21 * eb1 + g22 * eb2),
        sa + (g11 * n21 + g12 * n22),
        g11 * m11 + g12 * m21,
        g11 * m12 + g12 * m22,
        g21 * m11 + g22 * m21,
        g21 * m12 + g22 * m22,
        fc1 + (h11 * eb1 + h21 * eb2),
        fc2 + (h12 * eb1 + h22 * eb2),
        gs + (m11 * h12 + m21 * h22),
    )
    return joined, (i11, i12, i22, g11, g12, g21, g22, h11, h12, h21, h22)


def merge_leaf(sa, sb, n1, n2, m1, m2):
    r1, r2 = 1.0 + (n1 + m1), 1.0 + (n2 + m2)
    i11, i12, i22 = inverse(sb, r1, r2)
    g11, g12, g21, g22 = n1 * i11, n1 * i12, n2 * i12, n2 * i22
    h11, h12, h21, h22 = i11 * m1, i12 * m2, i12 * m1, i22 * m2
    joined = (
        1.0 + (g11 + g12),
        1.0 + (g21 + g22),
        sa + g12 * n2,
        g11 * m1,
        g12 * m2,
        g21 * m1,
        g22 * m2,
        h11 + h21,
        h12 + h22,
        m1 * h12,
    )
    return joined, (i11, i12, i22, g11, g12, g21, g22, h11, h12, h21, h22)


def merge_loads(back, left, right):
    i11, i12, i22, g11, g12, g21, g22, h11, h12, h21, h22 = back
    a1, a2, b1, b2 = left
    c1, c2, d1, d2 = right
    b1, b2 = b1 + c1, b2 + c2
    loads = (
        a1 + (g11 * b1 + g12 * b2),
        a2 + (g21 * b1 + g22 * b2),
        d1 + (h11 * b1 + h21 * b2),
        d2 + (h12 * b1 + h22 * b2),
    )
    return loads, (i11 * b1 + i12 * b2, i12 * b1 + i22 * b2)


def merge_leaf_loads(back, a, b):
    i11, i12, i22, g11, g12, g21, g22, h11, h12, h21, h22 = back
    a1, a2 = a
    b1, b2 = b
    loads = (
        a1 + (g11 * b1 + g12 * b2),
        a2 + (g21 * b1 + g22 * b2),
        h11 * b1 + h21 * b2,
        h12 * b1 + h22 * b2,
    )
    return loads, (i11 * b1 + i12 * b2, i12 * b1 + i22 * b2)


def middle(back, own, before, after):
    g11, g12, g21, g22, h11, h12, h21, h22 = back[3:]
    a1, a2 = before
    c1, c2 = after
    return (
        own[0] + ((g11 * a1 + g21 * a2) + (h11 * c1 + h12 * c2)),
        own[1] + ((g12 * a1 + g22 * a2) + (h21 * c1 + h22 * c2)),
    )


def kernel(
    temp_hbm,
    face_hbm,
    diff_hbm,
    sheet_hbm,
    out_ref,
    temp,
    face,
    diff,
    sheet,
    source,
    edge_send,
    edge_own,
    edge_far,
    flux_send,
    flux_recv,
    part_send,
    late_send,
    part_recv,
    extra,
    node_send,
    node_recv,
    in_sem,
    edge_ssem,
    own_rsem,
    far_rsem,
    flux_ssem,
    flux_rsem,
    part_ssem,
    part_rsem,
    node_ssem,
    node_rsem,
):
    solve = lax.axis_index("solve")
    cross = lax.axis_index("cross")
    n_cross = lax.axis_size("cross")
    place = lax.rem(solve, GROUP)
    group = lax.div(solve, GROUP)

    loads_in = [
        pltpu.make_async_copy(src, dst, in_sem.at[i])
        for i, (src, dst) in enumerate(
            ((face_hbm, face), (sheet_hbm, sheet), (temp_hbm, temp), (diff_hbm, diff))
        )
    ]
    for copy in loads_in:
        copy.start()

    owner = place < 2
    column_row = group * 2 + place
    outer = (solve == FIRST) | (solve == LAST)
    rows_of = [lax.rem(solve + step, OWNERS) for step in range(OWNERS)]

    def device_of(index):
        return lax.div(index, 2) * GROUP + lax.rem(index, 2)

    right = lax.rem(cross + 1, n_cross)
    left = lax.rem(cross + n_cross - 1, n_cross)

    barrier = pltpu.get_barrier_semaphore()
    for column, side in ((FIRST, left), (LAST, right)):

        @pl.when(solve == column)
        def _():
            def greet(index, _):
                pl.semaphore_signal(
                    barrier,
                    1,
                    device_id={"solve": index, "cross": side},
                    device_id_type=MESH,
                )
                return 0

            lax.fori_loop(0, PARTS, greet, 0)

    @pl.when(owner)
    def _():
        def greet(step, _):
            pl.semaphore_signal(
                barrier,
                1,
                device_id={"solve": lax.rem(solve + step, PARTS)},
                device_id_type=MESH,
            )
            return 0

        lax.fori_loop(1, PARTS, greet, 0)
        extra[...] = jnp.zeros((PARTS * LOADS, LANES), jnp.float32)

    lane = lax.broadcasted_iota(jnp.int32, (SUBS, LANES), 1)
    sub = lax.broadcasted_iota(jnp.int32, (SUBS, LANES), 0)

    zero = jnp.zeros((SUBS, LANES), jnp.float32)

    def spin(value, shift):
        return pltpu.roll(value, shift % LANES, 1)

    def tile(ref, block, column):
        return ref[pl.ds((block * SUBS + column) * SUBS, SUBS), :]

    def slot(ref, index, rows, used):
        start = index * rows if isinstance(index, int) else pl.multiple_of(index * rows, rows)
        return ref.at[pl.ds(start, used)]

    def row(ref, plane, i):
        start = (plane * 2 + i // SUBS) * SUBS * SUBS + i % SUBS
        return ref[pl.ds(start, SUBS, stride=SUBS), :]

    loads_in[0].wait()
    loads_in[1].wait()
    backs = []
    level = []
    back = []
    for m in range(ROWS // 2):
        element, way = merge_leaf(
            row(sheet, 0, 2 * m),
            row(sheet, 0, 2 * m + 1),
            row(face, 0, 2 * m),
            row(face, 1, 2 * m),
            row(face, 0, 2 * m + 1),
            row(face, 1, 2 * m + 1),
        )
        level.append(element)
        back.append(way)
    backs.append(back)
    while len(level) > 1:
        pairs = [merge(level[2 * m], level[2 * m + 1]) for m in range(len(level) // 2)]
        level = [pair[0] for pair in pairs]
        backs.append([pair[1] for pair in pairs])
    element = level[0]

    def send_parts(ref, slot_rows, skip, rows):
        def rows_at(ref, slot_rows, index):
            start = pl.multiple_of(index * slot_rows, slot_rows) + skip % slot_rows
            return ref.at[pl.ds(start, rows)]

        for index in rows_of:

            @pl.when(device_of(index) != solve)
            def _():
                pltpu.make_async_remote_copy(
                    src_ref=rows_at(ref, slot_rows, index),
                    dst_ref=rows_at(part_recv, SLOT, solve),
                    send_sem=part_ssem,
                    recv_sem=part_rsem,
                    device_id={"solve": device_of(index)},
                    device_id_type=MESH,
                ).start()

    for j, value in enumerate(element):
        part_send[pl.ds(LOADS + j, SUBS, stride=SLOT), :] = value
    @pl.when(owner)
    def _():
        pl.semaphore_wait(barrier, 2 + OWNERS - 1)

    @pl.when(jnp.logical_not(owner))
    def _():
        pl.semaphore_wait(barrier, 2 + OWNERS)

    send_parts(part_send, SLOT, LOADS, USED - LOADS)

    loads_in[2].wait()
    loads_in[3].wait()
    tracks = [(ref, j) for ref in (temp, diff, face) for j in range(4)]
    tracks += [(sheet, 0), (sheet, 1)]
    for i, (column, shift) in enumerate(((0, 0), (SUBS - 1, 1))):
        packed = jnp.zeros((SUBS, LANES), jnp.float32)
        for j, (ref, block) in enumerate(tracks):
            at = j * SUBS
            packed = jnp.where(lane == at, spin(tile(ref, block, column), at + shift), packed)
        for step in (1, 2, 4):
            packed = packed + spin(pltpu.roll(packed, SUBS - step, 0), step)
        edge_send[pl.ds(i, 1), :] = packed[0:1, :]
    flux_recv[pl.ds(4, 4), :] = zero[0:4, :]

    for i, (mine, theirs, side) in enumerate(
        ((FIRST, LAST, left), (LAST, FIRST, right))
    ):
        edge = edge_send.at[pl.ds(i, 1)]
        pltpu.make_async_remote_copy(
            src_ref=edge,
            dst_ref=slot(edge_far, solve, 1, 1),
            send_sem=edge_ssem,
            recv_sem=far_rsem,
            device_id={"solve": theirs, "cross": side},
            device_id_type=MESH,
        ).start()

        @pl.when(solve != mine)
        def _():
            pltpu.make_async_remote_copy(
                src_ref=edge,
                dst_ref=slot(edge_own, solve, 1, 1),
                send_sem=edge_ssem,
                recv_sem=own_rsem,
                device_id={"solve": mine},
                device_id_type=MESH,
            ).start()

        @pl.when(solve == mine)
        def _():
            edge_own[pl.ds(mine, 1), :] = edge_send[pl.ds(i, 1), :]

    for block in range(4):
        heat = [tile(temp, block, t) for t in range(SUBS)]
        cond = [tile(diff, block, t) for t in range(SUBS)]
        heat_turned = [spin(v, -1) for v in heat] + [zero]
        cond_turned = [spin(v, -1) for v in cond] + [zero]
        last = lane == LANES - 1
        before = zero
        for t in range(SUBS):
            next_heat = jnp.where(last, heat_turned[t + 1], heat_turned[t])
            next_cond = jnp.where(last, cond_turned[t + 1], cond_turned[t])
            flux = 0.5 * (cond[t] + next_cond) * (next_heat - heat[t])
            if t == SUBS - 1:
                flux = jnp.where(last, 0.0, flux)
            turned = spin(flux, 1)
            previous = jnp.where(lane == 0, before, turned)
            before = turned
            source[pl.ds((block * SUBS + t) * SUBS, SUBS), :] = heat[t] + flux - previous


    def climb_loads():
        owns = []
        level = []
        own = []
        for m in range(ROWS // 2):
            loads, value = merge_leaf_loads(
                backs[0][m],
                (row(source, 0, 2 * m), row(source, 1, 2 * m)),
                (row(source, 0, 2 * m + 1), row(source, 1, 2 * m + 1)),
            )
            level.append(loads)
            own.append(value)
        owns.append(own)
        for back in backs[1:]:
            pairs = [
                merge_loads(back[m], level[2 * m], level[2 * m + 1]) for m in range(len(back))
            ]
            level = [pair[0] for pair in pairs]
            owns.append([pair[1] for pair in pairs])
        return level[0], owns

    loads, _ = climb_loads()
    for j, value in enumerate(loads):
        late_send[pl.ds(j, SUBS, stride=LOADS), :] = value

    send_parts(late_send, LOADS, 0, LOADS)

    @pl.when(owner)
    def _():
        here = pl.multiple_of(solve * SLOT, SLOT)
        there = pl.multiple_of(column_row * SLOT, SLOT) + LOADS
        late = pl.ds(pl.multiple_of(column_row * LOADS, LOADS), LOADS)
        part_recv[pl.ds(here, LOADS), :] = late_send[late, :]
        part_recv[pl.ds(here + LOADS, USED - LOADS), :] = part_send[
            pl.ds(there, USED - LOADS), :
        ]

    def climb(left_fields, right_fields):
        element, way = merge(left_fields[LOADS:], right_fields[LOADS:])
        loads, value = merge_loads(way, left_fields[:LOADS], right_fields[:LOADS])
        return loads + element, way, value

    def wait_for(ref, rows, sem):
        part = ref.at[pl.ds(0, rows)]
        pltpu.make_async_copy(part, part, sem).wait()

    def to_all(first, last, send):
        def one(n, _):
            part = lax.rem(lax.div(n, 2), 4) * GROUP + lax.div(n, 8) * 2 + lax.rem(n, 2)

            @pl.when(part != solve)
            def _():
                send(part)

            return 0

        lax.fori_loop(first, last, one, 0)

    def flux_to(i):
        def send(part):
            pltpu.make_async_remote_copy(
                src_ref=slot(flux_send, lax.rem(part, SUBS), 2, 2),
                dst_ref=flux_recv.at[pl.ds(i * 2, 2)],
                send_sem=flux_ssem,
                recv_sem=flux_rsem,
                device_id={"solve": part},
                device_id_type=MESH,
            ).start()

        return send

    def along(ref, at, inside=None):
        value = zero
        for a in range(SUBS):
            part = spin(ref[pl.ds(a * SUBS, SUBS), :], a * ROWS - at)
            value = jnp.where(lax.div(lane, ROWS) == a, part, value)
        return value if inside is None else jnp.where(inside, value, 0.0)

    for i, (column, at, inside) in enumerate(
        ((FIRST, 0, cross > 0), (LAST, LANES - 1, cross < n_cross - 1))
    ):

        @pl.when(solve == column)
        def _():
            wait_for(edge_own, PARTS - 1, own_rsem)
            wait_for(edge_far, PARTS, far_rsem)
            sides = []
            for plane in (0, 1):
                warm, cond = plane * ROWS, (2 + plane) * ROWS
                total = along(edge_own, cond) + along(edge_far, cond, inside)
                step = along(edge_far, warm, inside) - along(edge_own, warm)
                sides.append(0.5 * total * step)
                flux_send[pl.ds(plane, SUBS, stride=2), :] = sides[plane]
            first1, first2, second = (along(edge_own, f * ROWS) for f in (4, 5, 6))
            element, way = merge_leaf(
                second, spin(second, -1), first1, first2, spin(first1, -1), spin(first2, -1)
            )
            loads, _ = merge_leaf_loads(way, sides, [spin(v, -1) for v in sides])
            fields = loads + element
            for shift in (2, 4, 8):
                fields, _, _ = climb(fields, tuple(spin(v, -shift) for v in fields))
            for a in range(SUBS):
                for j in range(LOADS):
                    at_rows = pl.ds(a * SUBS * LOADS + j, SUBS, stride=LOADS)
                    moved = spin(fields[j], at - a * ROWS)
                    extra[at_rows, :] = jnp.where(lane == at, moved, 0.0)
            to_all(0, 16, flux_to(i))
            flux_recv[pl.ds(i * 2, 2), :] = flux_send[pl.ds((column % SUBS) * 2, 2), :]

    @pl.when(owner)
    def _():
        wait_for(part_recv, (PARTS - 1) * USED, part_rsem)

        level = []
        for k in range(SUBS):
            loads = tuple(
                part_recv[pl.ds(k * SLOT + j, SUBS, stride=SUBS * SLOT), :]
                + extra[pl.ds(k * LOADS + j, SUBS, stride=SUBS * LOADS), :]
                for j in range(LOADS)
            )
            rest = tuple(
                part_recv[pl.ds(k * SLOT + j, SUBS, stride=SUBS * SLOT), :]
                for j in range(LOADS, USED)
            )
            level.append(loads + rest)
        steps = []
        while len(level) > 1:
            joined = [climb(level[2 * m], level[2 * m + 1]) for m in range(len(level) // 2)]
            steps.append([item[1:] for item in joined])
            level = [item[0] for item in joined]
        fields = level[0]
        trail = []
        for shift in (1, 2, 4):
            raised = tuple(pltpu.roll(v, SUBS - shift, 0) for v in fields)
            fields, way, value = climb(fields, raised)
            trail.append((way, value, shift))
        f1, f2, _, _, ea1, ea2, sa, n11, n12, n21, n22, _, _, _ = fields
        i11, i12, i22 = inverse(sa, ea1 + (n11 + n12), ea2 + (n21 + n22))
        before = (i11 * f1 + i12 * f2, i12 * f1 + i22 * f2)
        after = (zero, zero)

        for way, value, shift in reversed(trail):
            inner = middle(way, value, before, after)
            first = (sub & shift) == 0
            before = tuple(
                jnp.where(first, b, pltpu.roll(v, shift, 0)) for b, v in zip(before, inner)
            )
            after = tuple(
                jnp.where(first, v, pltpu.roll(a, shift, 0)) for v, a in zip(inner, after)
            )
        nodes = [before, after]
        for step in reversed(steps):
            finer = []
            for m, (way, value) in enumerate(step):
                finer += [nodes[m], middle(way, value, nodes[m], nodes[m + 1])]
            nodes = finer + [nodes[-1]]
        for k in range(SUBS):
            for j, value in enumerate(nodes[k] + nodes[k + 1]):
                node_send[pl.ds(k * LOADS + j, SUBS, stride=SUBS * LOADS), :] = value

        def values_to(part):
            pltpu.make_async_remote_copy(
                src_ref=slot(node_send, part, LOADS, LOADS),
                dst_ref=slot(node_recv, column_row, LOADS, LOADS),
                send_sem=node_ssem,
                recv_sem=node_rsem,
                device_id={"solve": part},
                device_id_type=MESH,
            ).start()

        for n in range(PARTS):
            part = (n // 2) % 4 * GROUP + n // 8 * 2 + n % 2
            if n < OWNERS:
                pl.when(solve != part)(functools.partial(values_to, part))
            else:
                values_to(part)
        here = pl.ds(pl.multiple_of(column_row * LOADS, LOADS), LOADS)
        there = pl.ds(pl.multiple_of(solve * LOADS, LOADS), LOADS)
        node_recv[here, :] = node_send[there, :]

    for i, column in enumerate((FIRST, LAST)):

        @pl.when(solve == column)
        def _():
            to_all(16, PARTS, flux_to(i))

    @pl.when(outer)
    def _():
        wait_for(flux_recv, 2, flux_rsem)

    @pl.when(jnp.logical_not(outer))
    def _():
        wait_for(flux_recv, 4, flux_rsem)

    shift = lax.rem(LANES - lax.div(solve, SUBS) * ROWS, LANES)
    flux = pltpu.roll(flux_recv[...], shift, 1)
    flux = jnp.concatenate([flux, jnp.zeros((LANES - SUBS, LANES), jnp.float32)], axis=0).T
    for i, (column, at) in enumerate(((0, 0), (SUBS - 1, LANES - 1))):
        for j in range(4):
            where = pl.ds((j * SUBS + column) * SUBS, SUBS)
            part = flux[(j % 2) * SUBS : (j % 2 + 1) * SUBS]
            moved = spin(part, at - 2 * i - j // 2)
            source[where, :] += jnp.where(lane == at, moved, 0.0)
    _, owns = climb_loads()

    @pl.when(owner)
    def _():
        wait_for(node_recv, (OWNERS - 1) * LOADS, node_rsem)

    @pl.when(jnp.logical_not(owner))
    def _():
        wait_for(node_recv, OWNERS * LOADS, node_rsem)

    values = [node_recv[pl.ds(j, SUBS, stride=LOADS), :] for j in range(LOADS)]
    ends = [tuple(values[:2]), tuple(values[2:])]

    nodes = ends
    for back, own in zip(reversed(backs), reversed(owns)):
        finer = []
        for m in range(len(back)):
            finer += [nodes[m], middle(back[m], own[m], nodes[m], nodes[m + 1])]
        nodes = finer + [nodes[-1]]
    for i in range(ROWS):
        for plane in (0, 1):
            start = (plane * 2 + i // SUBS) * SUBS * SUBS + i % SUBS
            out_ref[pl.ds(start, SUBS, stride=SUBS), :] = nodes[i][plane]

    @pl.when(outer)
    def _():
        wait_for(edge_own, 3, edge_ssem)
        wait_for(node_send, (PARTS - 1) * 2, flux_ssem)

    @pl.when(jnp.logical_not(outer))
    def _():
        wait_for(edge_own, 4, edge_ssem)

    @pl.when(owner)
    def _():
        wait_for(part_send, (OWNERS - 1) * USED, part_ssem)
        wait_for(node_send, (PARTS - 1) * LOADS, node_ssem)

    @pl.when(jnp.logical_not(owner))
    def _():
        wait_for(part_send, OWNERS * USED, part_ssem)


def tiles(array):
    array = array.reshape(-1, ROWS // SUBS, SUBS, SUBS, LANES)
    return array.transpose(0, 1, 3, 2, 4).reshape(-1, LANES)


def per_device(temperature, transfer, diffusivity, exchange):
    vmem = lambda *shape: pltpu.VMEM(shape, jnp.float32)
    dma = pltpu.SemaphoreType.DMA
    out = pl.pallas_call(
        kernel,
        out_shape=jax.ShapeDtypeStruct((FLAT, LANES), jnp.float32),
        in_specs=[pl.BlockSpec(memory_space=pltpu.HBM)] * 4,
        out_specs=pl.BlockSpec(memory_space=pltpu.VMEM),
        scratch_shapes=[
            vmem(FLAT, LANES),
            vmem(FLAT, LANES),
            vmem(FLAT, LANES),
            vmem(FLAT // 2, LANES),
            vmem(FLAT, LANES),
            vmem(SUBS, LANES),
            vmem(PARTS, LANES),
            vmem(PARTS, LANES),
            vmem(2 * SUBS, LANES),
            vmem(SUBS, LANES),
            vmem(OWNERS * SLOT, LANES),
            vmem(OWNERS * LOADS, LANES),
            vmem(PARTS * SLOT, LANES),
            vmem(PARTS * LOADS, LANES),
            vmem(PARTS * LOADS, LANES),
            vmem(OWNERS * LOADS, LANES),
            dma((4,)),
            dma,
            dma,
            dma,
            dma,
            dma,
            dma,
            dma,
            dma,
            dma,
        ],
        compiler_params=pltpu.CompilerParams(
            collective_id=0, has_side_effects=True, vmem_limit_bytes=16 * 1024 * 1024
        ),
        cost_estimate=pl.CostEstimate(
            flops=4_000_000, bytes_accessed=600_000, transcendentals=0
        ),
        name="line_step",
    )(
        *(
            pltpu.with_memory_space_constraint(tiles(array), pltpu.HBM)
            for array in (temperature, transfer, diffusivity, exchange)
        )
    )
    out = out.reshape(2, ROWS // SUBS, SUBS, SUBS, LANES).transpose(0, 1, 3, 2, 4)
    return out.reshape(2, ROWS, SUBS * LANES)


def solution(mesh):
    specs = (P(None, "solve", "cross"),) * 3 + (P("solve", "cross"),)
    return jax.shard_map(
        per_device,
        mesh=mesh,
        in_specs=specs,
        out_specs=P(None, "solve", "cross"),
        check_vma=False,
    )
```

```python
import functools

import jax
import jax.numpy as jnp
from jax import lax
from jax.experimental import pallas as pl
from jax.experimental.pallas import tpu as pltpu
from jax.sharding import PartitionSpec as P

MESH = pl.DeviceIdType.MESH
ROWS, SUBS, LANES = 16, 8, 128
GROUP, OWNERS, PARTS = 16, 8, 64
FIRST, LAST = 0, 49
FRONT = (1, 0, 16, 17, 32, 33, 48, 49)
LOADS, USED, SLOT = 4, 14, 16
FLAT = 2 * ROWS * SUBS


def inverse(coupling, first, second):
    scale = 1.0 / (coupling * (first + second) + first * second)
    return (coupling + second) * scale, coupling * scale, (coupling + first) * scale


def merge(left, right):
    ea1, ea2, sa, n11, n12, n21, n22, ec1, ec2, sc = left
    fa1, fa2, fs, m11, m12, m21, m22, fc1, fc2, gs = right
    eb1, eb2, sb = ec1 + fa1, ec2 + fa2, sc + fs
    r1 = eb1 + ((n11 + n21) + (m11 + m12))
    r2 = eb2 + ((n12 + n22) + (m21 + m22))
    i11, i12, i22 = inverse(sb, r1, r2)
    g11, g12 = n11 * i11 + n12 * i12, n11 * i12 + n12 * i22
    g21, g22 = n21 * i11 + n22 * i12, n21 * i12 + n22 * i22
    h11, h12 = i11 * m11 + i12 * m21, i11 * m12 + i12 * m22
    h21, h22 = i12 * m11 + i22 * m21, i12 * m12 + i22 * m22
    joined = (
        ea1 + (g11 * eb1 + g12 * eb2),
        ea2 + (g21 * eb1 + g22 * eb2),
        sa + (g11 * n21 + g12 * n22),
        g11 * m11 + g12 * m21,
        g11 * m12 + g12 * m22,
        g21 * m11 + g22 * m21,
        g21 * m12 + g22 * m22,
        fc1 + (h11 * eb1 + h21 * eb2),
        fc2 + (h12 * eb1 + h22 * eb2),
        gs + (m11 * h12 + m21 * h22),
    )
    return joined, (i11, i12, i22, g11, g12, g21, g22, h11, h12, h21, h22)


def merge_leaf(sa, sb, n1, n2, m1, m2):
    r1, r2 = 1.0 + (n1 + m1), 1.0 + (n2 + m2)
    i11, i12, i22 = inverse(sb, r1, r2)
    g11, g12, g21, g22 = n1 * i11, n1 * i12, n2 * i12, n2 * i22
    h11, h12, h21, h22 = i11 * m1, i12 * m2, i12 * m1, i22 * m2
    joined = (
        1.0 + (g11 + g12),
        1.0 + (g21 + g22),
        sa + g12 * n2,
        g11 * m1,
        g12 * m2,
        g21 * m1,
        g22 * m2,
        h11 + h21,
        h12 + h22,
        m1 * h12,
    )
    return joined, (i11, i12, i22, g11, g12, g21, g22, h11, h12, h21, h22)


def merge_loads(back, left, right):
    i11, i12, i22, g11, g12, g21, g22, h11, h12, h21, h22 = back
    a1, a2, b1, b2 = left
    c1, c2, d1, d2 = right
    b1, b2 = b1 + c1, b2 + c2
    loads = (
        a1 + (g11 * b1 + g12 * b2),
        a2 + (g21 * b1 + g22 * b2),
        d1 + (h11 * b1 + h21 * b2),
        d2 + (h12 * b1 + h22 * b2),
    )
    return loads, (i11 * b1 + i12 * b2, i12 * b1 + i22 * b2)


def merge_leaf_loads(back, a, b):
    i11, i12, i22, g11, g12, g21, g22, h11, h12, h21, h22 = back
    a1, a2 = a
    b1, b2 = b
    loads = (
        a1 + (g11 * b1 + g12 * b2),
        a2 + (g21 * b1 + g22 * b2),
        h11 * b1 + h21 * b2,
        h12 * b1 + h22 * b2,
    )
    return loads, (i11 * b1 + i12 * b2, i12 * b1 + i22 * b2)


def middle(back, own, before, after):
    g11, g12, g21, g22, h11, h12, h21, h22 = back[3:]
    a1, a2 = before
    c1, c2 = after
    return (
        own[0] + ((g11 * a1 + g21 * a2) + (h11 * c1 + h12 * c2)),
        own[1] + ((g12 * a1 + g22 * a2) + (h21 * c1 + h22 * c2)),
    )


def kernel(
    temp_hbm,
    face_hbm,
    diff_hbm,
    sheet_hbm,
    out_ref,
    temp,
    face,
    diff,
    sheet,
    source,
    edge_send,
    edge_own,
    edge_far,
    flux_send,
    flux_recv,
    part_send,
    late_send,
    part_recv,
    extra,
    node_send,
    node_recv,
    in_sem,
    edge_ssem,
    own_rsem,
    far_rsem,
    flux_ssem,
    flux_rsem,
    part_ssem,
    part_rsem,
    node_ssem,
    node_rsem,
):
    solve = lax.axis_index("solve")
    cross = lax.axis_index("cross")
    n_cross = lax.axis_size("cross")
    place = lax.rem(solve, GROUP)
    group = lax.div(solve, GROUP)

    loads_in = [
        pltpu.make_async_copy(src, dst, in_sem.at[i])
        for i, (src, dst) in enumerate(
            ((face_hbm, face), (sheet_hbm, sheet), (temp_hbm, temp), (diff_hbm, diff))
        )
    ]
    for copy in loads_in:
        copy.start()

    owner = place < 2
    column_row = group * 2 + place
    outer = (solve == FIRST) | (solve == LAST)
    rows_of = [lax.rem(solve + step, OWNERS) for step in range(OWNERS)]

    def device_of(index):
        return lax.div(index, 2) * GROUP + lax.rem(index, 2)

    right = lax.rem(cross + 1, n_cross)
    left = lax.rem(cross + n_cross - 1, n_cross)

    barrier = pltpu.get_barrier_semaphore()
    for column, side in ((FIRST, left), (LAST, right)):

        @pl.when(solve == column)
        def _():
            def greet(index, _):
                pl.semaphore_signal(
                    barrier,
                    1,
                    device_id={"solve": index, "cross": side},
                    device_id_type=MESH,
                )
                return 0

            lax.fori_loop(0, PARTS, greet, 0)

    @pl.when(owner)
    def _():
        def greet(step, _):
            pl.semaphore_signal(
                barrier,
                1,
                device_id={"solve": lax.rem(solve + step, PARTS)},
                device_id_type=MESH,
            )
            return 0

        lax.fori_loop(1, PARTS, greet, 0)
        extra[...] = jnp.zeros((PARTS * LOADS, LANES), jnp.float32)

    lane = lax.broadcasted_iota(jnp.int32, (SUBS, LANES), 1)
    sub = lax.broadcasted_iota(jnp.int32, (SUBS, LANES), 0)

    zero = jnp.zeros((SUBS, LANES), jnp.float32)

    def spin(value, shift):
        return pltpu.roll(value, shift % LANES, 1)

    def tile(ref, block, column):
        return ref[pl.ds((block * SUBS + column) * SUBS, SUBS), :]

    def slot(ref, index, rows, used):
        start = index * rows if isinstance(index, int) else pl.multiple_of(index * rows, rows)
        return ref.at[pl.ds(start, used)]

    def row(ref, plane, i):
        start = (plane * 2 + i // SUBS) * SUBS * SUBS + i % SUBS
        return ref[pl.ds(start, SUBS, stride=SUBS), :]

    loads_in[0].wait()
    loads_in[1].wait()
    backs = []
    level = []
    back = []
    for m in range(ROWS // 2):
        element, way = merge_leaf(
            row(sheet, 0, 2 * m),
            row(sheet, 0, 2 * m + 1),
            row(face, 0, 2 * m),
            row(face, 1, 2 * m),
            row(face, 0, 2 * m + 1),
            row(face, 1, 2 * m + 1),
        )
        level.append(element)
        back.append(way)
    backs.append(back)
    while len(level) > 1:
        pairs = [merge(level[2 * m], level[2 * m + 1]) for m in range(len(level) // 2)]
        level = [pair[0] for pair in pairs]
        backs.append([pair[1] for pair in pairs])
    element = level[0]

    def send_parts(ref, slot_rows, skip, rows):
        def rows_at(ref, slot_rows, index):
            start = pl.multiple_of(index * slot_rows, slot_rows) + skip % slot_rows
            return ref.at[pl.ds(start, rows)]

        for index in rows_of:

            @pl.when(device_of(index) != solve)
            def _():
                pltpu.make_async_remote_copy(
                    src_ref=rows_at(ref, slot_rows, index),
                    dst_ref=rows_at(part_recv, SLOT, solve),
                    send_sem=part_ssem,
                    recv_sem=part_rsem,
                    device_id={"solve": device_of(index)},
                    device_id_type=MESH,
                ).start()

    for j, value in enumerate(element):
        part_send[pl.ds(LOADS + j, SUBS, stride=SLOT), :] = value
    @pl.when(owner)
    def _():
        pl.semaphore_wait(barrier, 2 + OWNERS - 1)

    @pl.when(jnp.logical_not(owner))
    def _():
        pl.semaphore_wait(barrier, 2 + OWNERS)

    send_parts(part_send, SLOT, LOADS, USED - LOADS)

    loads_in[2].wait()
    loads_in[3].wait()
    tracks = [(ref, j) for ref in (temp, diff, face) for j in range(4)]
    tracks += [(sheet, 0), (sheet, 1)]
    for i, (column, shift) in enumerate(((0, 0), (SUBS - 1, 1))):
        packed = jnp.zeros((SUBS, LANES), jnp.float32)
        for j, (ref, block) in enumerate(tracks):
            at = j * SUBS
            packed = jnp.where(lane == at, spin(tile(ref, block, column), at + shift), packed)
        for step in (1, 2, 4):
            packed = packed + spin(pltpu.roll(packed, SUBS - step, 0), step)
        edge_send[pl.ds(i, 1), :] = packed[0:1, :]
    flux_recv[pl.ds(4, 4), :] = zero[0:4, :]

    for i, (mine, theirs, side) in enumerate(
        ((FIRST, LAST, left), (LAST, FIRST, right))
    ):
        edge = edge_send.at[pl.ds(i, 1)]
        pltpu.make_async_remote_copy(
            src_ref=edge,
            dst_ref=slot(edge_far, solve, 1, 1),
            send_sem=edge_ssem,
            recv_sem=far_rsem,
            device_id={"solve": theirs, "cross": side},
            device_id_type=MESH,
        ).start()

        @pl.when(solve != mine)
        def _():
            pltpu.make_async_remote_copy(
                src_ref=edge,
                dst_ref=slot(edge_own, solve, 1, 1),
                send_sem=edge_ssem,
                recv_sem=own_rsem,
                device_id={"solve": mine},
                device_id_type=MESH,
            ).start()

        @pl.when(solve == mine)
        def _():
            edge_own[pl.ds(mine, 1), :] = edge_send[pl.ds(i, 1), :]

    for block in range(4):
        heat = [tile(temp, block, t) for t in range(SUBS)]
        cond = [tile(diff, block, t) for t in range(SUBS)]
        heat_turned = [spin(v, -1) for v in heat] + [zero]
        cond_turned = [spin(v, -1) for v in cond] + [zero]
        last = lane == LANES - 1
        before = zero
        for t in range(SUBS):
            next_heat = jnp.where(last, heat_turned[t + 1], heat_turned[t])
            next_cond = jnp.where(last, cond_turned[t + 1], cond_turned[t])
            flux = 0.5 * (cond[t] + next_cond) * (next_heat - heat[t])
            if t == SUBS - 1:
                flux = jnp.where(last, 0.0, flux)
            turned = spin(flux, 1)
            previous = jnp.where(lane == 0, before, turned)
            before = turned
            source[pl.ds((block * SUBS + t) * SUBS, SUBS), :] = heat[t] + flux - previous


    def climb_loads():
        owns = []
        level = []
        own = []
        for m in range(ROWS // 2):
            loads, value = merge_leaf_loads(
                backs[0][m],
                (row(source, 0, 2 * m), row(source, 1, 2 * m)),
                (row(source, 0, 2 * m + 1), row(source, 1, 2 * m + 1)),
            )
            level.append(loads)
            own.append(value)
        owns.append(own)
        for back in backs[1:]:
            pairs = [
                merge_loads(back[m], level[2 * m], level[2 * m + 1]) for m in range(len(back))
            ]
            level = [pair[0] for pair in pairs]
            owns.append([pair[1] for pair in pairs])
        return level[0], owns

    loads, _ = climb_loads()
    for j, value in enumerate(loads):
        late_send[pl.ds(j, SUBS, stride=LOADS), :] = value

    send_parts(late_send, LOADS, 0, LOADS)

    @pl.when(owner)
    def _():
        here = pl.multiple_of(solve * SLOT, SLOT)
        there = pl.multiple_of(column_row * SLOT, SLOT) + LOADS
        late = pl.ds(pl.multiple_of(column_row * LOADS, LOADS), LOADS)
        part_recv[pl.ds(here, LOADS), :] = late_send[late, :]
        part_recv[pl.ds(here + LOADS, USED - LOADS), :] = part_send[
            pl.ds(there, USED - LOADS), :
        ]

    def climb(left_fields, right_fields):
        element, way = merge(left_fields[LOADS:], right_fields[LOADS:])
        loads, value = merge_loads(way, left_fields[:LOADS], right_fields[:LOADS])
        return loads + element, way, value

    def wait_for(ref, rows, sem):
        part = ref.at[pl.ds(0, rows)]
        pltpu.make_async_copy(part, part, sem).wait()

    def to_all(first, last, send):
        def one(n, _):
            part = lax.rem(lax.div(n, 2), 4) * GROUP + lax.div(n, 8) * 2 + lax.rem(n, 2)

            @pl.when(part != solve)
            def _():
                send(part)

            return 0

        lax.fori_loop(first, last, one, 0)

    def flux_to(i):
        def send(part):
            pltpu.make_async_remote_copy(
                src_ref=slot(flux_send, lax.rem(part, SUBS), 2, 2),
                dst_ref=flux_recv.at[pl.ds(i * 2, 2)],
                send_sem=flux_ssem,
                recv_sem=flux_rsem,
                device_id={"solve": part},
                device_id_type=MESH,
            ).start()

        return send

    def along(ref, at, inside=None):
        value = zero
        for a in range(SUBS):
            part = spin(ref[pl.ds(a * SUBS, SUBS), :], a * ROWS - at)
            value = jnp.where(lax.div(lane, ROWS) == a, part, value)
        return value if inside is None else jnp.where(inside, value, 0.0)

    for i, (column, at, inside) in enumerate(
        ((FIRST, 0, cross > 0), (LAST, LANES - 1, cross < n_cross - 1))
    ):

        @pl.when(solve == column)
        def _():
            wait_for(edge_own, PARTS - 1, own_rsem)
            first1, first2, second = (along(edge_own, f * ROWS) for f in (4, 5, 6))
            element, way = merge_leaf(
                second, spin(second, -1), first1, first2, spin(first1, -1), spin(first2, -1)
            )
            ways = [way]
            for shift in (2, 4, 8):
                element, way = merge(element, tuple(spin(v, -shift) for v in element))
                ways.append(way)
            own = [along(edge_own, f * ROWS) for f in range(4)]
            wait_for(edge_far, PARTS, far_rsem)
            far = [along(edge_far, f * ROWS, inside) for f in range(4)]
            sides = []
            for plane in (0, 1):
                total = own[2 + plane] + far[2 + plane]
                sides.append(0.5 * total * (far[plane] - own[plane]))
                flux_send[pl.ds(plane, SUBS, stride=2), :] = sides[plane]
            fields, _ = merge_leaf_loads(ways[0], sides, [spin(v, -1) for v in sides])
            for shift, way in zip((2, 4, 8), ways[1:]):
                fields, _ = merge_loads(way, fields, [spin(v, -shift) for v in fields])
            for a in range(SUBS):
                for j in range(LOADS):
                    at_rows = pl.ds(a * SUBS * LOADS + j, SUBS, stride=LOADS)
                    moved = spin(fields[j], at - a * ROWS)
                    extra[at_rows, :] = jnp.where(lane == at, moved, 0.0)
            for part in FRONT:
                if part != column:
                    flux_to(i)(part)
            flux_recv[pl.ds(i * 2, 2), :] = flux_send[pl.ds((column % SUBS) * 2, 2), :]

    @pl.when(owner)
    def _():
        wait_for(part_recv, (PARTS - 1) * USED, part_rsem)

        level = []
        for k in range(SUBS):
            loads = tuple(
                part_recv[pl.ds(k * SLOT + j, SUBS, stride=SUBS * SLOT), :]
                + extra[pl.ds(k * LOADS + j, SUBS, stride=SUBS * LOADS), :]
                for j in range(LOADS)
            )
            rest = tuple(
                part_recv[pl.ds(k * SLOT + j, SUBS, stride=SUBS * SLOT), :]
                for j in range(LOADS, USED)
            )
            level.append(loads + rest)
        steps = []
        while len(level) > 1:
            joined = [climb(level[2 * m], level[2 * m + 1]) for m in range(len(level) // 2)]
            steps.append([item[1:] for item in joined])
            level = [item[0] for item in joined]
        fields = level[0]
        trail = []
        for shift in (1, 2, 4):
            raised = tuple(pltpu.roll(v, SUBS - shift, 0) for v in fields)
            fields, way, value = climb(fields, raised)
            trail.append((way, value, shift))
        f1, f2, _, _, ea1, ea2, sa, n11, n12, n21, n22, _, _, _ = fields
        i11, i12, i22 = inverse(sa, ea1 + (n11 + n12), ea2 + (n21 + n22))
        before = (i11 * f1 + i12 * f2, i12 * f1 + i22 * f2)
        after = (zero, zero)

        for way, value, shift in reversed(trail):
            inner = middle(way, value, before, after)
            first = (sub & shift) == 0
            before = tuple(
                jnp.where(first, b, pltpu.roll(v, shift, 0)) for b, v in zip(before, inner)
            )
            after = tuple(
                jnp.where(first, v, pltpu.roll(a, shift, 0)) for v, a in zip(inner, after)
            )
        nodes = [before, after]
        for step in reversed(steps):
            finer = []
            for m, (way, value) in enumerate(step):
                finer += [nodes[m], middle(way, value, nodes[m], nodes[m + 1])]
            nodes = finer + [nodes[-1]]
        for k in range(SUBS):
            for j, value in enumerate(nodes[k] + nodes[k + 1]):
                node_send[pl.ds(k * LOADS + j, SUBS, stride=SUBS * LOADS), :] = value

        def values_to(part):
            pltpu.make_async_remote_copy(
                src_ref=slot(node_send, part, LOADS, LOADS),
                dst_ref=slot(node_recv, column_row, LOADS, LOADS),
                send_sem=node_ssem,
                recv_sem=node_rsem,
                device_id={"solve": part},
                device_id_type=MESH,
            ).start()

        for n in range(PARTS):
            part = (n // 2) % 4 * GROUP + n // 8 * 2 + n % 2
            if n < OWNERS:
                pl.when(solve != part)(functools.partial(values_to, part))
            else:
                values_to(part)
        here = pl.ds(pl.multiple_of(column_row * LOADS, LOADS), LOADS)
        there = pl.ds(pl.multiple_of(solve * LOADS, LOADS), LOADS)
        node_recv[here, :] = node_send[there, :]

    for i, column in enumerate((FIRST, LAST)):

        @pl.when(solve == column)
        def _():
            to_all(OWNERS, PARTS, flux_to(i))

    @pl.when(outer)
    def _():
        wait_for(flux_recv, 2, flux_rsem)

    @pl.when(jnp.logical_not(outer))
    def _():
        wait_for(flux_recv, 4, flux_rsem)

    shift = lax.rem(LANES - lax.div(solve, SUBS) * ROWS, LANES)
    flux = pltpu.roll(flux_recv[...], shift, 1)
    flux = jnp.concatenate([flux, jnp.zeros((LANES - SUBS, LANES), jnp.float32)], axis=0).T
    for i, (column, at) in enumerate(((0, 0), (SUBS - 1, LANES - 1))):
        for j in range(4):
            where = pl.ds((j * SUBS + column) * SUBS, SUBS)
            part = flux[(j % 2) * SUBS : (j % 2 + 1) * SUBS]
            moved = spin(part, at - 2 * i - j // 2)
            source[where, :] += jnp.where(lane == at, moved, 0.0)
    _, owns = climb_loads()

    @pl.when(owner)
    def _():
        wait_for(node_recv, (OWNERS - 1) * LOADS, node_rsem)

    @pl.when(jnp.logical_not(owner))
    def _():
        wait_for(node_recv, OWNERS * LOADS, node_rsem)

    values = [node_recv[pl.ds(j, SUBS, stride=LOADS), :] for j in range(LOADS)]
    ends = [tuple(values[:2]), tuple(values[2:])]

    nodes = ends
    for back, own in zip(reversed(backs), reversed(owns)):
        finer = []
        for m in range(len(back)):
            finer += [nodes[m], middle(back[m], own[m], nodes[m], nodes[m + 1])]
        nodes = finer + [nodes[-1]]
    for i in range(ROWS):
        for plane in (0, 1):
            start = (plane * 2 + i // SUBS) * SUBS * SUBS + i % SUBS
            out_ref[pl.ds(start, SUBS, stride=SUBS), :] = nodes[i][plane]

    @pl.when(outer)
    def _():
        wait_for(edge_own, 3, edge_ssem)
        wait_for(node_send, (PARTS - 1) * 2, flux_ssem)

    @pl.when(jnp.logical_not(outer))
    def _():
        wait_for(edge_own, 4, edge_ssem)

    @pl.when(owner)
    def _():
        wait_for(part_send, (OWNERS - 1) * USED, part_ssem)
        wait_for(node_send, (PARTS - 1) * LOADS, node_ssem)

    @pl.when(jnp.logical_not(owner))
    def _():
        wait_for(part_send, OWNERS * USED, part_ssem)


def tiles(array):
    array = array.reshape(-1, ROWS // SUBS, SUBS, SUBS, LANES)
    return array.transpose(0, 1, 3, 2, 4).reshape(-1, LANES)


def per_device(temperature, transfer, diffusivity, exchange):
    vmem = lambda *shape: pltpu.VMEM(shape, jnp.float32)
    dma = pltpu.SemaphoreType.DMA
    out = pl.pallas_call(
        kernel,
        out_shape=jax.ShapeDtypeStruct((FLAT, LANES), jnp.float32),
        in_specs=[pl.BlockSpec(memory_space=pltpu.HBM)] * 4,
        out_specs=pl.BlockSpec(memory_space=pltpu.VMEM),
        scratch_shapes=[
            vmem(FLAT, LANES),
            vmem(FLAT, LANES),
            vmem(FLAT, LANES),
            vmem(FLAT // 2, LANES),
            vmem(FLAT, LANES),
            vmem(SUBS, LANES),
            vmem(PARTS, LANES),
            vmem(PARTS, LANES),
            vmem(2 * SUBS, LANES),
            vmem(SUBS, LANES),
            vmem(OWNERS * SLOT, LANES),
            vmem(OWNERS * LOADS, LANES),
            vmem(PARTS * SLOT, LANES),
            vmem(PARTS * LOADS, LANES),
            vmem(PARTS * LOADS, LANES),
            vmem(OWNERS * LOADS, LANES),
            dma((4,)),
            dma,
            dma,
            dma,
            dma,
            dma,
            dma,
            dma,
            dma,
            dma,
        ],
        compiler_params=pltpu.CompilerParams(
            collective_id=0, has_side_effects=True, vmem_limit_bytes=16 * 1024 * 1024
        ),
        cost_estimate=pl.CostEstimate(
            flops=4_000_000, bytes_accessed=600_000, transcendentals=0
        ),
        name="line_step",
    )(
        *(
            pltpu.with_memory_space_constraint(tiles(array), pltpu.HBM)
            for array in (temperature, transfer, diffusivity, exchange)
        )
    )
    out = out.reshape(2, ROWS // SUBS, SUBS, SUBS, LANES).transpose(0, 1, 3, 2, 4)
    return out.reshape(2, ROWS, SUBS * LANES)


def solution(mesh):
    specs = (P(None, "solve", "cross"),) * 3 + (P("solve", "cross"),)
    return jax.shard_map(
        per_device,
        mesh=mesh,
        in_specs=specs,
        out_specs=P(None, "solve", "cross"),
        check_vma=False,
    )
```
